32 devices in a mesh: seq: 8 (over y, x, core), head: 4 (over z).
Axes of the slice: x: 2, y: 2, z: 4, core: 2. Of those that a mesh axis runs over, the one named last changes fastest.
Arguments:
- queries: bfloat16 [8192, 1024], P('seq', 'head'), may hold values from -6 to 6
- values: bfloat16 [8192, 1024], P('seq', 'head'), may hold values from -6 to 6
- w_out: bfloat16 [1024, 1024], P('head'), may hold values from -0.1875 to 0.1875
- out_grad: bfloat16 [8192, 1024], P('seq', 'head'), may hold values from -6 to 6
- slots: int32 [2, 16, 8192], P(None, 'head', 'seq'), may hold values from 0 to 8191, as said below
Outputs:
- output: bfloat16 [8192, 1024], P('seq', 'head')
- query_grad: bfloat16 [8192, 1024], P('seq', 'head')
- value_grad: bfloat16 [8192, 1024], P('seq', 'head')
- w_out_grad: float32 [1024, 1024], P('head')
The draws below stay inside these ranges and needn't reach their ends.
Inputs may be any that keep to these rules, and one draw needn't show every extreme that they name: slots[r, h] is a permutation of the token positions: each token's place in round r's stable sort of head h's bucket ids. Of the 1024 tokens of one device of seq, exactly 192 have places among the 1024 places of one device of seq (possibly itself), 64 among those of the next device cyclically, and 128 among those of each other device.
All inputs are finite; a program needn't handle non-finite values.
Results may differ from the reference program's by a relative error of at most 0.024.
Values may be sent and summed in bfloat16 or wider, within the bound.
No kernel may reach another device: no remote copies, remote signals or barrier semaphores. Data moves between devices by JAX's collectives and lax.ppermute only.
A program may use at most 64 MiB of HBM per device.

```python
import jax
import jax.numpy as jnp
from jax import lax

D = 1024
HEADS = 16
DH = 64
ROUNDS = 2
SPAN = 128
TOK_DEV = 1024
TOKENS = 8192
N_HEAD = 4


def draw_slots(key, part):
    shard_count = TOKENS // TOK_DEV
    even_share = TOK_DEV // shard_count
    token_index = jnp.arange(TOK_DEV, dtype=jnp.int32)
    labels = token_index // even_share
    global_index = jnp.arange(TOKENS, dtype=jnp.int32)

    def draw_single(seed_key):
        first_key, second_key, third_key = jax.random.split(seed_key, 3)
        heavy_target = jax.random.permutation(first_key, shard_count).astype(jnp.int32)
        light_target = (heavy_target + 1) % shard_count
        base_labels = jnp.broadcast_to(labels[None, :], (shard_count, TOK_DEV))
        moved_mask = (base_labels == light_target[:, None]) & ((token_index % even_share)[None, :] < even_share // 2)
        shaped_labels = jnp.where(moved_mask, heavy_target[:, None], base_labels)
        row_keys = jax.random.split(second_key, shard_count)
        shuffled = jax.vmap(jax.random.permutation)(row_keys, shaped_labels)
        destination = shuffled.reshape(TOKENS).astype(jnp.int32)
        bucket = jax.random.randint(third_key, (TOKENS,), 0, 64, dtype=jnp.int32)
        sort_key = (destination * 64 + bucket) * TOKENS + global_index
        sort_order = jnp.argsort(sort_key)
        return jnp.zeros((TOKENS,), jnp.int32).at[sort_order].set(global_index)
    seed_keys = jax.random.split(key, ROUNDS * HEADS)
    return jax.vmap(draw_single)(seed_keys).reshape(ROUNDS, HEADS, TOKENS)


def block_levels(own_key, extent, pieces, least, largest):
    def one(axis_at, parts):
        steps = jax.random.uniform(jax.random.fold_in(jax.random.fold_in(own_key, 6), axis_at), (parts,), jnp.float32, least / len(pieces), largest / len(pieces))
        return jnp.repeat(jnp.exp(steps), extent[axis_at] // parts).reshape((-1,) + (1,) * (len(extent) - axis_at - 1))

    level = one(*pieces[0])
    for cut in pieces[1:]:
        level = level * one(*cut)
    return level


def normal_values(key, extent, deviation, bound, cuts=(), kind=jnp.bfloat16):
    level = block_levels(key, extent, cuts, -0.22, 0.18) if cuts else 1.0
    values = jax.random.normal(key, extent, jnp.float32) * deviation * level
    return jnp.minimum(jnp.maximum(values, -bound), bound).astype(kind)


def setup_inputs(seed: int = 0) -> dict:
    key_of = jax.random.split(jax.random.key(seed), 6)
    return {
        "queries": normal_values(key_of[0], (TOKENS, HEADS * DH), 1.0, 6.0, ((0, 8), (1, 4))),
        "values": normal_values(key_of[1], (TOKENS, HEADS * DH), 1.0, 6.0, ((0, 8), (1, 4))),
        "w_out": normal_values(key_of[2], (HEADS * DH, D), (HEADS * DH) ** -0.5, 0.1875, ((0, 4),)),
        "out_grad": normal_values(key_of[3], (TOKENS, D), 1.0, 6.0, ((0, 8), (1, 4))),
        "slots": draw_slots(jax.random.fold_in(key_of[5], 71), 0),
    }


def window_of(blocks):
    return jnp.concatenate([blocks, jnp.roll(blocks, 1, axis=0)], axis=1)

def round_forward(query_rows, value_rows, slot_row):
    token_count = query_rows.shape[0]
    head_width = query_rows.shape[1]
    score_scale = head_width ** (-0.5)
    positions = jnp.arange(token_count, dtype=jnp.int32)
    sorted_query = jnp.zeros_like(query_rows).at[slot_row].set(query_rows)
    sorted_value = jnp.zeros_like(value_rows).at[slot_row].set(value_rows)
    sorted_place = jnp.zeros((token_count,), jnp.int32).at[slot_row].set(positions)
    block_count = token_count // SPAN
    query_float = sorted_query.astype(jnp.float32)
    inverse = lax.rsqrt(lax.optimization_barrier(jnp.mean(query_float * query_float, axis=-1, keepdims=True)) + 1e-06)
    sorted_key = (query_float * inverse).astype(jnp.bfloat16)
    query_blocks = sorted_query.reshape(block_count, SPAN, head_width)
    key_window = window_of(sorted_key.reshape(block_count, SPAN, head_width))
    value_window = window_of(sorted_value.reshape(block_count, SPAN, head_width))
    place_blocks = sorted_place.reshape(block_count, SPAN)
    place_window = window_of(place_blocks)
    raw_scores = jnp.einsum('cqd,ckd->cqk', query_blocks.astype(jnp.float32), key_window.astype(jnp.float32)) * score_scale
    own_token = (jnp.arange(SPAN)[:, None] == jnp.arange(2 * SPAN)[None, :]).astype(jnp.float32)
    future = (place_window[:, None, :] > place_blocks[:, :, None]).astype(jnp.float32)
    scores = raw_scores - 100000.0 * own_token - 1000000000.0 * future
    row_top = lax.optimization_barrier(jnp.max(scores, axis=-1))
    log_total = row_top + jnp.log(lax.optimization_barrier(jnp.sum(jnp.exp(scores - row_top[..., None]), axis=-1)))
    weights = jnp.exp(scores - log_total[..., None])
    rounded_probs = weights.astype(jnp.bfloat16)
    block_out = jnp.einsum('cqk,ckd->cqd', rounded_probs.astype(jnp.float32), value_window.astype(jnp.float32)).astype(jnp.bfloat16)
    token_out = block_out.reshape(token_count, head_width)[slot_row]
    token_log = log_total.reshape(token_count)[slot_row]
    saved = (query_blocks, key_window, value_window, weights, rounded_probs, query_float, inverse)
    return (saved, token_out, token_log)

def round_backward(saved, grad_rows, delta_rows, slot_row):
    query_blocks, key_window, value_window, weights, rounded_probs, query_float, inverse = saved
    token_count = grad_rows.shape[0]
    head_width = grad_rows.shape[1]
    score_scale = head_width ** (-0.5)
    block_count = token_count // SPAN
    sorted_grad = jnp.zeros_like(grad_rows).at[slot_row].set(grad_rows)
    sorted_delta = jnp.zeros((token_count,), jnp.float32).at[slot_row].set(delta_rows)
    grad_blocks = sorted_grad.reshape(block_count, SPAN, head_width)
    delta_blocks = sorted_delta.reshape(block_count, SPAN)
    dot_grad = jnp.einsum('cqd,ckd->cqk', grad_blocks.astype(jnp.float32), value_window.astype(jnp.float32))
    score_grad = (weights * (dot_grad - delta_blocks[..., None])).astype(jnp.bfloat16)
    query_part = jnp.einsum('cqk,ckd->cqd', score_grad.astype(jnp.float32), key_window.astype(jnp.float32)) * score_scale
    key_part = jnp.einsum('cqk,cqd->ckd', score_grad.astype(jnp.float32), query_blocks.astype(jnp.float32)) * score_scale
    value_part = jnp.einsum('cqk,cqd->ckd', rounded_probs.astype(jnp.float32), grad_blocks.astype(jnp.float32))
    key_grad = key_part[:, :SPAN] + jnp.roll(key_part[:, SPAN:], -1, axis=0)
    value_sum = value_part[:, :SPAN] + jnp.roll(value_part[:, SPAN:], -1, axis=0)
    key_grad = key_grad.reshape(token_count, head_width)
    value_sum = value_sum.reshape(token_count, head_width)
    query_total = query_part.reshape(token_count, head_width) + inverse * key_grad - query_float * (inverse * inverse * inverse) * lax.optimization_barrier(jnp.mean(query_float * key_grad, axis=-1, keepdims=True))
    return (query_total.astype(jnp.bfloat16)[slot_row], value_sum.astype(jnp.bfloat16)[slot_row])

def reference(queries, values, w_out, out_grad, slots):
    token_count = queries.shape[0]
    head_width = DH
    back_full = jnp.dot(out_grad, w_out.T, preferred_element_type=jnp.float32).astype(jnp.bfloat16)
    attention_columns = []
    query_columns = []
    value_columns = []
    for head_index in range(HEADS):
        first_column = head_index * head_width
        query_rows = queries[:, first_column:first_column + head_width]
        value_rows = values[:, first_column:first_column + head_width]
        results = [round_forward(query_rows, value_rows, slots[turn_index, head_index]) for turn_index in range(ROUNDS)]
        log_stack = jnp.stack([result_entry[2] for result_entry in results])
        mixing = jax.nn.softmax(log_stack, axis=0)
        combined = jnp.zeros((token_count, head_width), jnp.float32)
        for turn_index in range(ROUNDS):
            combined = combined + mixing[turn_index][:, None] * results[turn_index][1].astype(jnp.float32)
        attention_columns.append(combined.astype(jnp.bfloat16))
        back_head = back_full[:, first_column:first_column + head_width].astype(jnp.float32)
        inner_rows = lax.optimization_barrier(jnp.sum(back_head * combined, axis=-1))
        query_sum = jnp.zeros((token_count, head_width), jnp.float32)
        value_sum = jnp.zeros((token_count, head_width), jnp.float32)
        for turn_index in range(ROUNDS):
            grad_rows = (mixing[turn_index][:, None] * back_head).astype(jnp.bfloat16)
            delta_rows = mixing[turn_index] * inner_rows
            query_part, value_part = round_backward(results[turn_index][0], grad_rows, delta_rows, slots[turn_index, head_index])
            query_sum = query_sum + query_part.astype(jnp.float32)
            value_sum = value_sum + value_part.astype(jnp.float32)
        query_columns.append(query_sum.astype(jnp.bfloat16))
        value_columns.append(value_sum.astype(jnp.bfloat16))
    attention = jnp.concatenate(attention_columns, axis=1)
    group_width = HEADS * DH // N_HEAD
    mixed = jnp.zeros((token_count, D), jnp.float32)
    for member in range(N_HEAD):
        partial_value = jnp.dot(attention[:, member * group_width:(member + 1) * group_width], w_out[member * group_width:(member + 1) * group_width], preferred_element_type=jnp.float32).astype(jnp.bfloat16)
        partial_value = lax.optimization_barrier(partial_value)
        mixed = mixed + partial_value.astype(jnp.float32)
    output = mixed.astype(jnp.bfloat16)
    w_out_grad = jnp.dot(attention.T, out_grad, preferred_element_type=jnp.float32) * token_count ** (-0.5)
    query_grad = jnp.concatenate(query_columns, axis=1)
    value_grad = jnp.concatenate(value_columns, axis=1)
    return (output, query_grad, value_grad, w_out_grad)
```

```python
import functools

import jax
import jax.numpy as jnp
from jax import lax
from jax.experimental import pallas as pl
from jax.experimental.pallas import tpu as pltpu
from jax.sharding import PartitionSpec as P

DH = 64
SPAN = 128
LANES = 128
GROUP = 8
F32 = jnp.float32
BF16 = jnp.bfloat16
NT = (((1,), (1,)), ((), ()))
TN = (((0,), (0,)), ((), ()))
MIB = 1 << 20


def whole(space):
    return pl.BlockSpec(memory_space=space)


def fixed(shape):
    return pl.BlockSpec(shape, lambda g: (0,) * len(shape))


def lane_of(shape):
    return lax.broadcasted_iota(jnp.int32, shape, len(shape) - 1)


def invert_kernel(slot_ref, place_ref):
    step = 16

    def body(i, carry):
        base = i * step
        spots = [slot_ref[base + j] for j in range(step)]
        for j in range(step):
            place_ref[spots[j]] = base + j
        return carry

    lax.fori_loop(0, slot_ref.shape[0] // step, body, 0)


def invert(slot_row):
    count = slot_row.shape[0]
    return pl.pallas_call(
        invert_kernel,
        out_shape=jax.ShapeDtypeStruct((count,), jnp.int32),
        in_specs=[whole(pltpu.SMEM)],
        out_specs=whole(pltpu.SMEM),
        cost_estimate=pl.CostEstimate(flops=0, bytes_accessed=40 * MIB, transcendentals=0),
        name="invert_slots",
    )(slot_row)


def gather_rows(addr_ref, base, source, target):
    for j in range(SPAN):
        target[pl.ds(j, 1), :] = source[pl.ds(addr_ref[base + j], 1), :]


def scatter_rows(addr_ref, base, source, target):
    for j in range(SPAN):
        target[pl.ds(addr_ref[base + j], 1), :] = source[pl.ds(j, 1), :]


def sorted_parts(rows):
    lane = lane_of(rows.shape)
    turned = pltpu.roll(rows, DH, 1)
    low = lane < DH
    mean = jnp.sum(jnp.where(low, rows * rows, 0.0), axis=1, keepdims=True) * (1.0 / DH)
    inverse = lax.rsqrt(mean + 1e-06)
    query_key = jnp.where(low, rows, turned * inverse).astype(BF16)
    value_one = jnp.where(low, turned, 1.0).astype(BF16)
    query_high = jnp.where(low, 0.0, turned).astype(BF16)
    return query_key, value_one, query_high


def forward_kernel(
    addr_ref, mine_ref, other_ref, key_place, query_place, offset_ref,
    home_ref, prob_ref, qk_ref, va_ref,
    tokens, result, rows_in, rows_out, qk_win, va_win,
):
    step = pl.program_id(0)
    half = mine_ref.shape[0]
    total = 2 * half
    score_scale = DH ** (-0.5) * 1.4426950408889634

    @pl.when(step == 0)
    def _():
        tokens[:half, :] = mine_ref[...].astype(F32)
        tokens[half:, :] = other_ref[...].astype(F32)
        gather_rows(addr_ref, total - SPAN, tokens, rows_in.at[0])
        query_key, value_one, _ = sorted_parts(rows_in[0])
        qk_win[:SPAN] = query_key
        va_win[:SPAN] = value_one

    for b in range(GROUP):
        base = (step * GROUP + b) * SPAN
        gather_rows(addr_ref, base, tokens, rows_in.at[b])
        query_key, value_one, query_high = sorted_parts(rows_in[b])
        own = slice((b + 1) * SPAN, (b + 2) * SPAN)
        window = slice(b * SPAN, (b + 2) * SPAN)
        qk_win[own] = query_key
        va_win[own] = value_one
        qk_ref[b * SPAN : (b + 1) * SPAN] = query_key
        va_ref[b * SPAN : (b + 1) * SPAN] = value_one
        raw = lax.dot_general(query_high, qk_win[window], NT, preferred_element_type=F32)
        seen = key_place[b] < query_place[0, :, b : b + 1]
        grown = jnp.where(seen, jnp.exp2(raw * score_scale), 0.0)
        mixed = jnp.dot(grown.astype(BF16), va_win[window], preferred_element_type=F32)
        lane = lane_of(mixed.shape)
        low = lane < DH
        sums = jnp.where(low, pltpu.roll(mixed, DH, 1), mixed)
        recip = 1.0 / sums
        prob_ref[b] = (grown * jnp.concatenate([recip, recip], axis=1)).astype(BF16)
        log_total = jnp.log(sums) - offset_ref[0, :, b : b + 1]
        high = log_total.astype(BF16).astype(F32)
        rest = log_total - high
        middle = rest.astype(BF16).astype(F32)
        tail = jnp.where(lane == DH, high, jnp.where(lane == DH + 1, middle, rest - middle))
        rows_out[b] = jnp.where(low, mixed * recip, jnp.where(lane < DH + 3, tail, 0.0))
        scatter_rows(addr_ref, base, rows_out.at[b], result)

    qk_win[:SPAN] = qk_win[GROUP * SPAN :]
    va_win[:SPAN] = va_win[GROUP * SPAN :]

    @pl.when(step == pl.num_programs(0) - 1)
    def _():
        home_ref[...] = result[...].astype(BF16)


def forward(addr, mine, other, key_place, query_place, offset):
    half = mine.shape[0]
    total = 2 * half
    blocks = total // SPAN
    rows = GROUP * SPAN
    return pl.pallas_call(
        forward_kernel,
        grid=(blocks // GROUP,),
        out_shape=[
            jax.ShapeDtypeStruct((total, LANES), BF16),
            jax.ShapeDtypeStruct((blocks, SPAN, 2 * SPAN), BF16),
            jax.ShapeDtypeStruct((total, LANES), BF16),
            jax.ShapeDtypeStruct((total, LANES), BF16),
        ],
        in_specs=[
            whole(pltpu.SMEM),
            fixed((half, LANES)),
            fixed((half, LANES)),
            pl.BlockSpec((GROUP, 1, 2 * SPAN), lambda g: (g, 0, 0)),
            pl.BlockSpec((1, SPAN, GROUP), lambda g: (g, 0, 0)),
            pl.BlockSpec((1, SPAN, GROUP), lambda g: (g, 0, 0)),
        ],
        out_specs=[
            fixed((total, LANES)),
            pl.BlockSpec((GROUP, SPAN, 2 * SPAN), lambda g: (g, 0, 0)),
            pl.BlockSpec((rows, LANES), lambda g: (g, 0)),
            pl.BlockSpec((rows, LANES), lambda g: (g, 0)),
        ],
        scratch_shapes=[
            pltpu.VMEM((total, LANES), F32),
            pltpu.VMEM((total, LANES), F32),
            pltpu.VMEM((GROUP, SPAN, LANES), F32),
            pltpu.VMEM((GROUP, SPAN, LANES), F32),
            pltpu.VMEM((rows + SPAN, LANES), BF16),
            pltpu.VMEM((rows + SPAN, LANES), BF16),
        ],
        compiler_params=pltpu.CompilerParams(vmem_limit_bytes=40 * MIB),
        cost_estimate=pl.CostEstimate(flops=0, bytes_accessed=64 * MIB, transcendentals=0),
        name="span_forward",
    )(addr, mine, other, key_place, query_place, offset)


def mix_kernel(own_ref, peer_ref, grad_ref, att_ref, grad_own, grad_peer):
    count = own_ref.shape[0]
    lane = lane_of((count, LANES))
    low = lane < DH
    row = lax.broadcasted_iota(jnp.int32, (LANES, LANES), 0)
    pick_log = ((row >= DH) & (row < DH + 3)).astype(BF16)
    ones = jnp.ones((LANES, LANES), BF16)
    own = own_ref[...]
    peer = peer_ref[...]
    difference = jnp.dot(own, pick_log, preferred_element_type=F32) - jnp.dot(
        peer, pick_log, preferred_element_type=F32
    )
    mix_own = 1.0 / (1.0 + jnp.exp(-difference))
    mix_peer = 1.0 / (1.0 + jnp.exp(difference))
    combined = jnp.where(low, mix_own * own.astype(F32) + mix_peer * peer.astype(F32), 0.0)
    packed = grad_ref[0].astype(F32)
    grad = jnp.concatenate([packed, pltpu.roll(packed, DH, 1)], axis=0)
    product = grad * combined
    high = product.astype(BF16)
    rest = (product - high.astype(F32)).astype(BF16)
    inner = jnp.dot(high, ones, preferred_element_type=F32) + jnp.dot(
        rest, ones, preferred_element_type=F32
    )
    for mix, out in ((mix_own, grad_own), (mix_peer, grad_peer)):
        delta = -(mix * inner)
        top = delta.astype(BF16).astype(F32)
        tail = jnp.where(lane == DH, top, jnp.where(lane == DH + 1, delta - top, 0.0))
        out[...] = jnp.where(low, mix * grad, tail).astype(BF16)
    turned = pltpu.roll(combined, DH, 1)
    att_ref[0] = (combined[: count // 2] + turned[count // 2 :]).astype(BF16)


def mix_rounds(home, peer, grad):
    half = peer.shape[0]
    pieces = grad.shape[0]
    rows = half // pieces
    by_rows = pl.BlockSpec((rows, LANES), lambda g: (g, 0))
    packed = pl.BlockSpec((1, rows // 2, LANES), lambda g: (g, 0, 0))
    return pl.pallas_call(
        mix_kernel,
        grid=(pieces,),
        out_shape=[
            jax.ShapeDtypeStruct(grad.shape, BF16),
            jax.ShapeDtypeStruct((half, LANES), BF16),
            jax.ShapeDtypeStruct((half, LANES), BF16),
        ],
        in_specs=[by_rows, by_rows, packed],
        out_specs=[packed, by_rows, by_rows],
        cost_estimate=pl.CostEstimate(flops=0, bytes_accessed=10 * MIB, transcendentals=0),
        name="mix_rounds",
    )(home, peer, grad)


def finished_rows(query_key, query_part, key_value):
    lane = lane_of(query_part.shape)
    low = lane < DH
    scale = DH ** (-0.5)
    query = jnp.where(low, query_key.astype(F32), 0.0)
    mean = jnp.sum(query * query, axis=1, keepdims=True) * (1.0 / DH)
    inverse = lax.rsqrt(mean + 1e-06)
    key = query * inverse
    term = key_value * (inverse * scale)
    along = jnp.sum(key * term, axis=1, keepdims=True) * (1.0 / DH)
    return jnp.where(low, pltpu.roll(query_part, DH, 1) * scale + term - key * along, key_value)


def backward_kernel(
    addr_ref, mine_ref, other_ref, prob_ref, qk_ref, qk_before, va_ref, va_before,
    out_ref,
    tokens, result, rows_in, rows_out, qk_win, va_win, keep_kv, keep_query, first_kv,
):
    step = pl.program_id(0)
    half = mine_ref.shape[0]
    total = 2 * half

    @pl.when(step == 0)
    def _():
        tokens[:half, :] = mine_ref[...].astype(F32)
        tokens[half:, :] = other_ref[...].astype(F32)

    qk_win[:SPAN] = qk_before[...]
    qk_win[SPAN:] = qk_ref[...]
    va_win[:SPAN] = va_before[...]
    va_win[SPAN:] = va_ref[...]
    kept_kv = keep_kv[...]
    kept_query = keep_query[...]
    for b in range(GROUP):
        block = step * GROUP + b
        base = block * SPAN
        gather_rows(addr_ref, base, tokens, rows_in.at[b])
        grad = rows_in[b]
        low = lane_of(grad.shape) < DH
        window = slice(b * SPAN, (b + 2) * SPAN)
        prob = prob_ref[b]
        dot_grad = lax.dot_general(
            grad.astype(BF16), va_win[window], NT, preferred_element_type=F32
        )
        score_grad = (prob.astype(F32) * dot_grad).astype(BF16)
        query_part = jnp.dot(score_grad, qk_win[window], preferred_element_type=F32)
        own_qk = qk_win[(b + 1) * SPAN : (b + 2) * SPAN]
        query_low = jnp.where(low, own_qk.astype(F32), 0.0).astype(BF16)
        grad_high = jnp.where(low, 0.0, pltpu.roll(grad, DH, 1)).astype(BF16)
        key_value = lax.dot_general(
            jnp.concatenate([score_grad, prob], axis=0),
            jnp.concatenate([query_low, grad_high], axis=0),
            TN,
            preferred_element_type=F32,
        )
        if b == 0:

            @pl.when(step == 0)
            def _():
                first_kv[...] = key_value[:SPAN]

        rows_out[b] = finished_rows(
            qk_win[b * SPAN : (b + 1) * SPAN], kept_query, kept_kv + key_value[:SPAN]
        )
        before = lax.rem(base + (total - SPAN), total)
        scatter_rows(addr_ref, before, rows_out.at[b], result)
        kept_kv = key_value[SPAN:]
        kept_query = query_part
    keep_kv[...] = kept_kv
    keep_query[...] = kept_query

    @pl.when(step == pl.num_programs(0) - 1)
    def _():
        rows_out[0] = finished_rows(
            qk_win[GROUP * SPAN :], keep_query[...], keep_kv[...] + first_kv[...]
        )
        scatter_rows(addr_ref, total - SPAN, rows_out.at[0], result)
        out_ref[...] = result[...].astype(BF16)


def backward(addr, mine, other, prob, query_key, value_one):
    half = mine.shape[0]
    total = 2 * half
    blocks = total // SPAN
    rows = GROUP * SPAN
    by_rows = pl.BlockSpec((rows, LANES), lambda g: (g, 0))
    before = pl.BlockSpec((SPAN, LANES), lambda g: (lax.rem(g * GROUP + blocks - 1, blocks), 0))
    return pl.pallas_call(
        backward_kernel,
        grid=(blocks // GROUP,),
        out_shape=jax.ShapeDtypeStruct((total, LANES), BF16),
        in_specs=[
            whole(pltpu.SMEM),
            fixed((half, LANES)),
            fixed((half, LANES)),
            pl.BlockSpec((GROUP, SPAN, 2 * SPAN), lambda g: (g, 0, 0)),
            by_rows,
            before,
            by_rows,
            before,
        ],
        out_specs=fixed((total, LANES)),
        scratch_shapes=[
            pltpu.VMEM((total, LANES), F32),
            pltpu.VMEM((total, LANES), F32),
            pltpu.VMEM((GROUP, SPAN, LANES), F32),
            pltpu.VMEM((GROUP, SPAN, LANES), F32),
            pltpu.VMEM((rows + SPAN, LANES), BF16),
            pltpu.VMEM((rows + SPAN, LANES), BF16),
            pltpu.VMEM((SPAN, LANES), F32),
            pltpu.VMEM((SPAN, LANES), F32),
            pltpu.VMEM((SPAN, LANES), F32),
        ],
        compiler_params=pltpu.CompilerParams(vmem_limit_bytes=40 * MIB),
        cost_estimate=pl.CostEstimate(flops=0, bytes_accessed=64 * MIB, transcendentals=0),
        name="span_backward",
    )(addr, mine, other, prob, query_key, query_key, value_one, value_one)


def swap_pair(value):
    count = lax.axis_size("seq")
    return lax.ppermute(value, "seq", [(i, i ^ 1) for i in range(count)])


def to_all(value):
    return lax.all_to_all(value, "seq", split_axis=0, concat_axis=0, tiled=True)


def along_head(value, cuts):
    count = lax.axis_size("head")
    place = lax.axis_index("head")
    rows = value.shape[0] // cuts
    parts = [value[i * rows : (i + 1) * rows] for i in range(cuts)]
    ups = [parts]
    downs = [parts]
    for k in range(1, count):
        up = [(i, i + 1) for i in range(k - 1, count - 1)]
        down = [(count - 1 - i, count - 2 - i) for i in range(k - 1, count - 1)]
        ups.append([lax.ppermute(part, "head", up) for part in ups[-1]])
        downs.append([lax.ppermute(part, "head", down) for part in downs[-1]])
    out = [value]
    for k in range(1, count):
        out.append(
            jnp.concatenate(
                [jnp.where(place >= k, u, d) for u, d in zip(ups[k], downs[count - k])], axis=0
            )
        )
    return out


def column_part(matrix, index, parts):
    width = matrix.shape[1] // parts
    return lax.dynamic_slice_in_dim(matrix, index * width, width, axis=1)


def by_sequence(queries, values, w_out, out_grad, slots):
    rows = queries.shape[0]
    rounds, heads, _ = slots.shape
    shards = lax.axis_size("seq")
    groups = lax.axis_size("head")
    group = lax.axis_index("head")
    core = lax.rem(lax.axis_index("seq"), rounds)
    total = shards * rows
    half_rows = rows // 2
    blocks = total // SPAN

    slot_row = to_all(slots.transpose(1, 0, 2).reshape(shards, rows)).reshape(total)
    place = invert(slot_row)
    source = place // rows
    part = (place // half_rows) % 2
    addr = ((part ^ core) * shards + source) * half_rows + place % half_rows

    head_rows = jnp.concatenate(
        [queries.reshape(rows, heads, DH), values.reshape(rows, heads, DH)], axis=2
    ).transpose(1, 0, 2)
    mine = to_all(head_rows.reshape(shards, half_rows, LANES)).reshape(total // 2, LANES)
    other = swap_pair(mine)

    grads = along_head(out_grad, 2)
    back = sum(
        lax.dot_general(
            grads[k], column_part(w_out, (group - k) % groups, groups), NT,
            preferred_element_type=F32,
        )
        for k in range(groups)
    ).astype(BF16)
    quarter = half_rows // 2
    back = back.reshape(2, 2, quarter, heads, DH).transpose(3, 0, 2, 1, 4)
    grad_half = to_all(back.reshape(shards, quarter, LANES))

    place_rows = place.reshape(blocks, SPAN).astype(F32)
    window = jnp.concatenate([jnp.roll(place_rows, 1, axis=0), place_rows], axis=1)
    least = jnp.min(window, axis=1, keepdims=True)
    key_place = jnp.where(window == least, window - 0.5, window).reshape(blocks, 1, 2 * SPAN)
    query_place = place_rows.reshape(blocks // GROUP, GROUP, SPAN).transpose(0, 2, 1)
    alone = jnp.where(place_rows == least, 100000.0, 0.0)
    alone = alone.reshape(blocks // GROUP, GROUP, SPAN).transpose(0, 2, 1)

    home, prob, query_key, value_one = forward(addr, mine, other, key_place, query_place, alone)
    peer = swap_pair(home[total // 2 :])
    att_half, grad_own, grad_peer = mix_rounds(home, peer, grad_half)
    grad_other = swap_pair(grad_peer)
    both = backward(addr, grad_own, grad_other, prob, query_key, value_one)

    att = to_all(att_half).reshape(heads, 2, quarter, 2, DH)
    att = att.transpose(1, 3, 2, 0, 4).reshape(rows, heads * DH)
    weight = jnp.concatenate(
        [
            lax.dot_general(att, grads[k], TN, preferred_element_type=F32).astype(BF16)
            for k in range(groups)
        ],
        axis=0,
    ).reshape(groups, heads * DH, -1)
    order = (group - jnp.arange(groups)) % groups
    weight = jnp.take(weight, order, axis=0)
    weight = weight.transpose(1, 0, 2).reshape(shards, heads * DH // shards, -1)
    weight = jnp.sum(to_all(weight).astype(F32), axis=0).astype(BF16)
    weight = to_all(jnp.broadcast_to(weight[None], (shards,) + weight.shape))
    w_out_grad = weight.reshape(heads * DH, -1).astype(F32) * total ** (-0.5)
    weights = lax.all_to_all(w_out, "head", split_axis=1, concat_axis=0, tiled=True)
    weights = weights.reshape(groups, heads * DH, -1)
    atts = along_head(att, 2)
    output = sum(
        jnp.dot(
            atts[k],
            lax.dynamic_index_in_dim(weights, (group - k) % groups, 0, keepdims=False),
            preferred_element_type=F32,
        ).astype(BF16).astype(F32)
        for k in range(groups)
    ).astype(BF16)

    arrived = swap_pair(both[total // 2 :])
    summed = (both[: total // 2].astype(F32) + arrived.astype(F32)).astype(BF16)
    summed = to_all(summed.reshape(shards, half_rows, LANES)).reshape(heads, rows, 2, DH)
    summed = summed.transpose(2, 1, 0, 3).reshape(2, rows, heads * DH)
    return (output, summed[0], summed[1], w_out_grad)


def shifted(value, axis, steps):
    count = lax.axis_size(axis)
    pairs = [(source, (source + steps) % count) for source in range(count)]
    return lax.ppermute(value, axis, pairs)


def with_before(blocks, before):
    earlier = jnp.concatenate([before[:, None], blocks[:, :-1]], axis=1)
    return jnp.concatenate([blocks, earlier], axis=2)


def normalized(query_rows):
    query_float = query_rows.astype(jnp.float32)
    inverse = lax.rsqrt(jnp.mean(query_float * query_float, axis=-1, keepdims=True) + 1e-06)
    return ((query_float * inverse).astype(jnp.bfloat16), query_float, inverse)


def move_wide(matrix, data, form):
    return jnp.einsum(form, matrix, data, preferred_element_type=jnp.float32).astype(jnp.bfloat16)


def move_exact(matrix, data, form):
    return jnp.einsum(form, matrix, data.astype(jnp.float32), precision=lax.Precision.HIGHEST)


def by_span(queries, values, w_out, out_grad, slots):
    row_count = queries.shape[0]
    head_width = DH
    rounds = slots.shape[0]
    head_group = queries.shape[1] // head_width
    batch_size = rounds * head_group
    shards = lax.axis_size("seq")
    my_index = lax.axis_index("seq")
    even_share = row_count // shards
    capacity = even_share * 3 // 2
    slot_total = shards * capacity
    block_count = row_count // SPAN
    score_scale = head_width ** (-0.5)

    def per_head(matrix):
        split_heads = matrix.reshape(row_count, head_group, head_width).transpose(1, 0, 2)
        return jnp.concatenate([split_heads] * rounds, axis=0)

    flat_slot = slots.reshape(batch_size, row_count)
    target = flat_slot // row_count
    local_slot = flat_slot - target * row_count
    onehot_target = (
        target[:, :, None] == jnp.arange(shards, dtype=jnp.int32)[None, None, :]
    ).astype(jnp.int32)
    earlier_count = jnp.sum(jnp.cumsum(onehot_target, axis=1) * onehot_target, axis=2) - 1
    send_spot = target * capacity + earlier_count
    positions = my_index * row_count + jnp.arange(row_count, dtype=jnp.int32)
    position_rows = jnp.broadcast_to(positions[None, :], (batch_size, row_count))
    pack_float = (
        send_spot[:, None, :] == jnp.arange(slot_total, dtype=jnp.int32)[None, :, None]
    ).astype(jnp.float32)
    pack_half = pack_float.astype(jnp.bfloat16)
    full_grad = lax.all_gather(out_grad, "head", axis=1, tiled=True)
    back_attn = lax.dot_general(
        full_grad, w_out, (((1,), (1,)), ((), ())), preferred_element_type=jnp.float32
    ).astype(jnp.bfloat16)
    query_value = jnp.concatenate([per_head(queries), per_head(values)], axis=2)
    packed_rows = move_wide(pack_half, query_value, "bsr,brd->bsd").reshape(
        batch_size, shards, capacity, 2 * head_width
    )
    packed_place = (
        move_exact(pack_float, position_rows, "bsr,br->bs")
        .astype(jnp.int32)
        .reshape(batch_size, shards, capacity)
    )
    packed_slot = (
        move_exact(pack_float, local_slot + 1, "bsr,br->bs")
        .astype(jnp.int32)
        .reshape(batch_size, shards, capacity)
    )
    got_rows, got_place, got_slot = (
        lax.all_to_all(packed_rows, "seq", split_axis=1, concat_axis=1, tiled=True),
        lax.all_to_all(packed_place, "seq", split_axis=1, concat_axis=1, tiled=True),
        lax.all_to_all(packed_slot, "seq", split_axis=1, concat_axis=1, tiled=True),
    )
    got_spot = got_slot.reshape(batch_size, slot_total)
    got_spot = jnp.where(got_spot == 0, row_count, got_spot - 1)
    sort_float = (
        got_spot[:, :, None] == jnp.arange(row_count, dtype=jnp.int32)[None, None, :]
    ).astype(jnp.float32)
    sort_half = sort_float.astype(jnp.bfloat16)
    sorted_rows = move_wide(
        sort_half, got_rows.reshape(batch_size, slot_total, 2 * head_width), "bsr,bsd->brd"
    )
    sorted_place = move_exact(
        sort_float, got_place.reshape(batch_size, slot_total), "bsr,bs->br"
    ).astype(jnp.int32)
    last_rows = sorted_rows[:, row_count - SPAN :]
    last_place = sorted_place[:, row_count - SPAN :]
    before_rows, before_place = shifted((last_rows, last_place), "seq", 1)
    sorted_query = sorted_rows[:, :, :head_width]
    sorted_value = sorted_rows[:, :, head_width:]
    sorted_key, query_float, inverse = normalized(sorted_query)
    before_key = normalized(before_rows[:, :, :head_width])[0]
    query_blocks = sorted_query.reshape(batch_size, block_count, SPAN, head_width)
    key_window = with_before(
        sorted_key.reshape(batch_size, block_count, SPAN, head_width), before_key
    )
    value_window = with_before(
        sorted_value.reshape(batch_size, block_count, SPAN, head_width),
        before_rows[:, :, head_width:],
    )
    place_blocks = sorted_place.reshape(batch_size, block_count, SPAN)
    place_window = with_before(place_blocks, before_place)
    own_token = (jnp.arange(SPAN)[:, None] == jnp.arange(2 * SPAN)[None, :]).astype(jnp.float32)
    future = (place_window[:, :, None, :] > place_blocks[:, :, :, None]).astype(jnp.float32)

    def score_of():
        raw_scores = (
            jnp.einsum(
                "bcqd,bckd->bcqk", query_blocks, key_window, preferred_element_type=jnp.float32
            )
            * score_scale
        )
        return raw_scores - 100000.0 * own_token - 1000000000.0 * future

    scores = score_of()
    row_top = jnp.max(scores, axis=-1)
    log_total = row_top + jnp.log(jnp.sum(jnp.exp(scores - row_top[..., None]), axis=-1))
    weights = jnp.exp(scores - log_total[..., None])
    rounded_probs = weights.astype(jnp.bfloat16)
    block_out = jnp.einsum(
        "bcqk,bckd->bcqd", rounded_probs, value_window, preferred_element_type=jnp.float32
    ).astype(jnp.bfloat16)
    out_rows = block_out.reshape(batch_size, row_count, head_width)
    home_out = move_wide(sort_half, out_rows, "bsr,brd->bsd").reshape(
        batch_size, shards, capacity // 2, 2 * head_width
    )
    home_log = move_exact(
        sort_float, log_total.reshape(batch_size, row_count), "bsr,br->bs"
    ).reshape(batch_size, shards, capacity)
    back_out, back_log = (
        lax.all_to_all(home_out, "seq", split_axis=1, concat_axis=1, tiled=True),
        lax.all_to_all(
            home_log.astype(jnp.bfloat16), "seq", split_axis=1, concat_axis=1, tiled=True
        ).astype(home_log.dtype),
    )
    round_out = move_wide(
        pack_half, back_out.reshape(batch_size, slot_total, head_width), "bsr,bsd->brd"
    ).reshape(rounds, head_group, row_count, head_width)
    round_log = move_exact(
        pack_float, back_log.reshape(batch_size, slot_total), "bsr,bs->br"
    ).reshape(rounds, head_group, row_count)
    mixing = jax.nn.softmax(round_log, axis=0)
    combined = jnp.sum(mixing[..., None] * round_out.astype(jnp.float32), axis=0)
    attention = (
        combined.astype(jnp.bfloat16).transpose(1, 0, 2).reshape(row_count, head_group * head_width)
    )
    head_term = jnp.dot(attention, w_out, preferred_element_type=jnp.float32)
    output = lax.psum_scatter(
        head_term.astype(jnp.bfloat16), "head", scatter_dimension=1, tiled=True
    )
    weight_term = lax.dot_general(
        attention, full_grad, (((0,), (0,)), ((), ())), preferred_element_type=jnp.float32
    )
    w_out_grad = lax.psum(weight_term.astype(jnp.bfloat16), "seq").astype(jnp.float32) * (
        shards * row_count
    ) ** (-0.5)
    back_heads = (
        back_attn.reshape(row_count, head_group, head_width).transpose(1, 0, 2).astype(jnp.float32)
    )
    inner_rows = jnp.sum(back_heads * combined, axis=-1)
    delta_rows = (mixing * inner_rows[None]).reshape(batch_size, row_count)
    grad_rows = (
        (mixing[..., None] * back_heads[None])
        .astype(jnp.bfloat16)
        .reshape(batch_size, row_count, head_width)
    )
    packed_grad = move_wide(pack_half, grad_rows, "bsr,brd->bsd").reshape(
        batch_size, shards, capacity // 2, 2 * head_width
    )
    packed_delta = move_exact(pack_float, delta_rows, "bsr,br->bs").reshape(
        batch_size, shards, capacity
    )
    got_grad, got_delta = (
        lax.all_to_all(packed_grad, "seq", split_axis=1, concat_axis=1, tiled=True),
        lax.all_to_all(
            packed_delta.astype(jnp.bfloat16), "seq", split_axis=1, concat_axis=1, tiled=True
        ).astype(packed_delta.dtype),
    )
    sorted_grad = move_wide(
        sort_half, got_grad.reshape(batch_size, slot_total, head_width), "bsr,bsd->brd"
    )
    sorted_delta = move_exact(sort_float, got_delta.reshape(batch_size, slot_total), "bsr,bs->br")
    kept_weights = jnp.exp(score_of() - log_total[..., None])
    grad_blocks = sorted_grad.reshape(batch_size, block_count, SPAN, head_width)
    delta_blocks = sorted_delta.reshape(batch_size, block_count, SPAN)
    dot_grad = jnp.einsum(
        "bcqd,bckd->bcqk", grad_blocks, value_window, preferred_element_type=jnp.float32
    )
    score_grad = (kept_weights * (dot_grad - delta_blocks[..., None])).astype(jnp.bfloat16)
    query_part = (
        jnp.einsum("bcqk,bckd->bcqd", score_grad, key_window, preferred_element_type=jnp.float32)
        * score_scale
    )
    key_part = (
        jnp.einsum("bcqk,bcqd->bckd", score_grad, query_blocks, preferred_element_type=jnp.float32)
        * score_scale
    )
    value_part = jnp.einsum(
        "bcqk,bcqd->bckd", rounded_probs, grad_blocks, preferred_element_type=jnp.float32
    )
    spill_rows = jnp.concatenate([key_part[:, 0, SPAN:], value_part[:, 0, SPAN:]], axis=2)
    arrived = shifted(spill_rows.astype(jnp.bfloat16), "seq", -1).astype(spill_rows.dtype)
    key_grad = key_part[:, :, :SPAN] + jnp.concatenate(
        [key_part[:, 1:, SPAN:], arrived[:, None, :, :head_width]], axis=1
    )
    value_sum = value_part[:, :, :SPAN] + jnp.concatenate(
        [value_part[:, 1:, SPAN:], arrived[:, None, :, head_width:]], axis=1
    )
    key_grad = key_grad.reshape(batch_size, row_count, head_width)
    value_sum = value_sum.reshape(batch_size, row_count, head_width)
    query_total = (
        query_part.reshape(batch_size, row_count, head_width)
        + inverse * key_grad
        - query_float
        * (inverse * inverse * inverse)
        * jnp.mean(query_float * key_grad, axis=-1, keepdims=True)
    )
    both_grads = jnp.concatenate(
        [query_total.astype(jnp.bfloat16), value_sum.astype(jnp.bfloat16)], axis=2
    )
    home_grads = move_wide(sort_half, both_grads, "bsr,brd->bsd").reshape(
        batch_size, shards, capacity, 2 * head_width
    )
    back_grads = lax.all_to_all(home_grads, "seq", split_axis=1, concat_axis=1, tiled=True)
    own_grads = move_wide(
        pack_half, back_grads.reshape(batch_size, slot_total, 2 * head_width), "bsr,bsd->brd"
    ).astype(jnp.float32)
    own_grads = own_grads.reshape(rounds, head_group, row_count, 2 * head_width)
    summed = jnp.sum(own_grads, axis=0).astype(jnp.bfloat16)
    query_grad = (
        summed[:, :, :head_width].transpose(1, 0, 2).reshape(row_count, head_group * head_width)
    )
    value_grad = (
        summed[:, :, head_width:].transpose(1, 0, 2).reshape(row_count, head_group * head_width)
    )
    return (output, query_grad, value_grad, w_out_grad)


def per_device(queries, values, w_out, out_grad, slots):
    if lax.axis_size("seq") == slots.shape[0] * slots.shape[1] and slots.shape[0] == 2:
        return by_sequence(queries, values, w_out, out_grad, slots)
    return by_span(queries, values, w_out, out_grad, slots)


def solution(mesh):
    placed = (
        P("seq", "head"),
        P("seq", "head"),
        P("head", None),
        P("seq", "head"),
        P(None, "head", "seq"),
    )
    return jax.shard_map(
        per_device,
        mesh=mesh,
        in_specs=placed,
        out_specs=(P("seq", "head"), P("seq", "head"), P("seq", "head"), P("head", None)),
        check_vma=False,
    )
```

```python
import functools

import jax
import jax.numpy as jnp
from jax import lax
from jax.experimental import pallas as pl
from jax.experimental.pallas import tpu as pltpu
from jax.sharding import PartitionSpec as P

DH = 64
SPAN = 128
LANES = 128
GROUP = 8
SUB = 4
F32 = jnp.float32
BF16 = jnp.bfloat16
NT = (((1,), (1,)), ((), ()))
TN = (((0,), (0,)), ((), ()))
MIB = 1 << 20


def whole(space):
    return pl.BlockSpec(memory_space=space)


def fixed(shape):
    return pl.BlockSpec(shape, lambda g: (0,) * len(shape), pipeline_mode=pl.Buffered(1))


def lane_of(shape):
    return lax.broadcasted_iota(jnp.int32, shape, len(shape) - 1)


def places_kernel(mine_ref, addr_ref, key_place, query_place, sign_ref):
    sources, _, lanes = mine_ref.shape
    blocks = addr_ref.shape[0]
    rows = mine_ref.shape[1] - 16
    parts = (mine_ref.shape[1] - rows) // 2
    core = lax.rem(lax.axis_index("seq"), 2)
    block_row = lax.broadcasted_iota(jnp.int32, (blocks, lanes), 0).astype(F32)
    place_row = lax.broadcasted_iota(jnp.int32, (lanes, lanes), 0).astype(F32)
    token_low = lane_of((blocks, lanes)).astype(F32)
    total = jnp.zeros((2 * blocks, lanes), F32)
    for s in range(sources):
        slots = mine_ref[s, rows:, :].astype(F32)
        tall = []
        wide = []
        for j in range(parts):
            in_block = block_row == slots[j : j + 1, :]
            token_high = float(s * parts + j)
            tall.append(
                jnp.concatenate(
                    [jnp.where(in_block, token_high, 0.0), jnp.where(in_block, token_low, 0.0)],
                    axis=0,
                ).astype(BF16)
            )
            wide.append((place_row == slots[parts + j : parts + j + 1, :]).astype(BF16))
        total += lax.dot_general(
            jnp.concatenate(tall, axis=1),
            jnp.concatenate(wide, axis=1),
            NT,
            preferred_element_type=F32,
        )
    place = total[:blocks] * float(lanes) + total[blocks:]
    token = place.astype(jnp.int32)
    source = token // (2 * rows)
    within = token - source * (2 * rows)
    part = within // rows
    addr_ref[...] = ((part ^ core) * sources + source) * rows + (within - part * rows)
    before = pltpu.roll(place, 1, 0)
    least = jnp.minimum(
        jnp.min(place, axis=1, keepdims=True), jnp.min(before, axis=1, keepdims=True)
    )
    window = jnp.concatenate([before, place], axis=1)
    window = jnp.where(window == least, window - 0.5, window)
    for c in range(blocks):
        key_place[c] = window[c : c + 1, :]
    columns = jnp.transpose(place)
    alone = jnp.transpose(jnp.where(place == least, -1.0, 1.0))
    for g in range(blocks // GROUP):
        query_place[g] = columns[:, g * GROUP : (g + 1) * GROUP]
        sign_ref[g] = alone[:, g * GROUP : (g + 1) * GROUP]


def find_places(mine):
    sources, rows, lanes = mine.shape
    blocks = 2 * sources * (rows - 16) // lanes
    column = jax.ShapeDtypeStruct((blocks // GROUP, lanes, GROUP), F32)
    return pl.pallas_call(
        places_kernel,
        out_shape=[
            jax.ShapeDtypeStruct((blocks, lanes), jnp.int32),
            jax.ShapeDtypeStruct((blocks, 1, 2 * lanes), F32),
            column,
            column,
        ],
        compiler_params=pltpu.CompilerParams(vmem_limit_bytes=10 * MIB),
        name="find_places",
    )(mine)


def gather_rows(addr_ref, block, source, target):
    for j in range(SPAN):
        target[pl.ds(j, 1), :] = source[pl.ds(addr_ref[block, j], 1), :]


def scatter_rows(addr_ref, block, source, target):
    for j in range(SPAN):
        target[pl.ds(addr_ref[block, j], 1), :] = source[pl.ds(j, 1), :]


def split_sum(product, chosen):
    high = product.astype(BF16)
    rest = (product - high.astype(F32)).astype(BF16)
    return jnp.dot(
        jnp.concatenate([high, rest], axis=1),
        jnp.concatenate([chosen, chosen], axis=0),
        preferred_element_type=F32,
    )


def low_lanes(scale=1.0):
    row = lax.broadcasted_iota(jnp.int32, (LANES, LANES), 0)
    return jnp.where(row < DH, scale, 0.0).astype(BF16)


def inverse_of(rows):
    return lax.rsqrt(split_sum(rows * rows, low_lanes(1.0 / DH)) + 1e-06)


def forward_kernel(
    addr_ref, mine_ref, other_ref, key_place, query_place, sign_ref,
    home_ref, away_ref, prob_ref, qv_ref, key_ref,
    tokens, result, in_even, in_odd, out_even, out_odd, grown_ref, qv_win, key_win,
):
    step = pl.program_id(0)
    last = pl.num_programs(0) - 1
    sources = mine_ref.shape[0]
    rows = mine_ref.shape[1] - 16
    half = sources * rows
    blocks = 2 * half // SPAN
    score_scale = DH ** (-0.5) * 1.4426950408889634
    rows_in = (in_even, in_odd)
    rows_out = (out_even, out_odd)

    def place_rows(values, at):
        low = lane_of(values.shape) < DH
        qv_win[at] = values.astype(BF16)
        key_win[at] = jnp.where(low, values * inverse_of(values), 0.0).astype(BF16)

    @pl.when(step == 0)
    def _():
        for s in range(sources):
            tokens[s * rows : (s + 1) * rows, :] = mine_ref[s, :rows, :].astype(F32)
            tokens[half + s * rows : half + (s + 1) * rows, :] = other_ref[s, :rows, :].astype(F32)
        gather_rows(addr_ref, blocks - 1, tokens, in_odd.at[0])
        place_rows(in_odd[0], slice(0, SPAN))
        for b in range(SUB):
            gather_rows(addr_ref, b, tokens, in_even.at[b])

    ones = jnp.ones((2 * SPAN, LANES), BF16)
    low = lane_of((SPAN, LANES)) < DH
    first = lane_of((SPAN, LANES)) == 0
    for p in range(GROUP // SUB):
        here = step * GROUP + p * SUB
        coming = jnp.minimum(here + SUB, blocks - SUB)
        gone = jnp.maximum(here - SUB, 0)
        now, then = p % 2, 1 - p % 2
        spans = slice((p * SUB + 1) * SPAN, ((p + 1) * SUB + 1) * SPAN)
        place_rows(rows_in[now][...].reshape(SUB * SPAN, LANES), spans)
        for i in range(SUB):
            b = p * SUB + i
            own = slice((b + 1) * SPAN, (b + 2) * SPAN)
            window = slice(b * SPAN, (b + 2) * SPAN)
            raw = lax.dot_general(qv_win[own], key_win[window], NT, preferred_element_type=F32)
            seen = key_place[b] < query_place[0, :, b : b + 1]
            grown_ref[i] = jnp.where(seen, jnp.exp2(raw * score_scale), 0.0)
            gather_rows(addr_ref, coming + i, tokens, rows_in[then].at[i])
        for i in range(SUB):
            b = p * SUB + i
            window = slice(b * SPAN, (b + 2) * SPAN)
            grown = grown_ref[i]
            mixed = jnp.dot(
                grown.astype(BF16),
                jnp.concatenate([qv_win[window], ones], axis=1),
                preferred_element_type=F32,
            )
            sums = mixed[:, LANES:]
            recip = 1.0 / sums
            prob_ref[b] = (grown * jnp.concatenate([recip, recip], axis=1)).astype(BF16)
            signed = sums * sign_ref[0, :, b : b + 1]
            rest = signed - signed.astype(BF16).astype(F32)
            rows_out[now][i] = jnp.where(
                low, jnp.where(first, signed, rest), mixed[:, :LANES] * recip
            )
            scatter_rows(addr_ref, gone + i, rows_out[then].at[i], result)

    qv_ref[...] = qv_win[SPAN:]
    key_ref[...] = key_win[SPAN:]
    qv_win[:SPAN] = qv_win[GROUP * SPAN :]
    key_win[:SPAN] = key_win[GROUP * SPAN :]

    @pl.when(step == last)
    def _():
        for i in range(SUB):
            scatter_rows(addr_ref, blocks - SUB + i, out_odd.at[i], result)
        home_ref[...] = result[:half, :].astype(BF16)
        away_ref[...] = result[half:, :].astype(BF16)


def forward(addr, mine, other, key_place, query_place, sign):
    half = mine.shape[0] * (mine.shape[1] - 16)
    total = 2 * half
    blocks = total // SPAN
    rows = GROUP * SPAN
    return pl.pallas_call(
        forward_kernel,
        grid=(blocks // GROUP,),
        out_shape=[
            jax.ShapeDtypeStruct((half, LANES), BF16),
            jax.ShapeDtypeStruct((half, LANES), BF16),
            jax.ShapeDtypeStruct((blocks, SPAN, 2 * SPAN), BF16),
            jax.ShapeDtypeStruct((total, LANES), BF16),
            jax.ShapeDtypeStruct((total, LANES), BF16),
        ],
        in_specs=[
            whole(pltpu.SMEM),
            fixed(mine.shape),
            fixed(mine.shape),
            pl.BlockSpec((GROUP, 1, 2 * SPAN), lambda g: (g, 0, 0)),
            pl.BlockSpec((1, SPAN, GROUP), lambda g: (g, 0, 0)),
            pl.BlockSpec((1, SPAN, GROUP), lambda g: (g, 0, 0)),
        ],
        out_specs=[
            fixed((half, LANES)),
            fixed((half, LANES)),
            pl.BlockSpec((GROUP, SPAN, 2 * SPAN), lambda g: (g, 0, 0)),
            pl.BlockSpec((rows, LANES), lambda g: (g, 0)),
            pl.BlockSpec((rows, LANES), lambda g: (g, 0)),
        ],
        scratch_shapes=[
            pltpu.VMEM((total, LANES), F32),
            pltpu.VMEM((total, LANES), F32),
            *[pltpu.VMEM((SUB, SPAN, LANES), F32)] * 4,
            pltpu.VMEM((SUB, SPAN, 2 * SPAN), F32),
            pltpu.VMEM((rows + SPAN, LANES), BF16),
            pltpu.VMEM((rows + SPAN, LANES), BF16),
        ],
        compiler_params=pltpu.CompilerParams(vmem_limit_bytes=22 * MIB),
        cost_estimate=pl.CostEstimate(flops=0, bytes_accessed=64 * MIB, transcendentals=0),
        name="span_forward",
    )(addr, mine, other, key_place, query_place, sign)


def share_of(own, peer):
    row = lax.broadcasted_iota(jnp.int32, (LANES, LANES), 0)
    pick = (row < 2).astype(BF16)
    own_sum = jnp.dot(own, pick, preferred_element_type=F32)
    peer_sum = jnp.dot(peer, pick, preferred_element_type=F32)
    both = own_sum / (own_sum + peer_sum)
    own_alone = own_sum < 0.0
    peer_alone = peer_sum < 0.0
    return jnp.where(
        own_alone, jnp.where(peer_alone, both, 0.0), jnp.where(peer_alone, 1.0, both)
    )


def combined_rows(own, peer, share):
    high = lane_of(own.shape) >= DH
    own = own.astype(F32)
    peer = peer.astype(F32)
    return jnp.where(high, share * own + (1.0 - share) * peer, 0.0)


def mix_attention_kernel(own_ref, peer_ref, att_ref):
    half = own_ref.shape[0] // 2
    own = own_ref[...]
    peer = peer_ref[...]
    combined = combined_rows(own, peer, share_of(own, peer))
    att_ref[0] = (pltpu.roll(combined[:half], DH, 1) + combined[half:]).astype(BF16)


def mix_grad_kernel(own_ref, peer_ref, grad_ref, grad_own, grad_peer):
    own = own_ref[...]
    peer = peer_ref[...]
    share = share_of(own, peer)
    combined = combined_rows(own, peer, share)
    packed = grad_ref[0].astype(F32)
    grad = jnp.concatenate([pltpu.roll(packed, DH, 1), packed], axis=0)
    inner = split_sum(grad * combined, jnp.ones((LANES, LANES), BF16))
    lane = lane_of(grad.shape)
    for mix, out in ((share, grad_own), (1.0 - share, grad_peer)):
        delta = -(mix * inner)
        rest = delta - delta.astype(BF16).astype(F32)
        tail = jnp.where(lane == 0, delta, jnp.where(lane == 1, rest, 0.0))
        out[...] = jnp.where(lane < DH, tail, mix * grad).astype(BF16)


def mixing(home, peer, grad=None):
    half = peer.shape[0]
    pieces = lax.axis_size("seq")
    rows = half // pieces
    by_rows = pl.BlockSpec((rows, LANES), lambda g: (g, 0))
    packed = pl.BlockSpec((1, rows // 2, LANES), lambda g: (g, 0, 0))
    cost = pl.CostEstimate(flops=0, bytes_accessed=10 * MIB, transcendentals=0)
    if grad is None:
        return pl.pallas_call(
            mix_attention_kernel,
            grid=(pieces,),
            out_shape=jax.ShapeDtypeStruct((pieces, rows // 2, LANES), BF16),
            in_specs=[by_rows, by_rows],
            out_specs=packed,
            cost_estimate=cost,
            name="mix_attention",
        )(home, peer)
    return pl.pallas_call(
        mix_grad_kernel,
        grid=(pieces,),
        out_shape=[jax.ShapeDtypeStruct((half, LANES), BF16)] * 2,
        in_specs=[by_rows, by_rows, packed],
        out_specs=[by_rows, by_rows],
        cost_estimate=cost,
        name="mix_grad",
    )(home, peer, grad)


def pack_kernel(query_ref, value_ref, slot_ref, out_ref):
    rounds, heads, rows = slot_ref.shape
    half = rows // 2
    for h in range(heads):
        columns = slice(h * DH, (h + 1) * DH)
        pair = jnp.concatenate([query_ref[:, columns], value_ref[:, columns]], axis=1)
        for r in range(rounds):
            out_ref[2 * h + r, :half] = pair[r * half : (r + 1) * half]
            slots = slot_ref[r, h : h + 1, :]
            high = slots // LANES
            parts = [high, slots - high * LANES]
            lines = [p[:, j : j + LANES] for p in parts for j in range(0, rows, LANES)]
            out_ref[2 * h + r, half:] = jnp.concatenate(lines, axis=0).astype(F32).astype(BF16)


def pack_heads(queries, values, slots):
    rounds, heads, rows = slots.shape
    return pl.pallas_call(
        pack_kernel,
        out_shape=jax.ShapeDtypeStruct((rounds * heads, rows // 2 + 16, 2 * DH), BF16),
        compiler_params=pltpu.CompilerParams(vmem_limit_bytes=10 * MIB),
        name="pack_heads",
    )(queries, values, slots)


def unpack_kernel(in_ref, query_ref, value_ref):
    for h in range(in_ref.shape[0]):
        columns = slice(h * DH, (h + 1) * DH)
        query_ref[:, columns] = in_ref[h, :, :DH]
        value_ref[:, columns] = in_ref[h, :, DH:]


def unpack_heads(rows):
    heads, count, _ = rows.shape
    return pl.pallas_call(
        unpack_kernel,
        out_shape=[jax.ShapeDtypeStruct((count, heads * DH), BF16)] * 2,
        name="unpack_heads",
    )(rows)


def member(step, groups):
    return lax.rem(lax.axis_index("head") + (groups - step), groups)


def columns_of(index, width):
    return pl.ds(pl.multiple_of(index * width, width), width)


def members(refs, groups):
    place = lax.axis_index("head")
    own, ups, downs = refs[0], refs[1:groups], refs[groups:]
    out = [own[...]]
    for k in range(1, groups):
        out.append(jnp.where(place >= k, ups[k - 1][...], downs[groups - k - 1][...]))
    return out


def back_kernel(weight_ref, *refs):
    *grads, out_ref = refs
    groups = (len(grads) + 1) // 2
    grads = members(grads, groups)
    rows, width = grads[0].shape
    total = 0.0
    for k in range(groups):
        weight = weight_ref[:, columns_of(member(k, groups), width)]
        total += lax.dot_general(grads[k], weight, NT, preferred_element_type=F32)
    total = total.astype(BF16)
    quarter = rows // 4
    for h in range(width // DH):
        columns = slice(h * DH, (h + 1) * DH)
        for c in range(2):
            first = total[2 * c * quarter : (2 * c + 1) * quarter, columns]
            second = total[(2 * c + 1) * quarter : (2 * c + 2) * quarter, columns]
            out_ref[2 * h + c] = jnp.concatenate([first, second], axis=1)


def back_projection(weight, grads):
    rows, width = grads[0].shape
    return pl.pallas_call(
        back_kernel,
        out_shape=jax.ShapeDtypeStruct((2 * width // DH, rows // 4, 2 * DH), BF16),
        compiler_params=pltpu.CompilerParams(vmem_limit_bytes=10 * MIB),
        name="back_projection",
    )(weight, *grads)


def project_kernel(weight_ref, packed_ref, att_ref, *outs):
    groups = len(outs) // 2
    rows, width = att_ref.shape
    quarter = rows // 4
    for h in range(width // DH):
        columns = slice(h * DH, (h + 1) * DH)
        for c in range(2):
            packed = packed_ref[2 * h + c]
            att_ref[2 * c * quarter : (2 * c + 1) * quarter, columns] = packed[:, :DH]
            att_ref[(2 * c + 1) * quarter : (2 * c + 2) * quarter, columns] = packed[:, DH:]
    for k in range(groups):
        weight = weight_ref[:, columns_of(member(groups - k, groups), width)]
        for c in range(2):
            part = att_ref[2 * c * quarter : 2 * (c + 1) * quarter]
            outs[2 * k + c][...] = jnp.dot(part, weight, preferred_element_type=F32).astype(BF16)


def project(weight, packed):
    count, quarter, _ = packed.shape
    rows, width = 4 * quarter, count * DH // 2
    groups = weight.shape[1] // width
    return pl.pallas_call(
        project_kernel,
        out_shape=[jax.ShapeDtypeStruct((rows, width), BF16)]
        + [jax.ShapeDtypeStruct((rows // 2, width), BF16)] * (2 * groups),
        compiler_params=pltpu.CompilerParams(vmem_limit_bytes=10 * MIB),
        name="project",
    )(weight, packed)


def weight_grad_kernel(att_ref, *refs):
    *grads, keep_ref, give_ref = refs
    groups = (len(grads) + 1) // 2
    grads = members(grads, groups)
    width = grads[0].shape[1]
    part = keep_ref.shape[0]
    core = lax.rem(lax.axis_index("seq"), 2)
    for index, out_ref in ((core, keep_ref), (1 - core, give_ref)):
        att = att_ref[:, columns_of(index, part)]
        for k in range(groups):
            out_ref[:, columns_of(member(k, groups), width)] = lax.dot_general(
                att, grads[k], TN, preferred_element_type=F32
            ).astype(BF16)


def weight_grad(att, grads):
    width = att.shape[1]
    groups = (len(grads) + 1) // 2
    return pl.pallas_call(
        weight_grad_kernel,
        out_shape=[jax.ShapeDtypeStruct((width // 2, width * groups), BF16)] * 2,
        compiler_params=pltpu.CompilerParams(vmem_limit_bytes=10 * MIB),
        name="weight_grad",
    )(att, *grads)


def finished_rows(rows, query_part, key_value):
    low = lane_of(rows.shape) < DH
    scale = DH ** (-0.5)
    query = jnp.where(low, rows.astype(F32), 0.0)
    inverse = inverse_of(query)
    key = query * inverse
    term = key_value * (inverse * scale)
    along = split_sum(key * term, low_lanes(1.0 / DH))
    return jnp.where(low, query_part * scale + term - key * along, key_value)


def backward_kernel(
    addr_ref, mine_ref, other_ref, prob_ref, qv_ref, qv_before, key_ref, key_before,
    home_ref, away_ref,
    tokens, result, in_even, in_odd, out_even, out_odd, qv_win, key_win, tall, sums, query_sums,
    first_sums,
):
    step = pl.program_id(0)
    last = pl.num_programs(0) - 1
    half = mine_ref.shape[0]
    blocks = 2 * half // SPAN
    rows_in = (in_even, in_odd)
    rows_out = (out_even, out_odd)

    @pl.when(step == 0)
    def _():
        tokens[:half, :] = mine_ref[...].astype(F32)
        tokens[half:, :] = other_ref[...].astype(F32)
        for b in range(SUB):
            gather_rows(addr_ref, b, tokens, in_even.at[b])

    qv_win[:SPAN] = qv_before[...]
    qv_win[SPAN:] = qv_ref[...]
    key_win[:SPAN] = key_before[...]
    key_win[SPAN:] = key_ref[...]
    low = lane_of((SPAN, LANES)) < DH
    zero = jnp.zeros((SPAN, LANES), BF16)
    for p in range(GROUP // SUB):
        here = step * GROUP + p * SUB
        coming = jnp.minimum(here + SUB, blocks - SUB)
        gone = here + (blocks - SUB - 1)
        now, then = p % 2, 1 - p % 2
        spans = slice(p * SUB * SPAN, ((p + 1) * SUB + 1) * SPAN)
        everything = qv_win[spans]
        high = lane_of(everything.shape) >= DH
        value_one = jnp.where(high, everything, jnp.ones_like(everything))
        for i in range(SUB):
            b = p * SUB + i
            prob = prob_ref[b]
            dot_grad = lax.dot_general(
                rows_in[now][i].astype(BF16),
                value_one[i * SPAN : (i + 2) * SPAN],
                NT,
                preferred_element_type=F32,
            )
            tall[i, :SPAN] = (prob.astype(F32) * dot_grad).astype(BF16)
            tall[i, SPAN:] = prob
            gather_rows(addr_ref, coming + i, tokens, rows_in[then].at[i])
        for i in range(SUB):
            b = p * SUB + i
            own = slice((b + 1) * SPAN, (b + 2) * SPAN)
            window = slice(b * SPAN, (b + 2) * SPAN)
            query_sums[own] = jnp.dot(
                tall[i, :SPAN], key_win[window], preferred_element_type=F32
            )
            grad_high = jnp.where(low, 0.0, rows_in[now][i]).astype(BF16)
            key_value = lax.dot_general(
                tall[i],
                jnp.concatenate([jnp.where(low, qv_win[own], zero), grad_high], axis=0),
                TN,
                preferred_element_type=F32,
            )
            if b == 0:

                @pl.when(step == 0)
                def _():
                    first_sums[...] = key_value[:SPAN]

            sums[b * SPAN : (b + 1) * SPAN] += key_value[:SPAN]
            sums[own] = key_value[SPAN:]
            scatter_rows(addr_ref, lax.rem(gone + i, blocks), rows_out[then].at[i], result)
        spans = slice(p * SUB * SPAN, (p + 1) * SUB * SPAN)
        finished = finished_rows(qv_win[spans], query_sums[spans], sums[spans])
        rows_out[now][...] = finished.reshape(SUB, SPAN, LANES)
    sums[:SPAN] = sums[GROUP * SPAN :]
    query_sums[:SPAN] = query_sums[GROUP * SPAN :]

    @pl.when(step == last)
    def _():
        for i in range(SUB):
            scatter_rows(addr_ref, blocks - SUB - 1 + i, out_odd.at[i], result)
        out_even[0] = finished_rows(
            qv_win[GROUP * SPAN :], query_sums[:SPAN], sums[:SPAN] + first_sums[...]
        )
        scatter_rows(addr_ref, blocks - 1, out_even.at[0], result)
        home_ref[...] = result[:half, :].astype(BF16)
        away_ref[...] = result[half:, :].astype(BF16)


def backward(addr, mine, other, prob, query_key, value_one):
    half = mine.shape[0]
    total = 2 * half
    blocks = total // SPAN
    rows = GROUP * SPAN
    by_rows = pl.BlockSpec((rows, LANES), lambda g: (g, 0))
    before = pl.BlockSpec((SPAN, LANES), lambda g: (lax.rem(g * GROUP + blocks - 1, blocks), 0))
    return pl.pallas_call(
        backward_kernel,
        grid=(blocks // GROUP,),
        out_shape=[jax.ShapeDtypeStruct((half, LANES), BF16)] * 2,
        in_specs=[
            whole(pltpu.SMEM),
            fixed((half, LANES)),
            fixed((half, LANES)),
            pl.BlockSpec((GROUP, SPAN, 2 * SPAN), lambda g: (g, 0, 0)),
            by_rows,
            before,
            by_rows,
            before,
        ],
        out_specs=[fixed((half, LANES))] * 2,
        scratch_shapes=[
            pltpu.VMEM((total, LANES), F32),
            pltpu.VMEM((total, LANES), F32),
            *[pltpu.VMEM((SUB, SPAN, LANES), F32)] * 4,
            pltpu.VMEM((rows + SPAN, LANES), BF16),
            pltpu.VMEM((rows + SPAN, LANES), BF16),
            pltpu.VMEM((SUB, 2 * SPAN, 2 * SPAN), BF16),
            pltpu.VMEM((rows + SPAN, LANES), F32),
            pltpu.VMEM((rows + SPAN, LANES), F32),
            pltpu.VMEM((SPAN, LANES), F32),
        ],
        compiler_params=pltpu.CompilerParams(vmem_limit_bytes=22 * MIB),
        cost_estimate=pl.CostEstimate(flops=0, bytes_accessed=64 * MIB, transcendentals=0),
        name="span_backward",
    )(addr, mine, other, prob, query_key, query_key, value_one, value_one)


def swap(value, distance=1):
    count = lax.axis_size("seq")
    return lax.ppermute(value, "seq", [(i, i ^ distance) for i in range(count)])


def to_all(value):
    return lax.all_to_all(value, "seq", split_axis=0, concat_axis=0, tiled=True)


def rotate(value, step):
    count = lax.axis_size("head")
    return lax.ppermute(value, "head", [(i, (i + step) % count) for i in range(count)])


def step_along(value, step, count, way):
    pairs = [(i, i + 1) for i in range(step - 1, count - 1)]
    if way < 0:
        pairs = [(count - 1 - i, count - 1 - j) for i, j in pairs]
    return lax.ppermute(value, "head", pairs)


def after(values, *earlier):
    return lax.optimization_barrier((values, earlier))[0]


def by_sequence(queries, values, w_out, out_grad, slots):
    rows = queries.shape[0]
    _, heads, _ = slots.shape
    shards = lax.axis_size("seq")
    groups = lax.axis_size("head")
    core = lax.rem(lax.axis_index("seq"), 2)
    total = shards * rows
    half_rows = rows // 2

    packed = pack_heads(queries, values, slots)
    mine = to_all(packed)
    places = find_places(mine)

    ups, downs = [out_grad], [out_grad]
    for k in range(1, groups):
        ups.append(step_along(ups[-1], k, groups, 1))
        downs.append(step_along(downs[-1], k, groups, -1))
        if k == groups - 2:
            mine = after(mine, ups[-1], downs[-1])
    grads = [*ups, *downs[1:]]

    home, away, prob, query_key, value_one = forward(places[0], mine, swap(mine), *places[1:])
    away, *grads = after([away, *grads])
    peer = swap(away)

    grad_half = to_all(back_projection(w_out, grads))
    att_half, grad_half = after([mixing(home, peer), grad_half])
    att_packed = to_all(att_half)
    grad_own, grad_peer = mixing(home, peer, grad_half)
    grad_peer, att_packed = after([grad_peer, att_packed])
    grad_other = swap(grad_peer)

    att, *shares = project(w_out, att_packed)
    early = [rotate(shares[2 * k], k) for k in range(1, groups)]
    weight, give = weight_grad(att, grads)
    got = swap(give)

    own, others = backward(places[0], grad_own, grad_other, prob, query_key, value_one)
    others, got, *early = after([others, got, *early])
    late = after([shares[2 * k + 1] for k in range(1, groups)], own)
    late = [rotate(late[k - 1], k) for k in range(1, groups)]

    summed = (own.astype(F32) + swap(others).astype(F32)).astype(BF16)
    summed = to_all(summed.reshape(shards, half_rows, LANES))
    query_grad, value_grad = unpack_heads(summed.reshape(heads, rows, LANES))

    weight = (weight.astype(F32) + got.astype(F32)).astype(BF16)
    distance = 2
    while distance < shards:
        weight = (weight.astype(F32) + swap(weight, distance).astype(F32)).astype(BF16)
        distance *= 2
    rest = swap(weight)
    weight = jnp.where(
        core == 0,
        jnp.concatenate([weight, rest], axis=0),
        jnp.concatenate([rest, weight], axis=0),
    )
    w_out_grad = weight.astype(F32) * total ** (-0.5)

    output = []
    for c, received in enumerate((early, late)):
        part = shares[c].astype(F32)
        for share in received:
            part = part + share.astype(F32)
        output.append(part.astype(BF16))
    return (jnp.concatenate(output, axis=0), query_grad, value_grad, w_out_grad)


def shifted(value, axis, steps):
    count = lax.axis_size(axis)
    pairs = [(source, (source + steps) % count) for source in range(count)]
    return lax.ppermute(value, axis, pairs)


def with_before(blocks, before):
    earlier = jnp.concatenate([before[:, None], blocks[:, :-1]], axis=1)
    return jnp.concatenate([blocks, earlier], axis=2)


def normalized(query_rows):
    query_float = query_rows.astype(jnp.float32)
    inverse = lax.rsqrt(jnp.mean(query_float * query_float, axis=-1, keepdims=True) + 1e-06)
    return ((query_float * inverse).astype(jnp.bfloat16), query_float, inverse)


def move_wide(matrix, data, form):
    return jnp.einsum(form, matrix, data, preferred_element_type=jnp.float32).astype(jnp.bfloat16)


def move_exact(matrix, data, form):
    return jnp.einsum(form, matrix, data.astype(jnp.float32), precision=lax.Precision.HIGHEST)


def by_span(queries, values, w_out, out_grad, slots):
    row_count = queries.shape[0]
    head_width = DH
    rounds = slots.shape[0]
    head_group = queries.shape[1] // head_width
    batch_size = rounds * head_group
    shards = lax.axis_size("seq")
    my_index = lax.axis_index("seq")
    even_share = row_count // shards
    capacity = even_share * 3 // 2
    slot_total = shards * capacity
    block_count = row_count // SPAN
    score_scale = head_width ** (-0.5)

    def per_head(matrix):
        split_heads = matrix.reshape(row_count, head_group, head_width).transpose(1, 0, 2)
        return jnp.concatenate([split_heads] * rounds, axis=0)

    flat_slot = slots.reshape(batch_size, row_count)
    target = flat_slot // row_count
    local_slot = flat_slot - target * row_count
    onehot_target = (
        target[:, :, None] == jnp.arange(shards, dtype=jnp.int32)[None, None, :]
    ).astype(jnp.int32)
    earlier_count = jnp.sum(jnp.cumsum(onehot_target, axis=1) * onehot_target, axis=2) - 1
    send_spot = target * capacity + earlier_count
    positions = my_index * row_count + jnp.arange(row_count, dtype=jnp.int32)
    position_rows = jnp.broadcast_to(positions[None, :], (batch_size, row_count))
    pack_float = (
        send_spot[:, None, :] == jnp.arange(slot_total, dtype=jnp.int32)[None, :, None]
    ).astype(jnp.float32)
    pack_half = pack_float.astype(jnp.bfloat16)
    full_grad = lax.all_gather(out_grad, "head", axis=1, tiled=True)
    back_attn = lax.dot_general(
        full_grad, w_out, (((1,), (1,)), ((), ())), preferred_element_type=jnp.float32
    ).astype(jnp.bfloat16)
    query_value = jnp.concatenate([per_head(queries), per_head(values)], axis=2)
    packed_rows = move_wide(pack_half, query_value, "bsr,brd->bsd").reshape(
        batch_size, shards, capacity, 2 * head_width
    )
    packed_place = (
        move_exact(pack_float, position_rows, "bsr,br->bs")
        .astype(jnp.int32)
        .reshape(batch_size, shards, capacity)
    )
    packed_slot = (
        move_exact(pack_float, local_slot + 1, "bsr,br->bs")
        .astype(jnp.int32)
        .reshape(batch_size, shards, capacity)
    )
    got_rows, got_place, got_slot = (
        lax.all_to_all(packed_rows, "seq", split_axis=1, concat_axis=1, tiled=True),
        lax.all_to_all(packed_place, "seq", split_axis=1, concat_axis=1, tiled=True),
        lax.all_to_all(packed_slot, "seq", split_axis=1, concat_axis=1, tiled=True),
    )
    got_spot = got_slot.reshape(batch_size, slot_total)
    got_spot = jnp.where(got_spot == 0, row_count, got_spot - 1)
    sort_float = (
        got_spot[:, :, None] == jnp.arange(row_count, dtype=jnp.int32)[None, None, :]
    ).astype(jnp.float32)
    sort_half = sort_float.astype(jnp.bfloat16)
    sorted_rows = move_wide(
        sort_half, got_rows.reshape(batch_size, slot_total, 2 * head_width), "bsr,bsd->brd"
    )
    sorted_place = move_exact(
        sort_float, got_place.reshape(batch_size, slot_total), "bsr,bs->br"
    ).astype(jnp.int32)
    last_rows = sorted_rows[:, row_count - SPAN :]
    last_place = sorted_place[:, row_count - SPAN :]
    before_rows, before_place = shifted((last_rows, last_place), "seq", 1)
    sorted_query = sorted_rows[:, :, :head_width]
    sorted_value = sorted_rows[:, :, head_width:]
    sorted_key, query_float, inverse = normalized(sorted_query)
    before_key = normalized(before_rows[:, :, :head_width])[0]
    query_blocks = sorted_query.reshape(batch_size, block_count, SPAN, head_width)
    key_window = with_before(
        sorted_key.reshape(batch_size, block_count, SPAN, head_width), before_key
    )
    value_window = with_before(
        sorted_value.reshape(batch_size, block_count, SPAN, head_width),
        before_rows[:, :, head_width:],
    )
    place_blocks = sorted_place.reshape(batch_size, block_count, SPAN)
    place_window = with_before(place_blocks, before_place)
    own_token = (jnp.arange(SPAN)[:, None] == jnp.arange(2 * SPAN)[None, :]).astype(jnp.float32)
    future = (place_window[:, :, None, :] > place_blocks[:, :, :, None]).astype(jnp.float32)

    def score_of():
        raw_scores = (
            jnp.einsum(
                "bcqd,bckd->bcqk", query_blocks, key_window, preferred_element_type=jnp.float32
            )
            * score_scale
        )
        return raw_scores - 100000.0 * own_token - 1000000000.0 * future

    scores = score_of()
    row_top = jnp.max(scores, axis=-1)
    log_total = row_top + jnp.log(jnp.sum(jnp.exp(scores - row_top[..., None]), axis=-1))
    weights = jnp.exp(scores - log_total[..., None])
    rounded_probs = weights.astype(jnp.bfloat16)
    block_out = jnp.einsum(
        "bcqk,bckd->bcqd", rounded_probs, value_window, preferred_element_type=jnp.float32
    ).astype(jnp.bfloat16)
    out_rows = block_out.reshape(batch_size, row_count, head_width)
    home_out = move_wide(sort_half, out_rows, "bsr,brd->bsd").reshape(
        batch_size, shards, capacity // 2, 2 * head_width
    )
    home_log = move_exact(
        sort_float, log_total.reshape(batch_size, row_count), "bsr,br->bs"
    ).reshape(batch_size, shards, capacity)
    back_out, back_log = (
        lax.all_to_all(home_out, "seq", split_axis=1, concat_axis=1, tiled=True),
        lax.all_to_all(
            home_log.astype(jnp.bfloat16), "seq", split_axis=1, concat_axis=1, tiled=True
        ).astype(home_log.dtype),
    )
    round_out = move_wide(
        pack_half, back_out.reshape(batch_size, slot_total, head_width), "bsr,bsd->brd"
    ).reshape(rounds, head_group, row_count, head_width)
    round_log = move_exact(
        pack_float, back_log.reshape(batch_size, slot_total), "bsr,bs->br"
    ).reshape(rounds, head_group, row_count)
    mixing = jax.nn.softmax(round_log, axis=0)
    combined = jnp.sum(mixing[..., None] * round_out.astype(jnp.float32), axis=0)
    attention = (
        combined.astype(jnp.bfloat16).transpose(1, 0, 2).reshape(row_count, head_group * head_width)
    )
    head_term = jnp.dot(attention, w_out, preferred_element_type=jnp.float32)
    output = lax.psum_scatter(
        head_term.astype(jnp.bfloat16), "head", scatter_dimension=1, tiled=True
    )
    weight_term = lax.dot_general(
        attention, full_grad, (((0,), (0,)), ((), ())), preferred_element_type=jnp.float32
    )
    w_out_grad = lax.psum(weight_term.astype(jnp.bfloat16), "seq").astype(jnp.float32) * (
        shards * row_count
    ) ** (-0.5)
    back_heads = (
        back_attn.reshape(row_count, head_group, head_width).transpose(1, 0, 2).astype(jnp.float32)
    )
    inner_rows = jnp.sum(back_heads * combined, axis=-1)
    delta_rows = (mixing * inner_rows[None]).reshape(batch_size, row_count)
    grad_rows = (
        (mixing[..., None] * back_heads[None])
        .astype(jnp.bfloat16)
        .reshape(batch_size, row_count, head_width)
    )
    packed_grad = move_wide(pack_half, grad_rows, "bsr,brd->bsd").reshape(
        batch_size, shards, capacity // 2, 2 * head_width
    )
    packed_delta = move_exact(pack_float, delta_rows, "bsr,br->bs").reshape(
        batch_size, shards, capacity
    )
    got_grad, got_delta = (
        lax.all_to_all(packed_grad, "seq", split_axis=1, concat_axis=1, tiled=True),
        lax.all_to_all(
            packed_delta.astype(jnp.bfloat16), "seq", split_axis=1, concat_axis=1, tiled=True
        ).astype(packed_delta.dtype),
    )
    sorted_grad = move_wide(
        sort_half, got_grad.reshape(batch_size, slot_total, head_width), "bsr,bsd->brd"
    )
    sorted_delta = move_exact(sort_float, got_delta.reshape(batch_size, slot_total), "bsr,bs->br")
    kept_weights = jnp.exp(score_of() - log_total[..., None])
    grad_blocks = sorted_grad.reshape(batch_size, block_count, SPAN, head_width)
    delta_blocks = sorted_delta.reshape(batch_size, block_count, SPAN)
    dot_grad = jnp.einsum(
        "bcqd,bckd->bcqk", grad_blocks, value_window, preferred_element_type=jnp.float32
    )
    score_grad = (kept_weights * (dot_grad - delta_blocks[..., None])).astype(jnp.bfloat16)
    query_part = (
        jnp.einsum("bcqk,bckd->bcqd", score_grad, key_window, preferred_element_type=jnp.float32)
        * score_scale
    )
    key_part = (
        jnp.einsum("bcqk,bcqd->bckd", score_grad, query_blocks, preferred_element_type=jnp.float32)
        * score_scale
    )
    value_part = jnp.einsum(
        "bcqk,bcqd->bckd", rounded_probs, grad_blocks, preferred_element_type=jnp.float32
    )
    spill_rows = jnp.concatenate([key_part[:, 0, SPAN:], value_part[:, 0, SPAN:]], axis=2)
    arrived = shifted(spill_rows.astype(jnp.bfloat16), "seq", -1).astype(spill_rows.dtype)
    key_grad = key_part[:, :, :SPAN] + jnp.concatenate(
        [key_part[:, 1:, SPAN:], arrived[:, None, :, :head_width]], axis=1
    )
    value_sum = value_part[:, :, :SPAN] + jnp.concatenate(
        [value_part[:, 1:, SPAN:], arrived[:, None, :, head_width:]], axis=1
    )
    key_grad = key_grad.reshape(batch_size, row_count, head_width)
    value_sum = value_sum.reshape(batch_size, row_count, head_width)
    query_total = (
        query_part.reshape(batch_size, row_count, head_width)
        + inverse * key_grad
        - query_float
        * (inverse * inverse * inverse)
        * jnp.mean(query_float * key_grad, axis=-1, keepdims=True)
    )
    both_grads = jnp.concatenate(
        [query_total.astype(jnp.bfloat16), value_sum.astype(jnp.bfloat16)], axis=2
    )
    home_grads = move_wide(sort_half, both_grads, "bsr,brd->bsd").reshape(
        batch_size, shards, capacity, 2 * head_width
    )
    back_grads = lax.all_to_all(home_grads, "seq", split_axis=1, concat_axis=1, tiled=True)
    own_grads = move_wide(
        pack_half, back_grads.reshape(batch_size, slot_total, 2 * head_width), "bsr,bsd->brd"
    ).astype(jnp.float32)
    own_grads = own_grads.reshape(rounds, head_group, row_count, 2 * head_width)
    summed = jnp.sum(own_grads, axis=0).astype(jnp.bfloat16)
    query_grad = (
        summed[:, :, :head_width].transpose(1, 0, 2).reshape(row_count, head_group * head_width)
    )
    value_grad = (
        summed[:, :, head_width:].transpose(1, 0, 2).reshape(row_count, head_group * head_width)
    )
    return (output, query_grad, value_grad, w_out_grad)


def per_device(queries, values, w_out, out_grad, slots):
    if lax.axis_size("seq") == slots.shape[0] * slots.shape[1] and slots.shape[0] == 2:
        return by_sequence(queries, values, w_out, out_grad, slots)
    return by_span(queries, values, w_out, out_grad, slots)


def solution(mesh):
    placed = (
        P("seq", "head"),
        P("seq", "head"),
        P("head", None),
        P("seq", "head"),
        P(None, "head", "seq"),
    )
    return jax.shard_map(
        per_device,
        mesh=mesh,
        in_specs=placed,
        out_specs=(P("seq", "head"), P("seq", "head"), P("seq", "head"), P("head", None)),
        check_vma=False,
    )
```

```python
import functools

import jax
import jax.numpy as jnp
from jax import lax
from jax.experimental import pallas as pl
from jax.experimental.pallas import tpu as pltpu
from jax.sharding import PartitionSpec as P

DH = 64
SPAN = 128
LANES = 128
GROUP = 8
SUB = 4
F32 = jnp.float32
BF16 = jnp.bfloat16
NT = (((1,), (1,)), ((), ()))
TN = (((0,), (0,)), ((), ()))
MIB = 1 << 20


def whole(space):
    return pl.BlockSpec(memory_space=space)


def in_hbm(value):
    return pltpu.with_memory_space_constraint(value, pltpu.HBM)


def fixed(shape):
    return pl.BlockSpec(shape, lambda g: (0,) * len(shape), pipeline_mode=pl.Buffered(1))


def lane_of(shape):
    return lax.broadcasted_iota(jnp.int32, shape, len(shape) - 1)


def places_kernel(mine_ref, addr_ref, key_place, query_place, sign_ref):
    sources, _, lanes = mine_ref.shape
    blocks = addr_ref.shape[0]
    rows = mine_ref.shape[1] - 16
    parts = (mine_ref.shape[1] - rows) // 2
    core = lax.rem(lax.axis_index("seq"), 2)
    block_row = lax.broadcasted_iota(jnp.int32, (blocks, lanes), 0).astype(F32)
    place_row = lax.broadcasted_iota(jnp.int32, (lanes, lanes), 0).astype(F32)
    token_low = lane_of((blocks, lanes)).astype(F32)
    total = jnp.zeros((2 * blocks, lanes), F32)
    for s in range(sources):
        slots = mine_ref[s, rows:, :].astype(F32)
        tall = []
        wide = []
        for j in range(parts):
            in_block = block_row == slots[j : j + 1, :]
            token_high = float(s * parts + j)
            tall.append(
                jnp.concatenate(
                    [jnp.where(in_block, token_high, 0.0), jnp.where(in_block, token_low, 0.0)],
                    axis=0,
                ).astype(BF16)
            )
            wide.append((place_row == slots[parts + j : parts + j + 1, :]).astype(BF16))
        total += lax.dot_general(
            jnp.concatenate(tall, axis=1),
            jnp.concatenate(wide, axis=1),
            NT,
            preferred_element_type=F32,
        )
    place = total[:blocks] * float(lanes) + total[blocks:]
    token = place.astype(jnp.int32)
    source = token // (2 * rows)
    within = token - source * (2 * rows)
    part = within // rows
    addr_ref[...] = ((part ^ core) * sources + source) * rows + (within - part * rows)
    before = pltpu.roll(place, 1, 0)
    least = jnp.minimum(
        jnp.min(place, axis=1, keepdims=True), jnp.min(before, axis=1, keepdims=True)
    )
    window = jnp.concatenate([before, place], axis=1)
    window = jnp.where(window == least, window - 0.5, window)
    for c in range(blocks):
        key_place[c] = window[c : c + 1, :]
    columns = jnp.transpose(place)
    alone = jnp.transpose(jnp.where(place == least, -1.0, 1.0))
    for g in range(blocks // GROUP):
        query_place[g] = columns[:, g * GROUP : (g + 1) * GROUP]
        sign_ref[g] = alone[:, g * GROUP : (g + 1) * GROUP]


def find_places(mine):
    sources, rows, lanes = mine.shape
    blocks = 2 * sources * (rows - 16) // lanes
    column = jax.ShapeDtypeStruct((blocks // GROUP, lanes, GROUP), F32)
    return pl.pallas_call(
        places_kernel,
        out_shape=[
            jax.ShapeDtypeStruct((blocks, lanes), jnp.int32),
            jax.ShapeDtypeStruct((blocks, 1, 2 * lanes), F32),
            column,
            column,
        ],
        compiler_params=pltpu.CompilerParams(vmem_limit_bytes=10 * MIB),
        name="find_places",
    )(mine)


def gather_rows(addr_ref, block, source, target):
    for j in range(SPAN):
        target[pl.ds(j, 1), :] = source[pl.ds(addr_ref[block, j], 1), :]


def scatter_rows(addr_ref, block, source, target):
    for j in range(SPAN):
        target[pl.ds(addr_ref[block, j], 1), :] = source[pl.ds(j, 1), :]


def split_sum(product, chosen):
    high = product.astype(BF16)
    rest = (product - high.astype(F32)).astype(BF16)
    return jnp.dot(
        jnp.concatenate([high, rest], axis=1),
        jnp.concatenate([chosen, chosen], axis=0),
        preferred_element_type=F32,
    )


def low_lanes(scale=1.0):
    row = lax.broadcasted_iota(jnp.int32, (LANES, LANES), 0)
    return jnp.where(row < DH, scale, 0.0).astype(BF16)


def inverse_of(rows):
    return lax.rsqrt(split_sum(rows * rows, low_lanes(1.0 / DH)) + 1e-06)


def forward_kernel(
    addr_ref, mine_ref, other_ref, key_place, query_place, sign_ref,
    home_ref, away_ref, prob_ref, qv_ref, key_ref,
    tokens, result, in_even, in_odd, out_even, out_odd, grown_ref, qv_win, key_win,
):
    step = pl.program_id(0)
    last = pl.num_programs(0) - 1
    sources = mine_ref.shape[0]
    rows = mine_ref.shape[1] - 16
    half = sources * rows
    blocks = 2 * half // SPAN
    score_scale = DH ** (-0.5) * 1.4426950408889634
    rows_in = (in_even, in_odd)
    rows_out = (out_even, out_odd)

    def place_rows(values, at):
        low = lane_of(values.shape) < DH
        qv_win[at] = values.astype(BF16)
        key_win[at] = jnp.where(low, values * inverse_of(values), 0.0).astype(BF16)

    @pl.when(step == 0)
    def _():
        for s in range(sources):
            tokens[s * rows : (s + 1) * rows, :] = mine_ref[s, :rows, :].astype(F32)
            tokens[half + s * rows : half + (s + 1) * rows, :] = other_ref[s, :rows, :].astype(F32)
        gather_rows(addr_ref, blocks - 1, tokens, in_odd.at[0])
        place_rows(in_odd[0], slice(0, SPAN))
        for b in range(SUB):
            gather_rows(addr_ref, b, tokens, in_even.at[b])

    ones = jnp.ones((2 * SPAN, LANES), BF16)
    low = lane_of((SPAN, LANES)) < DH
    for p in range(GROUP // SUB):
        here = step * GROUP + p * SUB
        coming = jnp.minimum(here + SUB, blocks - SUB)
        gone = jnp.maximum(here - SUB, 0)
        now, then = p % 2, 1 - p % 2
        spans = slice((p * SUB + 1) * SPAN, ((p + 1) * SUB + 1) * SPAN)
        place_rows(rows_in[now][...].reshape(SUB * SPAN, LANES), spans)
        for i in range(SUB):
            b = p * SUB + i
            own = slice((b + 1) * SPAN, (b + 2) * SPAN)
            window = slice(b * SPAN, (b + 2) * SPAN)
            raw = lax.dot_general(qv_win[own], key_win[window], NT, preferred_element_type=F32)
            seen = key_place[b] < query_place[0, :, b : b + 1]
            grown_ref[i] = jnp.where(seen, jnp.exp2(raw * score_scale), 0.0)
            gather_rows(addr_ref, coming + i, tokens, rows_in[then].at[i])
        for i in range(SUB):
            b = p * SUB + i
            window = slice(b * SPAN, (b + 2) * SPAN)
            grown = grown_ref[i]
            mixed = jnp.dot(
                grown.astype(BF16),
                jnp.concatenate([qv_win[window], ones], axis=1),
                preferred_element_type=F32,
            )
            sums = mixed[:, LANES:]
            recip = 1.0 / sums
            prob_ref[b] = (grown * jnp.concatenate([recip, recip], axis=1)).astype(BF16)
            signed = sums * sign_ref[0, :, b : b + 1]
            rows_out[now][i] = jnp.where(low, signed, mixed[:, :LANES] * recip)
            scatter_rows(addr_ref, gone + i, rows_out[then].at[i], result)

    qv_ref[...] = qv_win[SPAN:]
    key_ref[...] = key_win[SPAN:]
    qv_win[:SPAN] = qv_win[GROUP * SPAN :]
    key_win[:SPAN] = key_win[GROUP * SPAN :]

    @pl.when(step == last)
    def _():
        for i in range(SUB):
            scatter_rows(addr_ref, blocks - SUB + i, out_odd.at[i], result)
        home_ref[...] = result[:half, :].astype(BF16)
        away_ref[...] = result[half:, :].astype(BF16)


def forward(addr, mine, other, key_place, query_place, sign):
    half = mine.shape[0] * (mine.shape[1] - 16)
    total = 2 * half
    blocks = total // SPAN
    rows = GROUP * SPAN
    return pl.pallas_call(
        forward_kernel,
        grid=(blocks // GROUP,),
        out_shape=[
            jax.ShapeDtypeStruct((half, LANES), BF16),
            jax.ShapeDtypeStruct((half, LANES), BF16),
            pltpu.HBM((blocks, SPAN, 2 * SPAN), BF16),
            pltpu.HBM((total, LANES), BF16),
            pltpu.HBM((total, LANES), BF16),
        ],
        in_specs=[
            whole(pltpu.SMEM),
            fixed(mine.shape),
            fixed(mine.shape),
            pl.BlockSpec((GROUP, 1, 2 * SPAN), lambda g: (g, 0, 0)),
            pl.BlockSpec((1, SPAN, GROUP), lambda g: (g, 0, 0)),
            pl.BlockSpec((1, SPAN, GROUP), lambda g: (g, 0, 0)),
        ],
        out_specs=[
            fixed((half, LANES)),
            fixed((half, LANES)),
            pl.BlockSpec((GROUP, SPAN, 2 * SPAN), lambda g: (g, 0, 0)),
            pl.BlockSpec((rows, LANES), lambda g: (g, 0)),
            pl.BlockSpec((rows, LANES), lambda g: (g, 0)),
        ],
        scratch_shapes=[
            pltpu.VMEM((total, LANES), F32),
            pltpu.VMEM((total, LANES), F32),
            *[pltpu.VMEM((SUB, SPAN, LANES), F32)] * 4,
            pltpu.VMEM((SUB, SPAN, 2 * SPAN), F32),
            pltpu.VMEM((rows + SPAN, LANES), BF16),
            pltpu.VMEM((rows + SPAN, LANES), BF16),
        ],
        compiler_params=pltpu.CompilerParams(vmem_limit_bytes=22 * MIB),
        cost_estimate=pl.CostEstimate(flops=0, bytes_accessed=64 * MIB, transcendentals=0),
        name="span_forward",
    )(addr, mine, other, key_place, query_place, sign)


def share_of(own, peer):
    row = lax.broadcasted_iota(jnp.int32, (LANES, LANES), 0)
    pick = (row < 1).astype(BF16)
    own_sum = jnp.dot(own, pick, preferred_element_type=F32)
    peer_sum = jnp.dot(peer, pick, preferred_element_type=F32)
    both = own_sum / (own_sum + peer_sum)
    own_alone = own_sum < 0.0
    peer_alone = peer_sum < 0.0
    return jnp.where(
        own_alone, jnp.where(peer_alone, both, 0.0), jnp.where(peer_alone, 1.0, both)
    )


def combined_rows(own, peer, share):
    high = lane_of(own.shape) >= DH
    own = own.astype(F32)
    peer = peer.astype(F32)
    return jnp.where(high, share * own + (1.0 - share) * peer, 0.0)


def mix_attention_kernel(own_ref, peer_ref, att_ref):
    pieces = att_ref.shape[0]
    rows = own_ref.shape[0] // pieces
    half = rows // 2
    for i in range(pieces):
        own = own_ref[i * rows : (i + 1) * rows]
        peer = peer_ref[i * rows : (i + 1) * rows]
        combined = combined_rows(own, peer, share_of(own, peer))
        att_ref[i] = (pltpu.roll(combined[:half], DH, 1) + combined[half:]).astype(BF16)


def mix_grad_kernel(own_ref, peer_ref, grad_ref, grad_own, grad_peer):
    pieces = grad_ref.shape[0]
    rows = own_ref.shape[0] // pieces
    for i in range(pieces):
        at = slice(i * rows, (i + 1) * rows)
        own = own_ref[at]
        peer = peer_ref[at]
        share = share_of(own, peer)
        combined = combined_rows(own, peer, share)
        packed = grad_ref[i].astype(F32)
        grad = jnp.concatenate([pltpu.roll(packed, DH, 1), packed], axis=0)
        column = lane_of((LANES, LANES))
        inner = split_sum(grad * combined, (column < DH).astype(BF16))
        both = jnp.where(lane_of(grad.shape) < DH, -inner, grad)
        grad_own[at] = (share * both).astype(BF16)
        grad_peer[at] = ((1.0 - share) * both).astype(BF16)


def mixing(home, peer, grad=None):
    half = peer.shape[0]
    pieces = lax.axis_size("seq")
    rows = half // pieces
    by_rows = pl.BlockSpec((4 * rows, LANES), lambda g: (g, 0))
    packed = pl.BlockSpec((4, rows // 2, LANES), lambda g: (g, 0, 0))
    cost = pl.CostEstimate(flops=0, bytes_accessed=10 * MIB, transcendentals=0)
    if grad is None:
        return pl.pallas_call(
            mix_attention_kernel,
            grid=(pieces // 4,),
            out_shape=jax.ShapeDtypeStruct((pieces, rows // 2, LANES), BF16),
            in_specs=[by_rows, by_rows],
            out_specs=packed,
            cost_estimate=cost,
            name="mix_attention",
        )(home, peer)
    return pl.pallas_call(
        mix_grad_kernel,
        grid=(pieces // 4,),
        out_shape=[jax.ShapeDtypeStruct((half, LANES), BF16)] * 2,
        in_specs=[by_rows, by_rows, packed],
        out_specs=[by_rows, by_rows],
        cost_estimate=cost,
        name="mix_grad",
    )(home, peer, grad)


def pack_kernel(query_ref, value_ref, slot_ref, out_ref):
    rounds, heads, rows = slot_ref.shape
    half = rows // 2
    for h in range(heads):
        columns = slice(h * DH, (h + 1) * DH)
        pair = jnp.concatenate([query_ref[:, columns], value_ref[:, columns]], axis=1)
        for r in range(rounds):
            out_ref[2 * h + r, :half] = pair[r * half : (r + 1) * half]
            slots = slot_ref[r, h : h + 1, :]
            high = slots // LANES
            parts = [high, slots - high * LANES]
            lines = [p[:, j : j + LANES] for p in parts for j in range(0, rows, LANES)]
            out_ref[2 * h + r, half:] = jnp.concatenate(lines, axis=0).astype(F32).astype(BF16)


def pack_heads(queries, values, slots):
    rounds, heads, rows = slots.shape
    return pl.pallas_call(
        pack_kernel,
        out_shape=jax.ShapeDtypeStruct((rounds * heads, rows // 2 + 16, 2 * DH), BF16),
        compiler_params=pltpu.CompilerParams(vmem_limit_bytes=10 * MIB),
        name="pack_heads",
    )(in_hbm(queries), in_hbm(values), slots)


def unpack_kernel(in_ref, query_ref, value_ref):
    for h in range(in_ref.shape[0]):
        columns = slice(h * DH, (h + 1) * DH)
        query_ref[:, columns] = in_ref[h, :, :DH]
        value_ref[:, columns] = in_ref[h, :, DH:]


def unpack_heads(rows):
    heads, count, _ = rows.shape
    return pl.pallas_call(
        unpack_kernel,
        out_shape=[jax.ShapeDtypeStruct((count, heads * DH), BF16)] * 2,
        name="unpack_heads",
    )(rows)


def member(step, groups):
    return lax.rem(lax.axis_index("head") + (groups - step), groups)


def columns_of(index, width):
    return pl.ds(pl.multiple_of(index * width, width), width)


def back_kernel(weight_ref, *refs):
    *grads, out_ref = refs
    groups = len(grads)
    rows, width = grads[0].shape
    total = 0.0
    for k in range(groups):
        weight = weight_ref[:, columns_of(member(k, groups), width)]
        total += lax.dot_general(grads[k][...], weight, NT, preferred_element_type=F32)
    total = total.astype(BF16)
    quarter = rows // 4
    for h in range(width // DH):
        columns = slice(h * DH, (h + 1) * DH)
        for c in range(2):
            first = total[2 * c * quarter : (2 * c + 1) * quarter, columns]
            second = total[(2 * c + 1) * quarter : (2 * c + 2) * quarter, columns]
            out_ref[2 * h + c] = jnp.concatenate([first, second], axis=1)


def back_projection(weight, grads):
    rows, width = grads[0].shape
    return pl.pallas_call(
        back_kernel,
        out_shape=jax.ShapeDtypeStruct((2 * width // DH, rows // 4, 2 * DH), BF16),
        compiler_params=pltpu.CompilerParams(vmem_limit_bytes=10 * MIB),
        name="back_projection",
    )(weight, *grads)


def project_kernel(weight_ref, packed_ref, att_ref, *outs):
    groups = len(outs)
    rows, width = att_ref.shape
    quarter = rows // 4
    for h in range(width // DH):
        columns = slice(h * DH, (h + 1) * DH)
        for c in range(2):
            packed = packed_ref[2 * h + c]
            att_ref[2 * c * quarter : (2 * c + 1) * quarter, columns] = packed[:, :DH]
            att_ref[(2 * c + 1) * quarter : (2 * c + 2) * quarter, columns] = packed[:, DH:]
    for k in range(groups):
        weight = weight_ref[:, columns_of(member(groups - k, groups), width)]
        outs[k][...] = jnp.dot(att_ref[...], weight, preferred_element_type=F32).astype(BF16)


def project(weight, packed):
    count, quarter, _ = packed.shape
    rows, width = 4 * quarter, count * DH // 2
    groups = weight.shape[1] // width
    return pl.pallas_call(
        project_kernel,
        out_shape=[jax.ShapeDtypeStruct((rows, width), BF16)] * (1 + groups),
        compiler_params=pltpu.CompilerParams(vmem_limit_bytes=10 * MIB),
        name="project",
    )(weight, packed)


def weight_grad_kernel(att_ref, *refs):
    *grads, keep_ref, give_ref = refs
    groups = len(grads)
    width = grads[0].shape[1]
    part = keep_ref.shape[0]
    core = lax.rem(lax.axis_index("seq"), 2)
    for index, out_ref in ((core, keep_ref), (1 - core, give_ref)):
        att = att_ref[:, columns_of(index, part)]
        for k in range(groups):
            out_ref[:, columns_of(member(k, groups), width)] = lax.dot_general(
                att, grads[k][...], TN, preferred_element_type=F32
            ).astype(BF16)


def weight_grad(att, grads):
    width = att.shape[1]
    groups = len(grads)
    return pl.pallas_call(
        weight_grad_kernel,
        out_shape=[jax.ShapeDtypeStruct((width // 2, width * groups), BF16)] * 2,
        compiler_params=pltpu.CompilerParams(vmem_limit_bytes=10 * MIB),
        name="weight_grad",
    )(att, *grads)


def finished_rows(rows, query_part, key_value):
    low = lane_of(rows.shape) < DH
    scale = DH ** (-0.5)
    query = jnp.where(low, rows.astype(F32), 0.0)
    inverse = inverse_of(query)
    key = query * inverse
    term = key_value * (inverse * scale)
    along = split_sum(key * term, low_lanes(1.0 / DH))
    return jnp.where(low, query_part * scale + term - key * along, key_value)


def backward_kernel(
    addr_ref, mine_ref, other_ref, prob_ref, qv_ref, qv_before, key_ref, key_before,
    home_ref, away_ref,
    tokens, result, in_even, in_odd, out_even, out_odd, qv_win, key_win, tall, sums, query_sums,
    first_sums,
):
    step = pl.program_id(0)
    last = pl.num_programs(0) - 1
    half = mine_ref.shape[0]
    blocks = 2 * half // SPAN
    rows_in = (in_even, in_odd)
    rows_out = (out_even, out_odd)

    @pl.when(step == 0)
    def _():
        tokens[:half, :] = mine_ref[...].astype(F32)
        tokens[half:, :] = other_ref[...].astype(F32)
        for b in range(SUB):
            gather_rows(addr_ref, b, tokens, in_even.at[b])

    qv_win[:SPAN] = qv_before[...]
    qv_win[SPAN:] = qv_ref[...]
    key_win[:SPAN] = key_before[...]
    key_win[SPAN:] = key_ref[...]
    low = lane_of((SPAN, LANES)) < DH
    zero = jnp.zeros((SPAN, LANES), BF16)
    for p in range(GROUP // SUB):
        here = step * GROUP + p * SUB
        coming = jnp.minimum(here + SUB, blocks - SUB)
        gone = here + (blocks - SUB - 1)
        now, then = p % 2, 1 - p % 2
        spans = slice(p * SUB * SPAN, ((p + 1) * SUB + 1) * SPAN)
        everything = qv_win[spans]
        lane = lane_of(everything.shape)
        one = jnp.where(lane == 0, 1.0, 0.0).astype(BF16)
        value_one = jnp.where(lane >= DH, everything, one)
        for i in range(SUB):
            b = p * SUB + i
            prob = prob_ref[b]
            dot_grad = lax.dot_general(
                rows_in[now][i].astype(BF16),
                value_one[i * SPAN : (i + 2) * SPAN],
                NT,
                preferred_element_type=F32,
            )
            tall[i, :SPAN] = (prob.astype(F32) * dot_grad).astype(BF16)
            tall[i, SPAN:] = prob
            gather_rows(addr_ref, coming + i, tokens, rows_in[then].at[i])
        for i in range(SUB):
            b = p * SUB + i
            own = slice((b + 1) * SPAN, (b + 2) * SPAN)
            window = slice(b * SPAN, (b + 2) * SPAN)
            query_sums[own] = jnp.dot(
                tall[i, :SPAN], key_win[window], preferred_element_type=F32
            )
            grad_high = jnp.where(low, 0.0, rows_in[now][i]).astype(BF16)
            key_value = lax.dot_general(
                tall[i],
                jnp.concatenate([jnp.where(low, qv_win[own], zero), grad_high], axis=0),
                TN,
                preferred_element_type=F32,
            )
            if b == 0:

                @pl.when(step == 0)
                def _():
                    first_sums[...] = key_value[:SPAN]

            sums[b * SPAN : (b + 1) * SPAN] += key_value[:SPAN]
            sums[own] = key_value[SPAN:]
            scatter_rows(addr_ref, lax.rem(gone + i, blocks), rows_out[then].at[i], result)
        spans = slice(p * SUB * SPAN, (p + 1) * SUB * SPAN)
        finished = finished_rows(qv_win[spans], query_sums[spans], sums[spans])
        rows_out[now][...] = finished.reshape(SUB, SPAN, LANES)
    sums[:SPAN] = sums[GROUP * SPAN :]
    query_sums[:SPAN] = query_sums[GROUP * SPAN :]

    @pl.when(step == last)
    def _():
        for i in range(SUB):
            scatter_rows(addr_ref, blocks - SUB - 1 + i, out_odd.at[i], result)
        out_even[0] = finished_rows(
            qv_win[GROUP * SPAN :], query_sums[:SPAN], sums[:SPAN] + first_sums[...]
        )
        scatter_rows(addr_ref, blocks - 1, out_even.at[0], result)
        home_ref[...] = result[:half, :].astype(BF16)
        away_ref[...] = result[half:, :].astype(BF16)


def backward(addr, mine, other, prob, query_key, value_one):
    half = mine.shape[0]
    total = 2 * half
    blocks = total // SPAN
    rows = GROUP * SPAN
    by_rows = pl.BlockSpec((rows, LANES), lambda g: (g, 0))
    before = pl.BlockSpec((SPAN, LANES), lambda g: (lax.rem(g * GROUP + blocks - 1, blocks), 0))
    return pl.pallas_call(
        backward_kernel,
        grid=(blocks // GROUP,),
        out_shape=[jax.ShapeDtypeStruct((half, LANES), BF16)] * 2,
        in_specs=[
            whole(pltpu.SMEM),
            fixed((half, LANES)),
            fixed((half, LANES)),
            pl.BlockSpec((GROUP, SPAN, 2 * SPAN), lambda g: (g, 0, 0)),
            by_rows,
            before,
            by_rows,
            before,
        ],
        out_specs=[fixed((half, LANES))] * 2,
        scratch_shapes=[
            pltpu.VMEM((total, LANES), F32),
            pltpu.VMEM((total, LANES), F32),
            *[pltpu.VMEM((SUB, SPAN, LANES), F32)] * 4,
            pltpu.VMEM((rows + SPAN, LANES), BF16),
            pltpu.VMEM((rows + SPAN, LANES), BF16),
            pltpu.VMEM((SUB, 2 * SPAN, 2 * SPAN), BF16),
            pltpu.VMEM((rows + SPAN, LANES), F32),
            pltpu.VMEM((rows + SPAN, LANES), F32),
            pltpu.VMEM((SPAN, LANES), F32),
        ],
        compiler_params=pltpu.CompilerParams(vmem_limit_bytes=22 * MIB),
        cost_estimate=pl.CostEstimate(flops=0, bytes_accessed=64 * MIB, transcendentals=0),
        name="span_backward",
    )(addr, mine, other, *[in_hbm(x) for x in (prob, query_key, query_key, value_one, value_one)])


def swap(value, distance=1):
    count = lax.axis_size("seq")
    return lax.ppermute(value, "seq", [(i, i ^ distance) for i in range(count)])


def to_all(value):
    return lax.all_to_all(value, "seq", split_axis=0, concat_axis=0, tiled=True)


def rotate(value, step):
    count = lax.axis_size("head")
    return lax.ppermute(value, "head", [(i, (i + step) % count) for i in range(count)])


def after(values, *earlier):
    return lax.optimization_barrier((values, earlier))[0]


def by_sequence(queries, values, w_out, out_grad, slots):
    rows = queries.shape[0]
    _, heads, _ = slots.shape
    shards = lax.axis_size("seq")
    groups = lax.axis_size("head")
    core = lax.rem(lax.axis_index("seq"), 2)
    total = shards * rows
    half_rows = rows // 2

    packed = pack_heads(queries, values, slots)
    mine = to_all(packed)
    places = find_places(mine)

    first = rotate(out_grad, 1)
    grads = [out_grad, first, rotate(first, 1), rotate(out_grad, groups - 1)]
    mine = after(mine, *grads[1:3])

    home, away, prob, query_key, value_one = forward(places[0], mine, swap(mine), *places[1:])
    away, *grads = after([away, *grads])
    peer = swap(away)

    grad_half = to_all(back_projection(w_out, grads))
    att_half, grad_half = after([mixing(home, peer), grad_half])
    att_packed = to_all(att_half)
    grad_own, grad_peer = mixing(home, peer, grad_half)
    grad_peer, att_packed = after([grad_peer, att_packed])
    grad_other = swap(grad_peer)

    att, *shares = project(w_out, att_packed)
    early = [rotate(shares[k], k) for k in range(1, groups, 2)]
    weight, give = weight_grad(att, grads)
    weight = (weight.astype(F32) + swap(give).astype(F32)).astype(BF16)
    weights = [weight] + [swap(weight, distance) for distance in range(2, shards, 2)]

    own, others = backward(places[0], grad_own, grad_other, prob, query_key, value_one)
    others, *weights = after([others, *weights])
    others, *early = after([others, *early])
    late = [rotate(after(shares[k], own), k) for k in range(2, groups, 2)]

    summed = (own.astype(F32) + swap(others).astype(F32)).astype(BF16)
    summed = to_all(summed.reshape(shards, half_rows, LANES))
    query_grad, value_grad = unpack_heads(summed.reshape(heads, rows, LANES))

    weights = [w.astype(F32) for w in weights]
    while len(weights) > 1:
        weights = [weights[i] + weights[i + 1] for i in range(0, len(weights), 2)]
    weight = weights[0].astype(BF16)
    rest = swap(weight)
    weight = jnp.where(
        core == 0,
        jnp.concatenate([weight, rest], axis=0),
        jnp.concatenate([rest, weight], axis=0),
    )
    w_out_grad = weight.astype(F32) * total ** (-0.5)

    output = shares[0].astype(F32)
    for share in early + late:
        output = output + share.astype(F32)
    return (output.astype(BF16), query_grad, value_grad, w_out_grad)


def shifted(value, axis, steps):
    count = lax.axis_size(axis)
    pairs = [(source, (source + steps) % count) for source in range(count)]
    return lax.ppermute(value, axis, pairs)


def with_before(blocks, before):
    earlier = jnp.concatenate([before[:, None], blocks[:, :-1]], axis=1)
    return jnp.concatenate([blocks, earlier], axis=2)


def normalized(query_rows):
    query_float = query_rows.astype(jnp.float32)
    inverse = lax.rsqrt(jnp.mean(query_float * query_float, axis=-1, keepdims=True) + 1e-06)
    return ((query_float * inverse).astype(jnp.bfloat16), query_float, inverse)


def move_wide(matrix, data, form):
    return jnp.einsum(form, matrix, data, preferred_element_type=jnp.float32).astype(jnp.bfloat16)


def move_exact(matrix, data, form):
    return jnp.einsum(form, matrix, data.astype(jnp.float32), precision=lax.Precision.HIGHEST)


def by_span(queries, values, w_out, out_grad, slots):
    row_count = queries.shape[0]
    head_width = DH
    rounds = slots.shape[0]
    head_group = queries.shape[1] // head_width
    batch_size = rounds * head_group
    shards = lax.axis_size("seq")
    my_index = lax.axis_index("seq")
    even_share = row_count // shards
    capacity = even_share * 3 // 2
    slot_total = shards * capacity
    block_count = row_count // SPAN
    score_scale = head_width ** (-0.5)

    def per_head(matrix):
        split_heads = matrix.reshape(row_count, head_group, head_width).transpose(1, 0, 2)
        return jnp.concatenate([split_heads] * rounds, axis=0)

    flat_slot = slots.reshape(batch_size, row_count)
    target = flat_slot // row_count
    local_slot = flat_slot - target * row_count
    onehot_target = (
        target[:, :, None] == jnp.arange(shards, dtype=jnp.int32)[None, None, :]
    ).astype(jnp.int32)
    earlier_count = jnp.sum(jnp.cumsum(onehot_target, axis=1) * onehot_target, axis=2) - 1
    send_spot = target * capacity + earlier_count
    positions = my_index * row_count + jnp.arange(row_count, dtype=jnp.int32)
    position_rows = jnp.broadcast_to(positions[None, :], (batch_size, row_count))
    pack_float = (
        send_spot[:, None, :] == jnp.arange(slot_total, dtype=jnp.int32)[None, :, None]
    ).astype(jnp.float32)
    pack_half = pack_float.astype(jnp.bfloat16)
    full_grad = lax.all_gather(out_grad, "head", axis=1, tiled=True)
    back_attn = lax.dot_general(
        full_grad, w_out, (((1,), (1,)), ((), ())), preferred_element_type=jnp.float32
    ).astype(jnp.bfloat16)
    query_value = jnp.concatenate([per_head(queries), per_head(values)], axis=2)
    packed_rows = move_wide(pack_half, query_value, "bsr,brd->bsd").reshape(
        batch_size, shards, capacity, 2 * head_width
    )
    packed_place = (
        move_exact(pack_float, position_rows, "bsr,br->bs")
        .astype(jnp.int32)
        .reshape(batch_size, shards, capacity)
    )
    packed_slot = (
        move_exact(pack_float, local_slot + 1, "bsr,br->bs")
        .astype(jnp.int32)
        .reshape(batch_size, shards, capacity)
    )
    got_rows, got_place, got_slot = (
        lax.all_to_all(packed_rows, "seq", split_axis=1, concat_axis=1, tiled=True),
        lax.all_to_all(packed_place, "seq", split_axis=1, concat_axis=1, tiled=True),
        lax.all_to_all(packed_slot, "seq", split_axis=1, concat_axis=1, tiled=True),
    )
    got_spot = got_slot.reshape(batch_size, slot_total)
    got_spot = jnp.where(got_spot == 0, row_count, got_spot - 1)
    sort_float = (
        got_spot[:, :, None] == jnp.arange(row_count, dtype=jnp.int32)[None, None, :]
    ).astype(jnp.float32)
    sort_half = sort_float.astype(jnp.bfloat16)
    sorted_rows = move_wide(
        sort_half, got_rows.reshape(batch_size, slot_total, 2 * head_width), "bsr,bsd->brd"
    )
    sorted_place = move_exact(
        sort_float, got_place.reshape(batch_size, slot_total), "bsr,bs->br"
    ).astype(jnp.int32)
    last_rows = sorted_rows[:, row_count - SPAN :]
    last_place = sorted_place[:, row_count - SPAN :]
    before_rows, before_place = shifted((last_rows, last_place), "seq", 1)
    sorted_query = sorted_rows[:, :, :head_width]
    sorted_value = sorted_rows[:, :, head_width:]
    sorted_key, query_float, inverse = normalized(sorted_query)
    before_key = normalized(before_rows[:, :, :head_width])[0]
    query_blocks = sorted_query.reshape(batch_size, block_count, SPAN, head_width)
    key_window = with_before(
        sorted_key.reshape(batch_size, block_count, SPAN, head_width), before_key
    )
    value_window = with_before(
        sorted_value.reshape(batch_size, block_count, SPAN, head_width),
        before_rows[:, :, head_width:],
    )
    place_blocks = sorted_place.reshape(batch_size, block_count, SPAN)
    place_window = with_before(place_blocks, before_place)
    own_token = (jnp.arange(SPAN)[:, None] == jnp.arange(2 * SPAN)[None, :]).astype(jnp.float32)
    future = (place_window[:, :, None, :] > place_blocks[:, :, :, None]).astype(jnp.float32)

    def score_of():
        raw_scores = (
            jnp.einsum(
                "bcqd,bckd->bcqk", query_blocks, key_window, preferred_element_type=jnp.float32
            )
            * score_scale
        )
        return raw_scores - 100000.0 * own_token - 1000000000.0 * future

    scores = score_of()
    row_top = jnp.max(scores, axis=-1)
    log_total = row_top + jnp.log(jnp.sum(jnp.exp(scores - row_top[..., None]), axis=-1))
    weights = jnp.exp(scores - log_total[..., None])
    rounded_probs = weights.astype(jnp.bfloat16)
    block_out = jnp.einsum(
        "bcqk,bckd->bcqd", rounded_probs, value_window, preferred_element_type=jnp.float32
    ).astype(jnp.bfloat16)
    out_rows = block_out.reshape(batch_size, row_count, head_width)
    home_out = move_wide(sort_half, out_rows, "bsr,brd->bsd").reshape(
        batch_size, shards, capacity // 2, 2 * head_width
    )
    home_log = move_exact(
        sort_float, log_total.reshape(batch_size, row_count), "bsr,br->bs"
    ).reshape(batch_size, shards, capacity)
    back_out, back_log = (
        lax.all_to_all(home_out, "seq", split_axis=1, concat_axis=1, tiled=True),
        lax.all_to_all(
            home_log.astype(jnp.bfloat16), "seq", split_axis=1, concat_axis=1, tiled=True
        ).astype(home_log.dtype),
    )
    round_out = move_wide(
        pack_half, back_out.reshape(batch_size, slot_total, head_width), "bsr,bsd->brd"
    ).reshape(rounds, head_group, row_count, head_width)
    round_log = move_exact(
        pack_float, back_log.reshape(batch_size, slot_total), "bsr,bs->br"
    ).reshape(rounds, head_group, row_count)
    mixing = jax.nn.softmax(round_log, axis=0)
    combined = jnp.sum(mixing[..., None] * round_out.astype(jnp.float32), axis=0)
    attention = (
        combined.astype(jnp.bfloat16).transpose(1, 0, 2).reshape(row_count, head_group * head_width)
    )
    head_term = jnp.dot(attention, w_out, preferred_element_type=jnp.float32)
    output = lax.psum_scatter(
        head_term.astype(jnp.bfloat16), "head", scatter_dimension=1, tiled=True
    )
    weight_term = lax.dot_general(
        attention, full_grad, (((0,), (0,)), ((), ())), preferred_element_type=jnp.float32
    )
    w_out_grad = lax.psum(weight_term.astype(jnp.bfloat16), "seq").astype(jnp.float32) * (
        shards * row_count
    ) ** (-0.5)
    back_heads = (
        back_attn.reshape(row_count, head_group, head_width).transpose(1, 0, 2).astype(jnp.float32)
    )
    inner_rows = jnp.sum(back_heads * combined, axis=-1)
    delta_rows = (mixing * inner_rows[None]).reshape(batch_size, row_count)
    grad_rows = (
        (mixing[..., None] * back_heads[None])
        .astype(jnp.bfloat16)
        .reshape(batch_size, row_count, head_width)
    )
    packed_grad = move_wide(pack_half, grad_rows, "bsr,brd->bsd").reshape(
        batch_size, shards, capacity // 2, 2 * head_width
    )
    packed_delta = move_exact(pack_float, delta_rows, "bsr,br->bs").reshape(
        batch_size, shards, capacity
    )
    got_grad, got_delta = (
        lax.all_to_all(packed_grad, "seq", split_axis=1, concat_axis=1, tiled=True),
        lax.all_to_all(
            packed_delta.astype(jnp.bfloat16), "seq", split_axis=1, concat_axis=1, tiled=True
        ).astype(packed_delta.dtype),
    )
    sorted_grad = move_wide(
        sort_half, got_grad.reshape(batch_size, slot_total, head_width), "bsr,bsd->brd"
    )
    sorted_delta = move_exact(sort_float, got_delta.reshape(batch_size, slot_total), "bsr,bs->br")
    kept_weights = jnp.exp(score_of() - log_total[..., None])
    grad_blocks = sorted_grad.reshape(batch_size, block_count, SPAN, head_width)
    delta_blocks = sorted_delta.reshape(batch_size, block_count, SPAN)
    dot_grad = jnp.einsum(
        "bcqd,bckd->bcqk", grad_blocks, value_window, preferred_element_type=jnp.float32
    )
    score_grad = (kept_weights * (dot_grad - delta_blocks[..., None])).astype(jnp.bfloat16)
    query_part = (
        jnp.einsum("bcqk,bckd->bcqd", score_grad, key_window, preferred_element_type=jnp.float32)
        * score_scale
    )
    key_part = (
        jnp.einsum("bcqk,bcqd->bckd", score_grad, query_blocks, preferred_element_type=jnp.float32)
        * score_scale
    )
    value_part = jnp.einsum(
        "bcqk,bcqd->bckd", rounded_probs, grad_blocks, preferred_element_type=jnp.float32
    )
    spill_rows = jnp.concatenate([key_part[:, 0, SPAN:], value_part[:, 0, SPAN:]], axis=2)
    arrived = shifted(spill_rows.astype(jnp.bfloat16), "seq", -1).astype(spill_rows.dtype)
    key_grad = key_part[:, :, :SPAN] + jnp.concatenate(
        [key_part[:, 1:, SPAN:], arrived[:, None, :, :head_width]], axis=1
    )
    value_sum = value_part[:, :, :SPAN] + jnp.concatenate(
        [value_part[:, 1:, SPAN:], arrived[:, None, :, head_width:]], axis=1
    )
    key_grad = key_grad.reshape(batch_size, row_count, head_width)
    value_sum = value_sum.reshape(batch_size, row_count, head_width)
    query_total = (
        query_part.reshape(batch_size, row_count, head_width)
        + inverse * key_grad
        - query_float
        * (inverse * inverse * inverse)
        * jnp.mean(query_float * key_grad, axis=-1, keepdims=True)
    )
    both_grads = jnp.concatenate(
        [query_total.astype(jnp.bfloat16), value_sum.astype(jnp.bfloat16)], axis=2
    )
    home_grads = move_wide(sort_half, both_grads, "bsr,brd->bsd").reshape(
        batch_size, shards, capacity, 2 * head_width
    )
    back_grads = lax.all_to_all(home_grads, "seq", split_axis=1, concat_axis=1, tiled=True)
    own_grads = move_wide(
        pack_half, back_grads.reshape(batch_size, slot_total, 2 * head_width), "bsr,bsd->brd"
    ).astype(jnp.float32)
    own_grads = own_grads.reshape(rounds, head_group, row_count, 2 * head_width)
    summed = jnp.sum(own_grads, axis=0).astype(jnp.bfloat16)
    query_grad = (
        summed[:, :, :head_width].transpose(1, 0, 2).reshape(row_count, head_group * head_width)
    )
    value_grad = (
        summed[:, :, head_width:].transpose(1, 0, 2).reshape(row_count, head_group * head_width)
    )
    return (output, query_grad, value_grad, w_out_grad)


def per_device(queries, values, w_out, out_grad, slots):
    if lax.axis_size("seq") == slots.shape[0] * slots.shape[1] and slots.shape[0] == 2:
        return by_sequence(queries, values, w_out, out_grad, slots)
    return by_span(queries, values, w_out, out_grad, slots)


def solution(mesh):
    placed = (
        P("seq", "head"),
        P("seq", "head"),
        P("head", None),
        P("seq", "head"),
        P(None, "head", "seq"),
    )
    return jax.shard_map(
        per_device,
        mesh=mesh,
        in_specs=placed,
        out_specs=(P("seq", "head"), P("seq", "head"), P("seq", "head"), P("head", None)),
        check_vma=False,
    )
```

```python
import functools

import jax
import jax.numpy as jnp
from jax import lax
from jax.experimental import pallas as pl
from jax.experimental.pallas import tpu as pltpu
from jax.sharding import PartitionSpec as P

DH = 64
SPAN = 128
LANES = 128
GROUP = 8
SUB = 4
F32 = jnp.float32
BF16 = jnp.bfloat16
NT = (((1,), (1,)), ((), ()))
TN = (((0,), (0,)), ((), ()))
MIB = 1 << 20


def whole(space):
    return pl.BlockSpec(memory_space=space)


def in_hbm(value):
    return pltpu.with_memory_space_constraint(value, pltpu.HBM)


def fixed(shape):
    return pl.BlockSpec(shape, lambda g: (0,) * len(shape), pipeline_mode=pl.Buffered(1))


def lane_of(shape):
    return lax.broadcasted_iota(jnp.int32, shape, len(shape) - 1)


def places_kernel(mine_ref, addr_ref, key_place, query_place, sign_ref):
    sources, _, lanes = mine_ref.shape
    blocks = addr_ref.shape[0]
    rows = mine_ref.shape[1] - 16
    parts = (mine_ref.shape[1] - rows) // 2
    core = lax.rem(lax.axis_index("seq"), 2)
    block_row = lax.broadcasted_iota(jnp.int32, (blocks, lanes), 0).astype(F32)
    place_row = lax.broadcasted_iota(jnp.int32, (lanes, lanes), 0).astype(F32)
    token_low = lane_of((blocks, lanes)).astype(F32)
    total = jnp.zeros((2 * blocks, lanes), F32)
    for s in range(sources):
        slots = mine_ref[s, rows:, :].astype(F32)
        tall = []
        wide = []
        for j in range(parts):
            in_block = block_row == slots[j : j + 1, :]
            token_high = float(s * parts + j)
            tall.append(
                jnp.concatenate(
                    [jnp.where(in_block, token_high, 0.0), jnp.where(in_block, token_low, 0.0)],
                    axis=0,
                ).astype(BF16)
            )
            wide.append((place_row == slots[parts + j : parts + j + 1, :]).astype(BF16))
        total += lax.dot_general(
            jnp.concatenate(tall, axis=1),
            jnp.concatenate(wide, axis=1),
            NT,
            preferred_element_type=F32,
        )
    place = total[:blocks] * float(lanes) + total[blocks:]
    token = place.astype(jnp.int32)
    source = token // (2 * rows)
    within = token - source * (2 * rows)
    part = within // rows
    addr_ref[...] = ((part ^ core) * sources + source) * rows + (within - part * rows)
    before = pltpu.roll(place, 1, 0)
    least = jnp.minimum(
        jnp.min(place, axis=1, keepdims=True), jnp.min(before, axis=1, keepdims=True)
    )
    window = jnp.concatenate([before, place], axis=1)
    window = jnp.where(window == least, window - 0.5, window)
    for c in range(blocks):
        key_place[c] = window[c : c + 1, :]
    columns = jnp.transpose(place)
    alone = jnp.transpose(jnp.where(place == least, -1.0, 1.0))
    for g in range(blocks // GROUP):
        query_place[g] = columns[:, g * GROUP : (g + 1) * GROUP]
        sign_ref[g] = alone[:, g * GROUP : (g + 1) * GROUP]


def find_places(mine):
    sources, rows, lanes = mine.shape
    blocks = 2 * sources * (rows - 16) // lanes
    column = jax.ShapeDtypeStruct((blocks // GROUP, lanes, GROUP), F32)
    return pl.pallas_call(
        places_kernel,
        out_shape=[
            jax.ShapeDtypeStruct((blocks, lanes), jnp.int32),
            jax.ShapeDtypeStruct((blocks, 1, 2 * lanes), F32),
            column,
            column,
        ],
        compiler_params=pltpu.CompilerParams(vmem_limit_bytes=10 * MIB),
        name="find_places",
    )(mine)


def gather_rows(addr_ref, block, source, target):
    for j in range(SPAN):
        target[pl.ds(j, 1), :] = source[pl.ds(addr_ref[block, j], 1), :]


def scatter_rows(addr_ref, block, source, target):
    for j in range(SPAN):
        target[pl.ds(addr_ref[block, j], 1), :] = source[pl.ds(j, 1), :]


def split_sum(product, chosen):
    high = product.astype(BF16)
    rest = (product - high.astype(F32)).astype(BF16)
    return jnp.dot(
        jnp.concatenate([high, rest], axis=1),
        jnp.concatenate([chosen, chosen], axis=0),
        preferred_element_type=F32,
    )


def low_lanes(scale=1.0):
    row = lax.broadcasted_iota(jnp.int32, (LANES, LANES), 0)
    return jnp.where(row < DH, scale, 0.0).astype(BF16)


def inverse_of(rows):
    return lax.rsqrt(split_sum(rows * rows, low_lanes(1.0 / DH)) + 1e-06)


def forward_kernel(
    addr_ref, mine_ref, other_ref, key_place, query_place, sign_ref,
    home_ref, away_ref, prob_ref, qv_ref, key_ref,
    tokens, result, in_even, in_odd, out_even, out_odd, grown_ref, qv_win, key_win,
):
    step = pl.program_id(0)
    last = pl.num_programs(0) - 1
    sources = mine_ref.shape[0]
    rows = mine_ref.shape[1] - 16
    half = sources * rows
    blocks = 2 * half // SPAN
    score_scale = DH ** (-0.5) * 1.4426950408889634
    rows_in = (in_even, in_odd)
    rows_out = (out_even, out_odd)

    def place_rows(values, at):
        low = lane_of(values.shape) < DH
        qv_win[at] = values.astype(BF16)
        key_win[at] = jnp.where(low, values * inverse_of(values), 0.0).astype(BF16)

    @pl.when(step == 0)
    def _():
        for s in range(sources):
            tokens[s * rows : (s + 1) * rows, :] = mine_ref[s, :rows, :].astype(F32)
            tokens[half + s * rows : half + (s + 1) * rows, :] = other_ref[s, :rows, :].astype(F32)
        gather_rows(addr_ref, blocks - 1, tokens, in_odd.at[0])
        place_rows(in_odd[0], slice(0, SPAN))
        for b in range(SUB):
            gather_rows(addr_ref, b, tokens, in_even.at[b])

    ones = jnp.ones((2 * SPAN, LANES), BF16)
    low = lane_of((SPAN, LANES)) < DH
    for p in range(GROUP // SUB):
        here = step * GROUP + p * SUB
        coming = jnp.minimum(here + SUB, blocks - SUB)
        gone = jnp.maximum(here - SUB, 0)
        now, then = p % 2, 1 - p % 2
        spans = slice((p * SUB + 1) * SPAN, ((p + 1) * SUB + 1) * SPAN)
        place_rows(rows_in[now][...].reshape(SUB * SPAN, LANES), spans)
        for i in range(SUB):
            b = p * SUB + i
            own = slice((b + 1) * SPAN, (b + 2) * SPAN)
            window = slice(b * SPAN, (b + 2) * SPAN)
            raw = lax.dot_general(qv_win[own], key_win[window], NT, preferred_element_type=F32)
            seen = key_place[b] < query_place[0, :, b : b + 1]
            grown_ref[i] = jnp.where(seen, jnp.exp2(raw * score_scale), 0.0)
            gather_rows(addr_ref, coming + i, tokens, rows_in[then].at[i])
        for i in range(SUB):
            b = p * SUB + i
            window = slice(b * SPAN, (b + 2) * SPAN)
            grown = grown_ref[i]
            mixed = jnp.dot(
                grown.astype(BF16),
                jnp.concatenate([qv_win[window], ones], axis=1),
                preferred_element_type=F32,
            )
            sums = mixed[:, LANES:]
            recip = 1.0 / sums
            prob_ref[b] = (grown * jnp.concatenate([recip, recip], axis=1)).astype(BF16)
            signed = sums * sign_ref[0, :, b : b + 1]
            rows_out[now][i] = jnp.where(low, signed, mixed[:, :LANES] * recip)
            scatter_rows(addr_ref, gone + i, rows_out[then].at[i], result)

    qv_ref[...] = qv_win[SPAN:]
    key_ref[...] = key_win[SPAN:]
    qv_win[:SPAN] = qv_win[GROUP * SPAN :]
    key_win[:SPAN] = key_win[GROUP * SPAN :]

    @pl.when(step == last)
    def _():
        for i in range(SUB):
            scatter_rows(addr_ref, blocks - SUB + i, out_odd.at[i], result)
        home_ref[...] = result[:half, :].astype(BF16)
        away_ref[...] = result[half:, :].astype(BF16)


def forward(addr, mine, other, key_place, query_place, sign):
    half = mine.shape[0] * (mine.shape[1] - 16)
    total = 2 * half
    blocks = total // SPAN
    rows = GROUP * SPAN
    return pl.pallas_call(
        forward_kernel,
        grid=(blocks // GROUP,),
        out_shape=[
            jax.ShapeDtypeStruct((half, LANES), BF16),
            jax.ShapeDtypeStruct((half, LANES), BF16),
            pltpu.HBM((blocks, SPAN, 2 * SPAN), BF16),
            pltpu.HBM((total, LANES), BF16),
            pltpu.HBM((total, LANES), BF16),
        ],
        in_specs=[
            whole(pltpu.SMEM),
            fixed(mine.shape),
            fixed(mine.shape),
            pl.BlockSpec((GROUP, 1, 2 * SPAN), lambda g: (g, 0, 0)),
            pl.BlockSpec((1, SPAN, GROUP), lambda g: (g, 0, 0)),
            pl.BlockSpec((1, SPAN, GROUP), lambda g: (g, 0, 0)),
        ],
        out_specs=[
            fixed((half, LANES)),
            fixed((half, LANES)),
            pl.BlockSpec((GROUP, SPAN, 2 * SPAN), lambda g: (g, 0, 0)),
            pl.BlockSpec((rows, LANES), lambda g: (g, 0)),
            pl.BlockSpec((rows, LANES), lambda g: (g, 0)),
        ],
        scratch_shapes=[
            pltpu.VMEM((total, LANES), F32),
            pltpu.VMEM((total, LANES), F32),
            *[pltpu.VMEM((SUB, SPAN, LANES), F32)] * 4,
            pltpu.VMEM((SUB, SPAN, 2 * SPAN), F32),
            pltpu.VMEM((rows + SPAN, LANES), BF16),
            pltpu.VMEM((rows + SPAN, LANES), BF16),
        ],
        compiler_params=pltpu.CompilerParams(vmem_limit_bytes=22 * MIB),
        cost_estimate=pl.CostEstimate(flops=0, bytes_accessed=64 * MIB, transcendentals=0),
        name="span_forward",
    )(addr, mine, other, key_place, query_place, sign)


def share_of(own, peer):
    row = lax.broadcasted_iota(jnp.int32, (LANES, LANES), 0)
    pick = (row < 1).astype(BF16)
    own_sum = jnp.dot(own, pick, preferred_element_type=F32)
    peer_sum = jnp.dot(peer, pick, preferred_element_type=F32)
    both = own_sum / (own_sum + peer_sum)
    own_alone = own_sum < 0.0
    peer_alone = peer_sum < 0.0
    return jnp.where(
        own_alone, jnp.where(peer_alone, both, 0.0), jnp.where(peer_alone, 1.0, both)
    )


def combined_rows(own, peer, share):
    high = lane_of(own.shape) >= DH
    own = own.astype(F32)
    peer = peer.astype(F32)
    return jnp.where(high, share * own + (1.0 - share) * peer, 0.0)


def mix_attention_kernel(own_ref, peer_ref, grad_ref, out_ref):
    pieces, half, _ = grad_ref.shape
    rows = 2 * half
    for i in range(pieces):
        own = own_ref[i * rows : (i + 1) * rows]
        peer = peer_ref[i * rows : (i + 1) * rows]
        combined = combined_rows(own, peer, share_of(own, peer))
        out_ref[i, :half] = (pltpu.roll(combined[:half], DH, 1) + combined[half:]).astype(BF16)
        out_ref[i, half:] = grad_ref[i]


def mix_grad_kernel(own_ref, peer_ref, both_ref, grad_own, grad_peer):
    pieces, rows, _ = both_ref.shape
    for i in range(pieces):
        at = slice(i * rows, (i + 1) * rows)
        own = own_ref[at]
        peer = peer_ref[at]
        share = share_of(own, peer)
        combined = combined_rows(own, peer, share)
        packed = both_ref[i, rows // 2 :].astype(F32)
        grad = jnp.concatenate([pltpu.roll(packed, DH, 1), packed], axis=0)
        column = lane_of((LANES, LANES))
        inner = split_sum(grad * combined, (column < DH).astype(BF16))
        both = jnp.where(lane_of(grad.shape) < DH, -inner, grad)
        grad_own[at] = (share * both).astype(BF16)
        grad_peer[at] = ((1.0 - share) * both).astype(BF16)


def mix_attention(home, peer, grad):
    pieces, rows, _ = grad.shape
    return pl.pallas_call(
        mix_attention_kernel,
        out_shape=jax.ShapeDtypeStruct((pieces, 2 * rows, LANES), BF16),
        in_specs=[whole(pltpu.VMEM)] * 3,
        out_specs=whole(pltpu.VMEM),
        compiler_params=pltpu.CompilerParams(vmem_limit_bytes=12 * MIB),
        name="mix_attention",
    )(home, peer, grad)


def mix_grad(home, peer, both):
    return pl.pallas_call(
        mix_grad_kernel,
        out_shape=[jax.ShapeDtypeStruct(home.shape, BF16)] * 2,
        in_specs=[whole(pltpu.VMEM)] * 3,
        out_specs=[whole(pltpu.VMEM)] * 2,
        compiler_params=pltpu.CompilerParams(vmem_limit_bytes=12 * MIB),
        name="mix_grad",
    )(home, peer, both)


def pack_kernel(query_ref, value_ref, slot_ref, out_ref):
    rounds, heads, rows = slot_ref.shape
    half = rows // 2
    for h in range(heads):
        columns = slice(h * DH, (h + 1) * DH)
        pair = jnp.concatenate([query_ref[:, columns], value_ref[:, columns]], axis=1)
        for r in range(rounds):
            out_ref[2 * h + r, :half] = pair[r * half : (r + 1) * half]
            slots = slot_ref[r, h : h + 1, :]
            high = slots // LANES
            parts = [high, slots - high * LANES]
            lines = [p[:, j : j + LANES] for p in parts for j in range(0, rows, LANES)]
            out_ref[2 * h + r, half:] = jnp.concatenate(lines, axis=0).astype(F32).astype(BF16)


def pack_heads(queries, values, slots):
    rounds, heads, rows = slots.shape
    return pl.pallas_call(
        pack_kernel,
        out_shape=jax.ShapeDtypeStruct((rounds * heads, rows // 2 + 16, 2 * DH), BF16),
        compiler_params=pltpu.CompilerParams(vmem_limit_bytes=10 * MIB),
        name="pack_heads",
    )(in_hbm(queries), in_hbm(values), slots)


def unpack_kernel(in_ref, query_ref, value_ref):
    for h in range(in_ref.shape[0]):
        columns = slice(h * DH, (h + 1) * DH)
        query_ref[:, columns] = in_ref[h, :, :DH]
        value_ref[:, columns] = in_ref[h, :, DH:]


def unpack_heads(rows):
    heads, count, _ = rows.shape
    return pl.pallas_call(
        unpack_kernel,
        out_shape=[jax.ShapeDtypeStruct((count, heads * DH), BF16)] * 2,
        in_specs=[whole(pltpu.VMEM)],
        compiler_params=pltpu.CompilerParams(vmem_limit_bytes=10 * MIB),
        name="unpack_heads",
    )(rows)


def member(step, groups):
    return lax.rem(lax.axis_index("head") + (groups - step), groups)


def columns_of(index, width):
    return pl.ds(pl.multiple_of(index * width, width), width)


def back_kernel(weight_ref, *refs):
    *grads, out_ref = refs
    groups = len(grads)
    rows, width = grads[0].shape
    total = 0.0
    for k in range(groups):
        weight = weight_ref[:, columns_of(member(k, groups), width)]
        total += lax.dot_general(grads[k][...], weight, NT, preferred_element_type=F32)
    total = total.astype(BF16)
    quarter = rows // 4
    for h in range(width // DH):
        columns = slice(h * DH, (h + 1) * DH)
        for c in range(2):
            first = total[2 * c * quarter : (2 * c + 1) * quarter, columns]
            second = total[(2 * c + 1) * quarter : (2 * c + 2) * quarter, columns]
            out_ref[2 * h + c] = jnp.concatenate([first, second], axis=1)


def back_projection(weight, grads):
    rows, width = grads[0].shape
    return pl.pallas_call(
        back_kernel,
        out_shape=jax.ShapeDtypeStruct((2 * width // DH, rows // 4, 2 * DH), BF16),
        compiler_params=pltpu.CompilerParams(vmem_limit_bytes=10 * MIB),
        name="back_projection",
    )(weight, *grads)


def project_kernel(weight_ref, packed_ref, att_ref, *outs):
    groups = len(outs)
    rows, width = att_ref.shape
    quarter = rows // 4
    for h in range(width // DH):
        columns = slice(h * DH, (h + 1) * DH)
        for c in range(2):
            packed = packed_ref[2 * h + c, :quarter]
            att_ref[2 * c * quarter : (2 * c + 1) * quarter, columns] = packed[:, :DH]
            att_ref[(2 * c + 1) * quarter : (2 * c + 2) * quarter, columns] = packed[:, DH:]
    for k in range(groups):
        weight = weight_ref[:, columns_of(member(groups - k, groups), width)]
        outs[k][...] = jnp.dot(att_ref[...], weight, preferred_element_type=F32).astype(BF16)


def project(weight, packed):
    count, double, _ = packed.shape
    rows, width = 2 * double, count * DH // 2
    groups = weight.shape[1] // width
    return pl.pallas_call(
        project_kernel,
        out_shape=[jax.ShapeDtypeStruct((rows, width), BF16)] * (1 + groups),
        compiler_params=pltpu.CompilerParams(vmem_limit_bytes=10 * MIB),
        name="project",
    )(weight, packed)


def add_kernel(*refs):
    *shares, out_ref = refs
    total = shares[0][...].astype(F32)
    for share in shares[1:]:
        total += share[...].astype(F32)
    out_ref[...] = total.astype(BF16)


def add_shares(shares):
    return pl.pallas_call(
        add_kernel,
        out_shape=jax.ShapeDtypeStruct(shares[0].shape, BF16),
        in_specs=[whole(pltpu.VMEM)] * len(shares),
        compiler_params=pltpu.CompilerParams(vmem_limit_bytes=8 * MIB),
        name="add_shares",
    )(*shares)


def weight_grad_kernel(att_ref, *refs):
    *grads, keep_ref, give_ref = refs
    groups = len(grads)
    width = grads[0].shape[1]
    part = keep_ref.shape[0]
    core = lax.rem(lax.axis_index("seq"), 2)
    for index, out_ref in ((core, keep_ref), (1 - core, give_ref)):
        att = att_ref[:, columns_of(index, part)]
        for k in range(groups):
            out_ref[:, columns_of(member(k, groups), width)] = lax.dot_general(
                att, grads[k][...], TN, preferred_element_type=F32
            ).astype(BF16)


def weight_grad(att, grads):
    width = att.shape[1]
    groups = len(grads)
    return pl.pallas_call(
        weight_grad_kernel,
        out_shape=[jax.ShapeDtypeStruct((width // 2, width * groups), BF16)] * 2,
        compiler_params=pltpu.CompilerParams(vmem_limit_bytes=10 * MIB),
        name="weight_grad",
    )(att, *grads)


def finished_rows(rows, query_part, key_value):
    low = lane_of(rows.shape) < DH
    scale = DH ** (-0.5)
    query = jnp.where(low, rows.astype(F32), 0.0)
    inverse = inverse_of(query)
    key = query * inverse
    term = key_value * (inverse * scale)
    along = split_sum(key * term, low_lanes(1.0 / DH))
    return jnp.where(low, query_part * scale + term - key * along, key_value)


def backward_kernel(
    addr_ref, mine_ref, other_ref, prob_ref, qv_ref, qv_before, key_ref, key_before,
    home_ref, away_ref,
    tokens, result, in_even, in_odd, out_even, out_odd, qv_win, key_win, tall, sums, query_sums,
    first_sums,
):
    step = pl.program_id(0)
    last = pl.num_programs(0) - 1
    half = mine_ref.shape[0]
    blocks = 2 * half // SPAN
    rows_in = (in_even, in_odd)
    rows_out = (out_even, out_odd)

    @pl.when(step == 0)
    def _():
        tokens[:half, :] = mine_ref[...].astype(F32)
        tokens[half:, :] = other_ref[...].astype(F32)
        for b in range(SUB):
            gather_rows(addr_ref, b, tokens, in_even.at[b])

    qv_win[:SPAN] = qv_before[...]
    qv_win[SPAN:] = qv_ref[...]
    key_win[:SPAN] = key_before[...]
    key_win[SPAN:] = key_ref[...]
    low = lane_of((SPAN, LANES)) < DH
    zero = jnp.zeros((SPAN, LANES), BF16)
    for p in range(GROUP // SUB):
        here = step * GROUP + p * SUB
        coming = jnp.minimum(here + SUB, blocks - SUB)
        gone = here + (blocks - SUB - 1)
        now, then = p % 2, 1 - p % 2
        spans = slice(p * SUB * SPAN, ((p + 1) * SUB + 1) * SPAN)
        everything = qv_win[spans]
        lane = lane_of(everything.shape)
        one = jnp.where(lane == 0, 1.0, 0.0).astype(BF16)
        value_one = jnp.where(lane >= DH, everything, one)
        for i in range(SUB):
            b = p * SUB + i
            prob = prob_ref[b]
            dot_grad = lax.dot_general(
                rows_in[now][i].astype(BF16),
                value_one[i * SPAN : (i + 2) * SPAN],
                NT,
                preferred_element_type=F32,
            )
            tall[i, :SPAN] = (prob.astype(F32) * dot_grad).astype(BF16)
            tall[i, SPAN:] = prob
            gather_rows(addr_ref, coming + i, tokens, rows_in[then].at[i])
        for i in range(SUB):
            b = p * SUB + i
            own = slice((b + 1) * SPAN, (b + 2) * SPAN)
            window = slice(b * SPAN, (b + 2) * SPAN)
            query_sums[own] = jnp.dot(
                tall[i, :SPAN], key_win[window], preferred_element_type=F32
            )
            grad_high = jnp.where(low, 0.0, rows_in[now][i]).astype(BF16)
            key_value = lax.dot_general(
                tall[i],
                jnp.concatenate([jnp.where(low, qv_win[own], zero), grad_high], axis=0),
                TN,
                preferred_element_type=F32,
            )
            if b == 0:

                @pl.when(step == 0)
                def _():
                    first_sums[...] = key_value[:SPAN]

            sums[b * SPAN : (b + 1) * SPAN] += key_value[:SPAN]
            sums[own] = key_value[SPAN:]
            scatter_rows(addr_ref, lax.rem(gone + i, blocks), rows_out[then].at[i], result)
        spans = slice(p * SUB * SPAN, (p + 1) * SUB * SPAN)
        finished = finished_rows(qv_win[spans], query_sums[spans], sums[spans])
        rows_out[now][...] = finished.reshape(SUB, SPAN, LANES)
    sums[:SPAN] = sums[GROUP * SPAN :]
    query_sums[:SPAN] = query_sums[GROUP * SPAN :]

    @pl.when(step == last)
    def _():
        for i in range(SUB):
            scatter_rows(addr_ref, blocks - SUB - 1 + i, out_odd.at[i], result)
        out_even[0] = finished_rows(
            qv_win[GROUP * SPAN :], query_sums[:SPAN], sums[:SPAN] + first_sums[...]
        )
        scatter_rows(addr_ref, blocks - 1, out_even.at[0], result)
        home_ref[...] = result[:half, :].astype(BF16)
        away_ref[...] = result[half:, :].astype(BF16)


def backward(addr, mine, other, prob, query_key, value_one):
    half = mine.shape[0]
    total = 2 * half
    blocks = total // SPAN
    rows = GROUP * SPAN
    by_rows = pl.BlockSpec((rows, LANES), lambda g: (g, 0))
    before = pl.BlockSpec((SPAN, LANES), lambda g: (lax.rem(g * GROUP + blocks - 1, blocks), 0))
    return pl.pallas_call(
        backward_kernel,
        grid=(blocks // GROUP,),
        out_shape=[jax.ShapeDtypeStruct((half, LANES), BF16)] * 2,
        in_specs=[
            whole(pltpu.SMEM),
            fixed((half, LANES)),
            fixed((half, LANES)),
            pl.BlockSpec((GROUP, SPAN, 2 * SPAN), lambda g: (g, 0, 0)),
            by_rows,
            before,
            by_rows,
            before,
        ],
        out_specs=[fixed((half, LANES))] * 2,
        scratch_shapes=[
            pltpu.VMEM((total, LANES), F32),
            pltpu.VMEM((total, LANES), F32),
            *[pltpu.VMEM((SUB, SPAN, LANES), F32)] * 4,
            pltpu.VMEM((rows + SPAN, LANES), BF16),
            pltpu.VMEM((rows + SPAN, LANES), BF16),
            pltpu.VMEM((SUB, 2 * SPAN, 2 * SPAN), BF16),
            pltpu.VMEM((rows + SPAN, LANES), F32),
            pltpu.VMEM((rows + SPAN, LANES), F32),
            pltpu.VMEM((SPAN, LANES), F32),
        ],
        compiler_params=pltpu.CompilerParams(vmem_limit_bytes=22 * MIB),
        cost_estimate=pl.CostEstimate(flops=0, bytes_accessed=64 * MIB, transcendentals=0),
        name="span_backward",
    )(addr, mine, other, *[in_hbm(x) for x in (prob, query_key, query_key, value_one, value_one)])


def swap(value, distance=1):
    count = lax.axis_size("seq")
    return lax.ppermute(value, "seq", [(i, i ^ distance) for i in range(count)])


def to_all(value):
    return lax.all_to_all(value, "seq", split_axis=0, concat_axis=0, tiled=True)


def rotate(value, step):
    count = lax.axis_size("head")
    return lax.ppermute(value, "head", [(i, (i + step) % count) for i in range(count)])


def after(values, *earlier):
    return lax.optimization_barrier((values, earlier))[0]


def by_sequence(queries, values, w_out, out_grad, slots):
    rows = queries.shape[0]
    _, heads, _ = slots.shape
    shards = lax.axis_size("seq")
    groups = lax.axis_size("head")
    core = lax.rem(lax.axis_index("seq"), 2)
    total = shards * rows
    half_rows = rows // 2

    packed = pack_heads(queries, values, slots)
    mine = to_all(packed)
    places = find_places(mine)

    first = rotate(out_grad, 1)
    grads = [out_grad, first, rotate(first, 1), rotate(out_grad, groups - 1)]
    mine = after(mine, first)

    home, away, prob, query_key, value_one = forward(places[0], mine, swap(mine), *places[1:])
    away, *grads = after([away, *grads])
    peer = swap(away)

    grad_packed = back_projection(w_out, grads)
    both = to_all(mix_attention(home, peer, grad_packed))
    grad_own, grad_peer = mix_grad(home, peer, both)
    grad_other = swap(grad_peer)

    att, *shares = project(w_out, both)
    early = [rotate(shares[k], k) for k in range(1, groups, 2)]
    weight, give = weight_grad(att, grads)
    weight = (weight.astype(F32) + swap(give).astype(F32)).astype(BF16)
    weights = [weight] + [swap(weight, distance) for distance in range(2, shards, 2)]

    own, others = backward(places[0], grad_own, grad_other, prob, query_key, value_one)
    others, *weights = after([others, *weights])
    others, *early = after([others, *early])
    late = [rotate(after(shares[k], own), k) for k in range(2, groups, 2)]

    summed = (own.astype(F32) + swap(others).astype(F32)).astype(BF16)
    summed = to_all(summed.reshape(shards, half_rows, LANES))
    query_grad, value_grad = unpack_heads(summed.reshape(heads, rows, LANES))

    weights = [w.astype(F32) for w in weights]
    while len(weights) > 1:
        weights = [weights[i] + weights[i + 1] for i in range(0, len(weights), 2)]
    weight = weights[0].astype(BF16)
    rest = swap(weight)
    weight = jnp.where(
        core == 0,
        jnp.concatenate([weight, rest], axis=0),
        jnp.concatenate([rest, weight], axis=0),
    )
    w_out_grad = weight.astype(F32) * total ** (-0.5)

    output = shares[0].astype(F32)
    for share in early + late:
        output = output + share.astype(F32)
    return (output.astype(BF16), query_grad, value_grad, w_out_grad)


def shifted(value, axis, steps):
    count = lax.axis_size(axis)
    pairs = [(source, (source + steps) % count) for source in range(count)]
    return lax.ppermute(value, axis, pairs)


def with_before(blocks, before):
    earlier = jnp.concatenate([before[:, None], blocks[:, :-1]], axis=1)
    return jnp.concatenate([blocks, earlier], axis=2)


def normalized(query_rows):
    query_float = query_rows.astype(jnp.float32)
    inverse = lax.rsqrt(jnp.mean(query_float * query_float, axis=-1, keepdims=True) + 1e-06)
    return ((query_float * inverse).astype(jnp.bfloat16), query_float, inverse)


def move_wide(matrix, data, form):
    return jnp.einsum(form, matrix, data, preferred_element_type=jnp.float32).astype(jnp.bfloat16)


def move_exact(matrix, data, form):
    return jnp.einsum(form, matrix, data.astype(jnp.float32), precision=lax.Precision.HIGHEST)


def by_span(queries, values, w_out, out_grad, slots):
    row_count = queries.shape[0]
    head_width = DH
    rounds = slots.shape[0]
    head_group = queries.shape[1] // head_width
    batch_size = rounds * head_group
    shards = lax.axis_size("seq")
    my_index = lax.axis_index("seq")
    even_share = row_count // shards
    capacity = even_share * 3 // 2
    slot_total = shards * capacity
    block_count = row_count // SPAN
    score_scale = head_width ** (-0.5)

    def per_head(matrix):
        split_heads = matrix.reshape(row_count, head_group, head_width).transpose(1, 0, 2)
        return jnp.concatenate([split_heads] * rounds, axis=0)

    flat_slot = slots.reshape(batch_size, row_count)
    target = flat_slot // row_count
    local_slot = flat_slot - target * row_count
    onehot_target = (
        target[:, :, None] == jnp.arange(shards, dtype=jnp.int32)[None, None, :]
    ).astype(jnp.int32)
    earlier_count = jnp.sum(jnp.cumsum(onehot_target, axis=1) * onehot_target, axis=2) - 1
    send_spot = target * capacity + earlier_count
    positions = my_index * row_count + jnp.arange(row_count, dtype=jnp.int32)
    position_rows = jnp.broadcast_to(positions[None, :], (batch_size, row_count))
    pack_float = (
        send_spot[:, None, :] == jnp.arange(slot_total, dtype=jnp.int32)[None, :, None]
    ).astype(jnp.float32)
    pack_half = pack_float.astype(jnp.bfloat16)
    full_grad = lax.all_gather(out_grad, "head", axis=1, tiled=True)
    back_attn = lax.dot_general(
        full_grad, w_out, (((1,), (1,)), ((), ())), preferred_element_type=jnp.float32
    ).astype(jnp.bfloat16)
    query_value = jnp.concatenate([per_head(queries), per_head(values)], axis=2)
    packed_rows = move_wide(pack_half, query_value, "bsr,brd->bsd").reshape(
        batch_size, shards, capacity, 2 * head_width
    )
    packed_place = (
        move_exact(pack_float, position_rows, "bsr,br->bs")
        .astype(jnp.int32)
        .reshape(batch_size, shards, capacity)
    )
    packed_slot = (
        move_exact(pack_float, local_slot + 1, "bsr,br->bs")
        .astype(jnp.int32)
        .reshape(batch_size, shards, capacity)
    )
    got_rows, got_place, got_slot = (
        lax.all_to_all(packed_rows, "seq", split_axis=1, concat_axis=1, tiled=True),
        lax.all_to_all(packed_place, "seq", split_axis=1, concat_axis=1, tiled=True),
        lax.all_to_all(packed_slot, "seq", split_axis=1, concat_axis=1, tiled=True),
    )
    got_spot = got_slot.reshape(batch_size, slot_total)
    got_spot = jnp.where(got_spot == 0, row_count, got_spot - 1)
    sort_float = (
        got_spot[:, :, None] == jnp.arange(row_count, dtype=jnp.int32)[None, None, :]
    ).astype(jnp.float32)
    sort_half = sort_float.astype(jnp.bfloat16)
    sorted_rows = move_wide(
        sort_half, got_rows.reshape(batch_size, slot_total, 2 * head_width), "bsr,bsd->brd"
    )
    sorted_place = move_exact(
        sort_float, got_place.reshape(batch_size, slot_total), "bsr,bs->br"
    ).astype(jnp.int32)
    last_rows = sorted_rows[:, row_count - SPAN :]
    last_place = sorted_place[:, row_count - SPAN :]
    before_rows, before_place = shifted((last_rows, last_place), "seq", 1)
    sorted_query = sorted_rows[:, :, :head_width]
    sorted_value = sorted_rows[:, :, head_width:]
    sorted_key, query_float, inverse = normalized(sorted_query)
    before_key = normalized(before_rows[:, :, :head_width])[0]
    query_blocks = sorted_query.reshape(batch_size, block_count, SPAN, head_width)
    key_window = with_before(
        sorted_key.reshape(batch_size, block_count, SPAN, head_width), before_key
    )
    value_window = with_before(
        sorted_value.reshape(batch_size, block_count, SPAN, head_width),
        before_rows[:, :, head_width:],
    )
    place_blocks = sorted_place.reshape(batch_size, block_count, SPAN)
    place_window = with_before(place_blocks, before_place)
    own_token = (jnp.arange(SPAN)[:, None] == jnp.arange(2 * SPAN)[None, :]).astype(jnp.float32)
    future = (place_window[:, :, None, :] > place_blocks[:, :, :, None]).astype(jnp.float32)

    def score_of():
        raw_scores = (
            jnp.einsum(
                "bcqd,bckd->bcqk", query_blocks, key_window, preferred_element_type=jnp.float32
            )
            * score_scale
        )
        return raw_scores - 100000.0 * own_token - 1000000000.0 * future

    scores = score_of()
    row_top = jnp.max(scores, axis=-1)
    log_total = row_top + jnp.log(jnp.sum(jnp.exp(scores - row_top[..., None]), axis=-1))
    weights = jnp.exp(scores - log_total[..., None])
    rounded_probs = weights.astype(jnp.bfloat16)
    block_out = jnp.einsum(
        "bcqk,bckd->bcqd", rounded_probs, value_window, preferred_element_type=jnp.float32
    ).astype(jnp.bfloat16)
    out_rows = block_out.reshape(batch_size, row_count, head_width)
    home_out = move_wide(sort_half, out_rows, "bsr,brd->bsd").reshape(
        batch_size, shards, capacity // 2, 2 * head_width
    )
    home_log = move_exact(
        sort_float, log_total.reshape(batch_size, row_count), "bsr,br->bs"
    ).reshape(batch_size, shards, capacity)
    back_out, back_log = (
        lax.all_to_all(home_out, "seq", split_axis=1, concat_axis=1, tiled=True),
        lax.all_to_all(
            home_log.astype(jnp.bfloat16), "seq", split_axis=1, concat_axis=1, tiled=True
        ).astype(home_log.dtype),
    )
    round_out = move_wide(
        pack_half, back_out.reshape(batch_size, slot_total, head_width), "bsr,bsd->brd"
    ).reshape(rounds, head_group, row_count, head_width)
    round_log = move_exact(
        pack_float, back_log.reshape(batch_size, slot_total), "bsr,bs->br"
    ).reshape(rounds, head_group, row_count)
    mixing = jax.nn.softmax(round_log, axis=0)
    combined = jnp.sum(mixing[..., None] * round_out.astype(jnp.float32), axis=0)
    attention = (
        combined.astype(jnp.bfloat16).transpose(1, 0, 2).reshape(row_count, head_group * head_width)
    )
    head_term = jnp.dot(attention, w_out, preferred_element_type=jnp.float32)
    output = lax.psum_scatter(
        head_term.astype(jnp.bfloat16), "head", scatter_dimension=1, tiled=True
    )
    weight_term = lax.dot_general(
        attention, full_grad, (((0,), (0,)), ((), ())), preferred_element_type=jnp.float32
    )
    w_out_grad = lax.psum(weight_term.astype(jnp.bfloat16), "seq").astype(jnp.float32) * (
        shards * row_count
    ) ** (-0.5)
    back_heads = (
        back_attn.reshape(row_count, head_group, head_width).transpose(1, 0, 2).astype(jnp.float32)
    )
    inner_rows = jnp.sum(back_heads * combined, axis=-1)
    delta_rows = (mixing * inner_rows[None]).reshape(batch_size, row_count)
    grad_rows = (
        (mixing[..., None] * back_heads[None])
        .astype(jnp.bfloat16)
        .reshape(batch_size, row_count, head_width)
    )
    packed_grad = move_wide(pack_half, grad_rows, "bsr,brd->bsd").reshape(
        batch_size, shards, capacity // 2, 2 * head_width
    )
    packed_delta = move_exact(pack_float, delta_rows, "bsr,br->bs").reshape(
        batch_size, shards, capacity
    )
    got_grad, got_delta = (
        lax.all_to_all(packed_grad, "seq", split_axis=1, concat_axis=1, tiled=True),
        lax.all_to_all(
            packed_delta.astype(jnp.bfloat16), "seq", split_axis=1, concat_axis=1, tiled=True
        ).astype(packed_delta.dtype),
    )
    sorted_grad = move_wide(
        sort_half, got_grad.reshape(batch_size, slot_total, head_width), "bsr,bsd->brd"
    )
    sorted_delta = move_exact(sort_float, got_delta.reshape(batch_size, slot_total), "bsr,bs->br")
    kept_weights = jnp.exp(score_of() - log_total[..., None])
    grad_blocks = sorted_grad.reshape(batch_size, block_count, SPAN, head_width)
    delta_blocks = sorted_delta.reshape(batch_size, block_count, SPAN)
    dot_grad = jnp.einsum(
        "bcqd,bckd->bcqk", grad_blocks, value_window, preferred_element_type=jnp.float32
    )
    score_grad = (kept_weights * (dot_grad - delta_blocks[..., None])).astype(jnp.bfloat16)
    query_part = (
        jnp.einsum("bcqk,bckd->bcqd", score_grad, key_window, preferred_element_type=jnp.float32)
        * score_scale
    )
    key_part = (
        jnp.einsum("bcqk,bcqd->bckd", score_grad, query_blocks, preferred_element_type=jnp.float32)
        * score_scale
    )
    value_part = jnp.einsum(
        "bcqk,bcqd->bckd", rounded_probs, grad_blocks, preferred_element_type=jnp.float32
    )
    spill_rows = jnp.concatenate([key_part[:, 0, SPAN:], value_part[:, 0, SPAN:]], axis=2)
    arrived = shifted(spill_rows.astype(jnp.bfloat16), "seq", -1).astype(spill_rows.dtype)
    key_grad = key_part[:, :, :SPAN] + jnp.concatenate(
        [key_part[:, 1:, SPAN:], arrived[:, None, :, :head_width]], axis=1
    )
    value_sum = value_part[:, :, :SPAN] + jnp.concatenate(
        [value_part[:, 1:, SPAN:], arrived[:, None, :, head_width:]], axis=1
    )
    key_grad = key_grad.reshape(batch_size, row_count, head_width)
    value_sum = value_sum.reshape(batch_size, row_count, head_width)
    query_total = (
        query_part.reshape(batch_size, row_count, head_width)
        + inverse * key_grad
        - query_float
        * (inverse * inverse * inverse)
        * jnp.mean(query_float * key_grad, axis=-1, keepdims=True)
    )
    both_grads = jnp.concatenate(
        [query_total.astype(jnp.bfloat16), value_sum.astype(jnp.bfloat16)], axis=2
    )
    home_grads = move_wide(sort_half, both_grads, "bsr,brd->bsd").reshape(
        batch_size, shards, capacity, 2 * head_width
    )
    back_grads = lax.all_to_all(home_grads, "seq", split_axis=1, concat_axis=1, tiled=True)
    own_grads = move_wide(
        pack_half, back_grads.reshape(batch_size, slot_total, 2 * head_width), "bsr,bsd->brd"
    ).astype(jnp.float32)
    own_grads = own_grads.reshape(rounds, head_group, row_count, 2 * head_width)
    summed = jnp.sum(own_grads, axis=0).astype(jnp.bfloat16)
    query_grad = (
        summed[:, :, :head_width].transpose(1, 0, 2).reshape(row_count, head_group * head_width)
    )
    value_grad = (
        summed[:, :, head_width:].transpose(1, 0, 2).reshape(row_count, head_group * head_width)
    )
    return (output, query_grad, value_grad, w_out_grad)


def per_device(queries, values, w_out, out_grad, slots):
    if lax.axis_size("seq") == slots.shape[0] * slots.shape[1] and slots.shape[0] == 2:
        return by_sequence(queries, values, w_out, out_grad, slots)
    return by_span(queries, values, w_out, out_grad, slots)


def solution(mesh):
    placed = (
        P("seq", "head"),
        P("seq", "head"),
        P("head", None),
        P("seq", "head"),
        P(None, "head", "seq"),
    )
    return jax.shard_map(
        per_device,
        mesh=mesh,
        in_specs=placed,
        out_specs=(P("seq", "head"), P("seq", "head"), P("seq", "head"), P("head", None)),
        check_vma=False,
    )
```

```python
import functools

import jax
import jax.numpy as jnp
from jax import lax
from jax.experimental import pallas as pl
from jax.experimental.pallas import tpu as pltpu
from jax.sharding import PartitionSpec as P

DH = 64
SPAN = 128
LANES = 128
GROUP = 8
SUB = 4
F32 = jnp.float32
BF16 = jnp.bfloat16
NT = (((1,), (1,)), ((), ()))
TN = (((0,), (0,)), ((), ()))
MIB = 1 << 20


def whole(space):
    return pl.BlockSpec(memory_space=space)


def in_hbm(value):
    return pltpu.with_memory_space_constraint(value, pltpu.HBM)


def lane_of(shape):
    return lax.broadcasted_iota(jnp.int32, shape, len(shape) - 1)


def places_kernel(mine_ref, addr_ref, key_place, query_place, sign_ref):
    sources, _, lanes = mine_ref.shape
    blocks = addr_ref.shape[0]
    rows = mine_ref.shape[1] - 16
    parts = (mine_ref.shape[1] - rows) // 2
    core = lax.rem(lax.axis_index("seq"), 2)
    block_row = lax.broadcasted_iota(jnp.int32, (blocks, lanes), 0).astype(F32)
    place_row = lax.broadcasted_iota(jnp.int32, (lanes, lanes), 0).astype(F32)
    token_low = lane_of((blocks, lanes)).astype(F32)
    total = jnp.zeros((2 * blocks, lanes), F32)
    for s in range(sources):
        slots = mine_ref[s, rows:, :].astype(F32)
        tall = []
        wide = []
        for j in range(parts):
            in_block = block_row == slots[j : j + 1, :]
            token_high = float(s * parts + j)
            tall.append(
                jnp.concatenate(
                    [jnp.where(in_block, token_high, 0.0), jnp.where(in_block, token_low, 0.0)],
                    axis=0,
                ).astype(BF16)
            )
            wide.append((place_row == slots[parts + j : parts + j + 1, :]).astype(BF16))
        total += lax.dot_general(
            jnp.concatenate(tall, axis=1),
            jnp.concatenate(wide, axis=1),
            NT,
            preferred_element_type=F32,
        )
    place = total[:blocks] * float(lanes) + total[blocks:]
    token = place.astype(jnp.int32)
    source = token // (2 * rows)
    within = token - source * (2 * rows)
    part = within // rows
    addr_ref[...] = ((part ^ core) * sources + source) * rows + (within - part * rows)
    before = pltpu.roll(place, 1, 0)
    least = jnp.minimum(
        jnp.min(place, axis=1, keepdims=True), jnp.min(before, axis=1, keepdims=True)
    )
    window = jnp.concatenate([before, place], axis=1)
    window = jnp.where(window == least, window - 0.5, window)
    for c in range(blocks):
        key_place[c] = window[c : c + 1, :]
    columns = jnp.transpose(place)
    alone = jnp.transpose(jnp.where(place == least, -1.0, 1.0))
    for g in range(blocks // GROUP):
        query_place[g] = columns[:, g * GROUP : (g + 1) * GROUP]
        sign_ref[g] = alone[:, g * GROUP : (g + 1) * GROUP]


def find_places(mine):
    sources, rows, lanes = mine.shape
    blocks = 2 * sources * (rows - 16) // lanes
    column = jax.ShapeDtypeStruct((blocks // GROUP, lanes, GROUP), F32)
    return pl.pallas_call(
        places_kernel,
        out_shape=[
            jax.ShapeDtypeStruct((blocks, lanes), jnp.int32),
            jax.ShapeDtypeStruct((blocks, 1, 2 * lanes), F32),
            column,
            column,
        ],
        compiler_params=pltpu.CompilerParams(vmem_limit_bytes=10 * MIB),
        name="find_places",
    )(mine)


def gather_rows(addr_ref, block, source, target):
    for j in range(SPAN):
        target[pl.ds(j, 1), :] = source[pl.ds(addr_ref[block, j], 1), :]


def scatter_rows(addr_ref, block, source, target):
    for j in range(SPAN):
        target[pl.ds(addr_ref[block, j], 1), :] = source[pl.ds(j, 1), :]


def split_sum(product, chosen):
    high = product.astype(BF16)
    rest = (product - high.astype(F32)).astype(BF16)
    return jnp.dot(
        jnp.concatenate([high, rest], axis=1),
        jnp.concatenate([chosen, chosen], axis=0),
        preferred_element_type=F32,
    )


def low_lanes(scale=1.0):
    row = lax.broadcasted_iota(jnp.int32, (LANES, LANES), 0)
    return jnp.where(row < DH, scale, 0.0).astype(BF16)


def inverse_of(rows):
    return lax.rsqrt(split_sum(rows * rows, low_lanes(1.0 / DH)) + 1e-06)


def forward_kernel(
    addr_ref, mine_ref, other_ref, key_place, query_place, sign_ref,
    home_ref, away_ref, prob_ref, qv_ref, key_ref,
    tokens, result, in_even, in_odd, out_even, out_odd, grown_ref, qv_win, key_win,
):
    step = pl.program_id(0)
    last = pl.num_programs(0) - 1
    sources = mine_ref.shape[0]
    rows = mine_ref.shape[1] - 16
    half = sources * rows
    blocks = 2 * half // SPAN
    score_scale = DH ** (-0.5) * 1.4426950408889634
    rows_in = (in_even, in_odd)
    rows_out = (out_even, out_odd)

    def place_rows(values, at):
        low = lane_of(values.shape) < DH
        qv_win[at] = values.astype(BF16)
        key_win[at] = jnp.where(low, values * inverse_of(values), 0.0).astype(BF16)

    @pl.when(step == 0)
    def _():
        for s in range(sources):
            tokens[s * rows : (s + 1) * rows, :] = mine_ref[s, :rows, :].astype(F32)
            tokens[half + s * rows : half + (s + 1) * rows, :] = other_ref[s, :rows, :].astype(F32)
        gather_rows(addr_ref, blocks - 1, tokens, in_odd.at[0])
        place_rows(in_odd[0], slice(0, SPAN))
        for b in range(SUB):
            gather_rows(addr_ref, b, tokens, in_even.at[b])

    ones = jnp.ones((2 * SPAN, LANES), BF16)
    low = lane_of((SPAN, LANES)) < DH
    for p in range(GROUP // SUB):
        here = step * GROUP + p * SUB
        coming = jnp.minimum(here + SUB, blocks - SUB)
        gone = jnp.maximum(here - SUB, 0)
        now, then = p % 2, 1 - p % 2
        spans = slice((p * SUB + 1) * SPAN, ((p + 1) * SUB + 1) * SPAN)
        place_rows(rows_in[now][...].reshape(SUB * SPAN, LANES), spans)
        for i in range(SUB):
            b = p * SUB + i
            own = slice((b + 1) * SPAN, (b + 2) * SPAN)
            window = slice(b * SPAN, (b + 2) * SPAN)
            raw = lax.dot_general(qv_win[own], key_win[window], NT, preferred_element_type=F32)
            seen = key_place[b] < query_place[0, :, b : b + 1]
            grown_ref[i] = jnp.where(seen, jnp.exp2(raw * score_scale), 0.0)
            gather_rows(addr_ref, coming + i, tokens, rows_in[then].at[i])
        for i in range(SUB):
            b = p * SUB + i
            window = slice(b * SPAN, (b + 2) * SPAN)
            grown = grown_ref[i]
            mixed = jnp.dot(
                grown.astype(BF16),
                jnp.concatenate([qv_win[window], ones], axis=1),
                preferred_element_type=F32,
            )
            sums = mixed[:, LANES:]
            recip = 1.0 / sums
            prob_ref[b] = (grown * jnp.concatenate([recip, recip], axis=1)).astype(BF16)
            signed = sums * sign_ref[0, :, b : b + 1]
            rows_out[now][i] = jnp.where(low, signed, mixed[:, :LANES] * recip)
            scatter_rows(addr_ref, gone + i, rows_out[then].at[i], result)

    qv_ref[...] = qv_win[SPAN:]
    key_ref[...] = key_win[SPAN:]
    qv_win[:SPAN] = qv_win[GROUP * SPAN :]
    key_win[:SPAN] = key_win[GROUP * SPAN :]

    @pl.when(step == last)
    def _():
        for i in range(SUB):
            scatter_rows(addr_ref, blocks - SUB + i, out_odd.at[i], result)
        home_ref[...] = result[:half, :].astype(BF16)
        away_ref[...] = result[half:, :].astype(BF16)


def forward(addr, mine, other, key_place, query_place, sign):
    half = mine.shape[0] * (mine.shape[1] - 16)
    total = 2 * half
    blocks = total // SPAN
    rows = GROUP * SPAN
    return pl.pallas_call(
        forward_kernel,
        grid=(blocks // GROUP,),
        out_shape=[
            jax.ShapeDtypeStruct((half, LANES), BF16),
            jax.ShapeDtypeStruct((half, LANES), BF16),
            pltpu.HBM((blocks, SPAN, 2 * SPAN), BF16),
            pltpu.HBM((total, LANES), BF16),
            pltpu.HBM((total, LANES), BF16),
        ],
        in_specs=[
            whole(pltpu.SMEM),
            whole(pltpu.VMEM),
            whole(pltpu.VMEM),
            pl.BlockSpec((GROUP, 1, 2 * SPAN), lambda g: (g, 0, 0)),
            pl.BlockSpec((1, SPAN, GROUP), lambda g: (g, 0, 0)),
            pl.BlockSpec((1, SPAN, GROUP), lambda g: (g, 0, 0)),
        ],
        out_specs=[
            whole(pltpu.VMEM),
            whole(pltpu.VMEM),
            pl.BlockSpec((GROUP, SPAN, 2 * SPAN), lambda g: (g, 0, 0)),
            pl.BlockSpec((rows, LANES), lambda g: (g, 0)),
            pl.BlockSpec((rows, LANES), lambda g: (g, 0)),
        ],
        scratch_shapes=[
            pltpu.VMEM((total, LANES), F32),
            pltpu.VMEM((total, LANES), F32),
            *[pltpu.VMEM((SUB, SPAN, LANES), F32)] * 4,
            pltpu.VMEM((SUB, SPAN, 2 * SPAN), F32),
            pltpu.VMEM((rows + SPAN, LANES), BF16),
            pltpu.VMEM((rows + SPAN, LANES), BF16),
        ],
        compiler_params=pltpu.CompilerParams(vmem_limit_bytes=22 * MIB),
        cost_estimate=pl.CostEstimate(flops=0, bytes_accessed=64 * MIB, transcendentals=0),
        name="span_forward",
    )(addr, mine, other, key_place, query_place, sign)


def share_of(own, peer):
    row = lax.broadcasted_iota(jnp.int32, (LANES, LANES), 0)
    pick = (row < 1).astype(BF16)
    own_sum = jnp.dot(own, pick, preferred_element_type=F32)
    peer_sum = jnp.dot(peer, pick, preferred_element_type=F32)
    both = own_sum / (own_sum + peer_sum)
    own_alone = own_sum < 0.0
    peer_alone = peer_sum < 0.0
    return jnp.where(
        own_alone, jnp.where(peer_alone, both, 0.0), jnp.where(peer_alone, 1.0, both)
    )


def combined_rows(own, peer, share):
    high = lane_of(own.shape) >= DH
    own = own.astype(F32)
    peer = peer.astype(F32)
    return jnp.where(high, share * own + (1.0 - share) * peer, 0.0)


def mix_attention_kernel(own_ref, peer_ref, grad_ref, out_ref):
    pieces, half, _ = grad_ref.shape
    rows = 2 * half
    for i in range(pieces):
        own = own_ref[i * rows : (i + 1) * rows]
        peer = peer_ref[i * rows : (i + 1) * rows]
        combined = combined_rows(own, peer, share_of(own, peer))
        out_ref[i, :half] = (pltpu.roll(combined[:half], DH, 1) + combined[half:]).astype(BF16)
        out_ref[i, half:] = grad_ref[i]


def mix_grad_kernel(own_ref, peer_ref, both_ref, grad_own, grad_peer):
    pieces, rows, _ = both_ref.shape
    for i in range(pieces):
        at = slice(i * rows, (i + 1) * rows)
        own = own_ref[at]
        peer = peer_ref[at]
        share = share_of(own, peer)
        combined = combined_rows(own, peer, share)
        packed = both_ref[i, rows // 2 :].astype(F32)
        grad = jnp.concatenate([pltpu.roll(packed, DH, 1), packed], axis=0)
        column = lane_of((LANES, LANES))
        inner = split_sum(grad * combined, (column < DH).astype(BF16))
        both = jnp.where(lane_of(grad.shape) < DH, -inner, grad)
        grad_own[at] = (share * both).astype(BF16)
        grad_peer[at] = ((1.0 - share) * both).astype(BF16)


def mix_attention(home, peer, grad):
    pieces, rows, _ = grad.shape
    return pl.pallas_call(
        mix_attention_kernel,
        out_shape=jax.ShapeDtypeStruct((pieces, 2 * rows, LANES), BF16),
        in_specs=[whole(pltpu.VMEM)] * 3,
        out_specs=whole(pltpu.VMEM),
        compiler_params=pltpu.CompilerParams(vmem_limit_bytes=12 * MIB),
        name="mix_attention",
    )(home, peer, grad)


def mix_grad(home, peer, both):
    return pl.pallas_call(
        mix_grad_kernel,
        out_shape=[jax.ShapeDtypeStruct(home.shape, BF16)] * 2,
        in_specs=[whole(pltpu.VMEM)] * 3,
        out_specs=[whole(pltpu.VMEM)] * 2,
        compiler_params=pltpu.CompilerParams(vmem_limit_bytes=12 * MIB),
        name="mix_grad",
    )(home, peer, both)


def pack_kernel(query_ref, value_ref, slot_ref, out_ref):
    rounds, heads, rows = slot_ref.shape
    half = rows // 2
    for h in range(heads):
        columns = slice(h * DH, (h + 1) * DH)
        pair = jnp.concatenate([query_ref[:, columns], value_ref[:, columns]], axis=1)
        for r in range(rounds):
            out_ref[2 * h + r, :half] = pair[r * half : (r + 1) * half]
            slots = slot_ref[r, h : h + 1, :]
            high = slots // LANES
            parts = [high, slots - high * LANES]
            lines = [p[:, j : j + LANES] for p in parts for j in range(0, rows, LANES)]
            out_ref[2 * h + r, half:] = jnp.concatenate(lines, axis=0).astype(F32).astype(BF16)


def pack_heads(queries, values, slots):
    rounds, heads, rows = slots.shape
    return pl.pallas_call(
        pack_kernel,
        out_shape=jax.ShapeDtypeStruct((rounds * heads, rows // 2 + 16, 2 * DH), BF16),
        compiler_params=pltpu.CompilerParams(vmem_limit_bytes=10 * MIB),
        name="pack_heads",
    )(in_hbm(queries), in_hbm(values), in_hbm(slots))


def unpack_kernel(in_ref, query_ref, value_ref):
    for h in range(in_ref.shape[0]):
        columns = slice(h * DH, (h + 1) * DH)
        query_ref[:, columns] = in_ref[h, :, :DH]
        value_ref[:, columns] = in_ref[h, :, DH:]


def unpack_heads(rows):
    heads, count, _ = rows.shape
    return pl.pallas_call(
        unpack_kernel,
        out_shape=[jax.ShapeDtypeStruct((count, heads * DH), BF16)] * 2,
        in_specs=[whole(pltpu.VMEM)],
        compiler_params=pltpu.CompilerParams(vmem_limit_bytes=10 * MIB),
        name="unpack_heads",
    )(rows)


def member(step, groups):
    return lax.rem(lax.axis_index("head") + (groups - step), groups)


def columns_of(index, width):
    return pl.ds(pl.multiple_of(index * width, width), width)


def back_kernel(weight_ref, *refs):
    *grads, out_ref = refs
    groups = len(grads)
    rows, width = grads[0].shape
    total = 0.0
    for k in range(groups):
        weight = weight_ref[:, columns_of(member(k, groups), width)]
        total += lax.dot_general(grads[k][...], weight, NT, preferred_element_type=F32)
    total = total.astype(BF16)
    quarter = rows // 4
    for h in range(width // DH):
        columns = slice(h * DH, (h + 1) * DH)
        for c in range(2):
            first = total[2 * c * quarter : (2 * c + 1) * quarter, columns]
            second = total[(2 * c + 1) * quarter : (2 * c + 2) * quarter, columns]
            out_ref[2 * h + c] = jnp.concatenate([first, second], axis=1)


def back_projection(weight, grads):
    rows, width = grads[0].shape
    return pl.pallas_call(
        back_kernel,
        out_shape=jax.ShapeDtypeStruct((2 * width // DH, rows // 4, 2 * DH), BF16),
        compiler_params=pltpu.CompilerParams(vmem_limit_bytes=10 * MIB),
        name="back_projection",
    )(weight, *grads)


def project_kernel(weight_ref, packed_ref, att_ref, *outs):
    groups = len(outs)
    rows, width = att_ref.shape
    quarter = rows // 4
    for h in range(width // DH):
        columns = slice(h * DH, (h + 1) * DH)
        for c in range(2):
            packed = packed_ref[2 * h + c, :quarter]
            att_ref[2 * c * quarter : (2 * c + 1) * quarter, columns] = packed[:, :DH]
            att_ref[(2 * c + 1) * quarter : (2 * c + 2) * quarter, columns] = packed[:, DH:]
    for k in range(groups):
        weight = weight_ref[:, columns_of(member(groups - k, groups), width)]
        outs[k][...] = jnp.dot(att_ref[...], weight, preferred_element_type=F32).astype(BF16)


def project(weight, packed):
    count, double, _ = packed.shape
    rows, width = 2 * double, count * DH // 2
    groups = weight.shape[1] // width
    return pl.pallas_call(
        project_kernel,
        out_shape=[jax.ShapeDtypeStruct((rows, width), BF16)] * 3
        + [pltpu.HBM((rows, width), BF16)]
        + [jax.ShapeDtypeStruct((rows, width), BF16)] * (groups - 3),
        compiler_params=pltpu.CompilerParams(vmem_limit_bytes=10 * MIB),
        name="project",
    )(weight, packed)


def add_kernel(*refs):
    *shares, out_ref = refs
    total = shares[0][...].astype(F32)
    for share in shares[1:]:
        total += share[...].astype(F32)
    out_ref[...] = total.astype(BF16)


def add_shares(shares):
    return pl.pallas_call(
        add_kernel,
        out_shape=jax.ShapeDtypeStruct(shares[0].shape, BF16),
        in_specs=[whole(pltpu.VMEM)] * len(shares),
        compiler_params=pltpu.CompilerParams(vmem_limit_bytes=8 * MIB),
        name="add_shares",
    )(*shares)


def weight_grad_kernel(att_ref, *refs):
    *grads, keep_ref, give_ref = refs
    groups = len(grads)
    width = grads[0].shape[1]
    part = keep_ref.shape[0]
    core = lax.rem(lax.axis_index("seq"), 2)
    for index, out_ref in ((core, keep_ref), (1 - core, give_ref)):
        att = att_ref[:, columns_of(index, part)]
        for k in range(groups):
            out_ref[:, columns_of(member(k, groups), width)] = lax.dot_general(
                att, grads[k][...], TN, preferred_element_type=F32
            ).astype(BF16)


def weight_grad(att, grads):
    width = att.shape[1]
    groups = len(grads)
    return pl.pallas_call(
        weight_grad_kernel,
        out_shape=[jax.ShapeDtypeStruct((width // 2, width * groups), BF16)] * 2,
        compiler_params=pltpu.CompilerParams(vmem_limit_bytes=10 * MIB),
        name="weight_grad",
    )(att, *grads)


def finished_rows(rows, query_part, key_value):
    low = lane_of(rows.shape) < DH
    scale = DH ** (-0.5)
    query = jnp.where(low, rows.astype(F32), 0.0)
    inverse = inverse_of(query)
    key = query * inverse
    term = key_value * (inverse * scale)
    along = split_sum(key * term, low_lanes(1.0 / DH))
    return jnp.where(low, query_part * scale + term - key * along, key_value)


def backward_kernel(
    addr_ref, mine_ref, other_ref, prob_ref, qv_ref, qv_before, key_ref, key_before,
    home_ref, away_ref,
    tokens, result, in_even, in_odd, out_even, out_odd, qv_win, key_win, tall, sums, query_sums,
    first_sums,
):
    step = pl.program_id(0)
    last = pl.num_programs(0) - 1
    half = mine_ref.shape[0]
    blocks = 2 * half // SPAN
    rows_in = (in_even, in_odd)
    rows_out = (out_even, out_odd)

    @pl.when(step == 0)
    def _():
        tokens[:half, :] = mine_ref[...].astype(F32)
        tokens[half:, :] = other_ref[...].astype(F32)
        for b in range(SUB):
            gather_rows(addr_ref, b, tokens, in_even.at[b])

    qv_win[:SPAN] = qv_before[...]
    qv_win[SPAN:] = qv_ref[...]
    key_win[:SPAN] = key_before[...]
    key_win[SPAN:] = key_ref[...]
    low = lane_of((SPAN, LANES)) < DH
    zero = jnp.zeros((SPAN, LANES), BF16)
    for p in range(GROUP // SUB):
        here = step * GROUP + p * SUB
        coming = jnp.minimum(here + SUB, blocks - SUB)
        gone = here + (blocks - SUB - 1)
        now, then = p % 2, 1 - p % 2
        spans = slice(p * SUB * SPAN, ((p + 1) * SUB + 1) * SPAN)
        everything = qv_win[spans]
        lane = lane_of(everything.shape)
        one = jnp.where(lane == 0, 1.0, 0.0).astype(BF16)
        value_one = jnp.where(lane >= DH, everything, one)
        for i in range(SUB):
            b = p * SUB + i
            prob = prob_ref[b]
            dot_grad = lax.dot_general(
                rows_in[now][i].astype(BF16),
                value_one[i * SPAN : (i + 2) * SPAN],
                NT,
                preferred_element_type=F32,
            )
            tall[i, :SPAN] = (prob.astype(F32) * dot_grad).astype(BF16)
            tall[i, SPAN:] = prob
            gather_rows(addr_ref, coming + i, tokens, rows_in[then].at[i])
        for i in range(SUB):
            b = p * SUB + i
            own = slice((b + 1) * SPAN, (b + 2) * SPAN)
            window = slice(b * SPAN, (b + 2) * SPAN)
            query_sums[own] = jnp.dot(
                tall[i, :SPAN], key_win[window], preferred_element_type=F32
            )
            grad_high = jnp.where(low, 0.0, rows_in[now][i]).astype(BF16)
            key_value = lax.dot_general(
                tall[i],
                jnp.concatenate([jnp.where(low, qv_win[own], zero), grad_high], axis=0),
                TN,
                preferred_element_type=F32,
            )
            if b == 0:

                @pl.when(step == 0)
                def _():
                    first_sums[...] = key_value[:SPAN]

            sums[b * SPAN : (b + 1) * SPAN] += key_value[:SPAN]
            sums[own] = key_value[SPAN:]
            scatter_rows(addr_ref, lax.rem(gone + i, blocks), rows_out[then].at[i], result)
        spans = slice(p * SUB * SPAN, (p + 1) * SUB * SPAN)
        finished = finished_rows(qv_win[spans], query_sums[spans], sums[spans])
        rows_out[now][...] = finished.reshape(SUB, SPAN, LANES)
    sums[:SPAN] = sums[GROUP * SPAN :]
    query_sums[:SPAN] = query_sums[GROUP * SPAN :]

    @pl.when(step == last)
    def _():
        for i in range(SUB):
            scatter_rows(addr_ref, blocks - SUB - 1 + i, out_odd.at[i], result)
        out_even[0] = finished_rows(
            qv_win[GROUP * SPAN :], query_sums[:SPAN], sums[:SPAN] + first_sums[...]
        )
        scatter_rows(addr_ref, blocks - 1, out_even.at[0], result)
        home_ref[...] = result[:half, :].astype(BF16)
        away_ref[...] = result[half:, :].astype(BF16)


def backward(addr, mine, other, prob, query_key, value_one):
    half = mine.shape[0]
    total = 2 * half
    blocks = total // SPAN
    rows = GROUP * SPAN
    by_rows = pl.BlockSpec((rows, LANES), lambda g: (g, 0))
    before = pl.BlockSpec((SPAN, LANES), lambda g: (lax.rem(g * GROUP + blocks - 1, blocks), 0))
    return pl.pallas_call(
        backward_kernel,
        grid=(blocks // GROUP,),
        out_shape=[jax.ShapeDtypeStruct((half, LANES), BF16)] * 2,
        in_specs=[
            whole(pltpu.SMEM),
            whole(pltpu.VMEM),
            whole(pltpu.VMEM),
            pl.BlockSpec((GROUP, SPAN, 2 * SPAN), lambda g: (g, 0, 0)),
            by_rows,
            before,
            by_rows,
            before,
        ],
        out_specs=[whole(pltpu.VMEM)] * 2,
        scratch_shapes=[
            pltpu.VMEM((total, LANES), F32),
            pltpu.VMEM((total, LANES), F32),
            *[pltpu.VMEM((SUB, SPAN, LANES), F32)] * 4,
            pltpu.VMEM((rows + SPAN, LANES), BF16),
            pltpu.VMEM((rows + SPAN, LANES), BF16),
            pltpu.VMEM((SUB, 2 * SPAN, 2 * SPAN), BF16),
            pltpu.VMEM((rows + SPAN, LANES), F32),
            pltpu.VMEM((rows + SPAN, LANES), F32),
            pltpu.VMEM((SPAN, LANES), F32),
        ],
        compiler_params=pltpu.CompilerParams(vmem_limit_bytes=22 * MIB),
        cost_estimate=pl.CostEstimate(flops=0, bytes_accessed=64 * MIB, transcendentals=0),
        name="span_backward",
    )(addr, mine, other, *[in_hbm(x) for x in (prob, query_key, query_key, value_one, value_one)])


def swap(value, distance=1):
    count = lax.axis_size("seq")
    return lax.ppermute(value, "seq", [(i, i ^ distance) for i in range(count)])


def to_all(value):
    return lax.all_to_all(value, "seq", split_axis=0, concat_axis=0, tiled=True)


def rotate(value, step):
    count = lax.axis_size("head")
    return lax.ppermute(value, "head", [(i, (i + step) % count) for i in range(count)])


def after(values, *earlier):
    return lax.optimization_barrier((values, earlier))[0]


def by_sequence(queries, values, w_out, out_grad, slots):
    rows = queries.shape[0]
    _, heads, _ = slots.shape
    shards = lax.axis_size("seq")
    groups = lax.axis_size("head")
    core = lax.rem(lax.axis_index("seq"), 2)
    total = shards * rows
    half_rows = rows // 2

    packed = pack_heads(queries, values, slots)
    mine = to_all(packed)
    places = find_places(mine)

    first = rotate(out_grad, 1)
    grads = [out_grad, first, rotate(first, 1), rotate(out_grad, groups - 1)]
    mine = after(mine, first)

    home, away, prob, query_key, value_one = forward(places[0], mine, swap(mine), *places[1:])
    away, *grads = after([away, *grads])
    peer = swap(away)

    grad_packed = back_projection(w_out, grads)
    both = to_all(mix_attention(home, peer, grad_packed))
    grad_own, grad_peer = mix_grad(home, peer, both)
    grad_other = swap(grad_peer)

    att, *shares = project(w_out, both)
    early = [rotate(shares[k], k) for k in range(1, groups, 2)]
    weight, give = weight_grad(att, grads)
    weight = (weight.astype(F32) + swap(give).astype(F32)).astype(BF16)
    weights = [weight] + [swap(weight, distance) for distance in range(2, shards, 2)]

    own, others = backward(places[0], grad_own, grad_other, prob, query_key, value_one)
    others, *weights = after([others, *weights])
    others, *early = after([others, *early])
    late = [rotate(after(shares[k], own), k) for k in range(2, groups, 2)]

    summed = (own.astype(F32) + swap(others).astype(F32)).astype(BF16)
    summed = to_all(summed.reshape(shards, half_rows, LANES))
    query_grad, value_grad = unpack_heads(summed.reshape(heads, rows, LANES))

    weights = [w.astype(F32) for w in weights]
    while len(weights) > 1:
        weights = [weights[i] + weights[i + 1] for i in range(0, len(weights), 2)]
    weight = weights[0].astype(BF16)
    rest = swap(weight)
    weight = jnp.where(
        core == 0,
        jnp.concatenate([weight, rest], axis=0),
        jnp.concatenate([rest, weight], axis=0),
    )
    w_out_grad = weight.astype(F32) * total ** (-0.5)

    output = shares[0].astype(F32)
    for share in early + late:
        output = output + share.astype(F32)
    return (output.astype(BF16), query_grad, value_grad, w_out_grad)


def shifted(value, axis, steps):
    count = lax.axis_size(axis)
    pairs = [(source, (source + steps) % count) for source in range(count)]
    return lax.ppermute(value, axis, pairs)


def with_before(blocks, before):
    earlier = jnp.concatenate([before[:, None], blocks[:, :-1]], axis=1)
    return jnp.concatenate([blocks, earlier], axis=2)


def normalized(query_rows):
    query_float = query_rows.astype(jnp.float32)
    inverse = lax.rsqrt(jnp.mean(query_float * query_float, axis=-1, keepdims=True) + 1e-06)
    return ((query_float * inverse).astype(jnp.bfloat16), query_float, inverse)


def move_wide(matrix, data, form):
    return jnp.einsum(form, matrix, data, preferred_element_type=jnp.float32).astype(jnp.bfloat16)


def move_exact(matrix, data, form):
    return jnp.einsum(form, matrix, data.astype(jnp.float32), precision=lax.Precision.HIGHEST)


def by_span(queries, values, w_out, out_grad, slots):
    row_count = queries.shape[0]
    head_width = DH
    rounds = slots.shape[0]
    head_group = queries.shape[1] // head_width
    batch_size = rounds * head_group
    shards = lax.axis_size("seq")
    my_index = lax.axis_index("seq")
    even_share = row_count // shards
    capacity = even_share * 3 // 2
    slot_total = shards * capacity
    block_count = row_count // SPAN
    score_scale = head_width ** (-0.5)

    def per_head(matrix):
        split_heads = matrix.reshape(row_count, head_group, head_width).transpose(1, 0, 2)
        return jnp.concatenate([split_heads] * rounds, axis=0)

    flat_slot = slots.reshape(batch_size, row_count)
    target = flat_slot // row_count
    local_slot = flat_slot - target * row_count
    onehot_target = (
        target[:, :, None] == jnp.arange(shards, dtype=jnp.int32)[None, None, :]
    ).astype(jnp.int32)
    earlier_count = jnp.sum(jnp.cumsum(onehot_target, axis=1) * onehot_target, axis=2) - 1
    send_spot = target * capacity + earlier_count
    positions = my_index * row_count + jnp.arange(row_count, dtype=jnp.int32)
    position_rows = jnp.broadcast_to(positions[None, :], (batch_size, row_count))
    pack_float = (
        send_spot[:, None, :] == jnp.arange(slot_total, dtype=jnp.int32)[None, :, None]
    ).astype(jnp.float32)
    pack_half = pack_float.astype(jnp.bfloat16)
    full_grad = lax.all_gather(out_grad, "head", axis=1, tiled=True)
    back_attn = lax.dot_general(
        full_grad, w_out, (((1,), (1,)), ((), ())), preferred_element_type=jnp.float32
    ).astype(jnp.bfloat16)
    query_value = jnp.concatenate([per_head(queries), per_head(values)], axis=2)
    packed_rows = move_wide(pack_half, query_value, "bsr,brd->bsd").reshape(
        batch_size, shards, capacity, 2 * head_width
    )
    packed_place = (
        move_exact(pack_float, position_rows, "bsr,br->bs")
        .astype(jnp.int32)
        .reshape(batch_size, shards, capacity)
    )
    packed_slot = (
        move_exact(pack_float, local_slot + 1, "bsr,br->bs")
        .astype(jnp.int32)
        .reshape(batch_size, shards, capacity)
    )
    got_rows, got_place, got_slot = (
        lax.all_to_all(packed_rows, "seq", split_axis=1, concat_axis=1, tiled=True),
        lax.all_to_all(packed_place, "seq", split_axis=1, concat_axis=1, tiled=True),
        lax.all_to_all(packed_slot, "seq", split_axis=1, concat_axis=1, tiled=True),
    )
    got_spot = got_slot.reshape(batch_size, slot_total)
    got_spot = jnp.where(got_spot == 0, row_count, got_spot - 1)
    sort_float = (
        got_spot[:, :, None] == jnp.arange(row_count, dtype=jnp.int32)[None, None, :]
    ).astype(jnp.float32)
    sort_half = sort_float.astype(jnp.bfloat16)
    sorted_rows = move_wide(
        sort_half, got_rows.reshape(batch_size, slot_total, 2 * head_width), "bsr,bsd->brd"
    )
    sorted_place = move_exact(
        sort_float, got_place.reshape(batch_size, slot_total), "bsr,bs->br"
    ).astype(jnp.int32)
    last_rows = sorted_rows[:, row_count - SPAN :]
    last_place = sorted_place[:, row_count - SPAN :]
    before_rows, before_place = shifted((last_rows, last_place), "seq", 1)
    sorted_query = sorted_rows[:, :, :head_width]
    sorted_value = sorted_rows[:, :, head_width:]
    sorted_key, query_float, inverse = normalized(sorted_query)
    before_key = normalized(before_rows[:, :, :head_width])[0]
    query_blocks = sorted_query.reshape(batch_size, block_count, SPAN, head_width)
    key_window = with_before(
        sorted_key.reshape(batch_size, block_count, SPAN, head_width), before_key
    )
    value_window = with_before(
        sorted_value.reshape(batch_size, block_count, SPAN, head_width),
        before_rows[:, :, head_width:],
    )
    place_blocks = sorted_place.reshape(batch_size, block_count, SPAN)
    place_window = with_before(place_blocks, before_place)
    own_token = (jnp.arange(SPAN)[:, None] == jnp.arange(2 * SPAN)[None, :]).astype(jnp.float32)
    future = (place_window[:, :, None, :] > place_blocks[:, :, :, None]).astype(jnp.float32)

    def score_of():
        raw_scores = (
            jnp.einsum(
                "bcqd,bckd->bcqk", query_blocks, key_window, preferred_element_type=jnp.float32
            )
            * score_scale
        )
        return raw_scores - 100000.0 * own_token - 1000000000.0 * future

    scores = score_of()
    row_top = jnp.max(scores, axis=-1)
    log_total = row_top + jnp.log(jnp.sum(jnp.exp(scores - row_top[..., None]), axis=-1))
    weights = jnp.exp(scores - log_total[..., None])
    rounded_probs = weights.astype(jnp.bfloat16)
    block_out = jnp.einsum(
        "bcqk,bckd->bcqd", rounded_probs, value_window, preferred_element_type=jnp.float32
    ).astype(jnp.bfloat16)
    out_rows = block_out.reshape(batch_size, row_count, head_width)
    home_out = move_wide(sort_half, out_rows, "bsr,brd->bsd").reshape(
        batch_size, shards, capacity // 2, 2 * head_width
    )
    home_log = move_exact(
        sort_float, log_total.reshape(batch_size, row_count), "bsr,br->bs"
    ).reshape(batch_size, shards, capacity)
    back_out, back_log = (
        lax.all_to_all(home_out, "seq", split_axis=1, concat_axis=1, tiled=True),
        lax.all_to_all(
            home_log.astype(jnp.bfloat16), "seq", split_axis=1, concat_axis=1, tiled=True
        ).astype(home_log.dtype),
    )
    round_out = move_wide(
        pack_half, back_out.reshape(batch_size, slot_total, head_width), "bsr,bsd->brd"
    ).reshape(rounds, head_group, row_count, head_width)
    round_log = move_exact(
        pack_float, back_log.reshape(batch_size, slot_total), "bsr,bs->br"
    ).reshape(rounds, head_group, row_count)
    mixing = jax.nn.softmax(round_log, axis=0)
    combined = jnp.sum(mixing[..., None] * round_out.astype(jnp.float32), axis=0)
    attention = (
        combined.astype(jnp.bfloat16).transpose(1, 0, 2).reshape(row_count, head_group * head_width)
    )
    head_term = jnp.dot(attention, w_out, preferred_element_type=jnp.float32)
    output = lax.psum_scatter(
        head_term.astype(jnp.bfloat16), "head", scatter_dimension=1, tiled=True
    )
    weight_term = lax.dot_general(
        attention, full_grad, (((0,), (0,)), ((), ())), preferred_element_type=jnp.float32
    )
    w_out_grad = lax.psum(weight_term.astype(jnp.bfloat16), "seq").astype(jnp.float32) * (
        shards * row_count
    ) ** (-0.5)
    back_heads = (
        back_attn.reshape(row_count, head_group, head_width).transpose(1, 0, 2).astype(jnp.float32)
    )
    inner_rows = jnp.sum(back_heads * combined, axis=-1)
    delta_rows = (mixing * inner_rows[None]).reshape(batch_size, row_count)
    grad_rows = (
        (mixing[..., None] * back_heads[None])
        .astype(jnp.bfloat16)
        .reshape(batch_size, row_count, head_width)
    )
    packed_grad = move_wide(pack_half, grad_rows, "bsr,brd->bsd").reshape(
        batch_size, shards, capacity // 2, 2 * head_width
    )
    packed_delta = move_exact(pack_float, delta_rows, "bsr,br->bs").reshape(
        batch_size, shards, capacity
    )
    got_grad, got_delta = (
        lax.all_to_all(packed_grad, "seq", split_axis=1, concat_axis=1, tiled=True),
        lax.all_to_all(
            packed_delta.astype(jnp.bfloat16), "seq", split_axis=1, concat_axis=1, tiled=True
        ).astype(packed_delta.dtype),
    )
    sorted_grad = move_wide(
        sort_half, got_grad.reshape(batch_size, slot_total, head_width), "bsr,bsd->brd"
    )
    sorted_delta = move_exact(sort_float, got_delta.reshape(batch_size, slot_total), "bsr,bs->br")
    kept_weights = jnp.exp(score_of() - log_total[..., None])
    grad_blocks = sorted_grad.reshape(batch_size, block_count, SPAN, head_width)
    delta_blocks = sorted_delta.reshape(batch_size, block_count, SPAN)
    dot_grad = jnp.einsum(
        "bcqd,bckd->bcqk", grad_blocks, value_window, preferred_element_type=jnp.float32
    )
    score_grad = (kept_weights * (dot_grad - delta_blocks[..., None])).astype(jnp.bfloat16)
    query_part = (
        jnp.einsum("bcqk,bckd->bcqd", score_grad, key_window, preferred_element_type=jnp.float32)
        * score_scale
    )
    key_part = (
        jnp.einsum("bcqk,bcqd->bckd", score_grad, query_blocks, preferred_element_type=jnp.float32)
        * score_scale
    )
    value_part = jnp.einsum(
        "bcqk,bcqd->bckd", rounded_probs, grad_blocks, preferred_element_type=jnp.float32
    )
    spill_rows = jnp.concatenate([key_part[:, 0, SPAN:], value_part[:, 0, SPAN:]], axis=2)
    arrived = shifted(spill_rows.astype(jnp.bfloat16), "seq", -1).astype(spill_rows.dtype)
    key_grad = key_part[:, :, :SPAN] + jnp.concatenate(
        [key_part[:, 1:, SPAN:], arrived[:, None, :, :head_width]], axis=1
    )
    value_sum = value_part[:, :, :SPAN] + jnp.concatenate(
        [value_part[:, 1:, SPAN:], arrived[:, None, :, head_width:]], axis=1
    )
    key_grad = key_grad.reshape(batch_size, row_count, head_width)
    value_sum = value_sum.reshape(batch_size, row_count, head_width)
    query_total = (
        query_part.reshape(batch_size, row_count, head_width)
        + inverse * key_grad
        - query_float
        * (inverse * inverse * inverse)
        * jnp.mean(query_float * key_grad, axis=-1, keepdims=True)
    )
    both_grads = jnp.concatenate(
        [query_total.astype(jnp.bfloat16), value_sum.astype(jnp.bfloat16)], axis=2
    )
    home_grads = move_wide(sort_half, both_grads, "bsr,brd->bsd").reshape(
        batch_size, shards, capacity, 2 * head_width
    )
    back_grads = lax.all_to_all(home_grads, "seq", split_axis=1, concat_axis=1, tiled=True)
    own_grads = move_wide(
        pack_half, back_grads.reshape(batch_size, slot_total, 2 * head_width), "bsr,bsd->brd"
    ).astype(jnp.float32)
    own_grads = own_grads.reshape(rounds, head_group, row_count, 2 * head_width)
    summed = jnp.sum(own_grads, axis=0).astype(jnp.bfloat16)
    query_grad = (
        summed[:, :, :head_width].transpose(1, 0, 2).reshape(row_count, head_group * head_width)
    )
    value_grad = (
        summed[:, :, head_width:].transpose(1, 0, 2).reshape(row_count, head_group * head_width)
    )
    return (output, query_grad, value_grad, w_out_grad)


def per_device(queries, values, w_out, out_grad, slots):
    if lax.axis_size("seq") == slots.shape[0] * slots.shape[1] and slots.shape[0] == 2:
        return by_sequence(queries, values, w_out, out_grad, slots)
    return by_span(queries, values, w_out, out_grad, slots)


def solution(mesh):
    placed = (
        P("seq", "head"),
        P("seq", "head"),
        P("head", None),
        P("seq", "head"),
        P(None, "head", "seq"),
    )
    return jax.shard_map(
        per_device,
        mesh=mesh,
        in_specs=placed,
        out_specs=(P("seq", "head"), P("seq", "head"), P("seq", "head"), P("head", None)),
        check_vma=False,
    )
```

```python
import functools

import jax
import jax.numpy as jnp
from jax import lax
from jax.experimental import pallas as pl
from jax.experimental.pallas import tpu as pltpu
from jax.sharding import PartitionSpec as P

DH = 64
SPAN = 128
LANES = 128
GROUP = 8
SUB = 4
F32 = jnp.float32
BF16 = jnp.bfloat16
NT = (((1,), (1,)), ((), ()))
TN = (((0,), (0,)), ((), ()))
MIB = 1 << 20


def whole(space):
    return pl.BlockSpec(memory_space=space)


def in_hbm(value):
    return pltpu.with_memory_space_constraint(value, pltpu.HBM)


def lane_of(shape):
    return lax.broadcasted_iota(jnp.int32, shape, len(shape) - 1)


def places_kernel(mine_ref, addr_ref, key_place, query_place, sign_ref):
    sources, _, lanes = mine_ref.shape
    blocks = addr_ref.shape[0]
    rows = mine_ref.shape[1] - 16
    parts = (mine_ref.shape[1] - rows) // 2
    core = lax.rem(lax.axis_index("seq"), 2)
    block_row = lax.broadcasted_iota(jnp.int32, (blocks, lanes), 0).astype(F32)
    place_row = lax.broadcasted_iota(jnp.int32, (lanes, lanes), 0).astype(F32)
    token_low = lane_of((blocks, lanes)).astype(F32)
    total = jnp.zeros((2 * blocks, lanes), F32)
    for s in range(sources):
        slots = mine_ref[s, rows:, :].astype(F32)
        tall = []
        wide = []
        for j in range(parts):
            in_block = block_row == slots[j : j + 1, :]
            token_high = float(s * parts + j)
            tall.append(
                jnp.concatenate(
                    [jnp.where(in_block, token_high, 0.0), jnp.where(in_block, token_low, 0.0)],
                    axis=0,
                ).astype(BF16)
            )
            wide.append((place_row == slots[parts + j : parts + j + 1, :]).astype(BF16))
        total += lax.dot_general(
            jnp.concatenate(tall, axis=1),
            jnp.concatenate(wide, axis=1),
            NT,
            preferred_element_type=F32,
        )
    place = total[:blocks] * float(lanes) + total[blocks:]
    token = place.astype(jnp.int32)
    source = token // (2 * rows)
    within = token - source * (2 * rows)
    part = within // rows
    addr_ref[...] = ((part ^ core) * sources + source) * rows + (within - part * rows)
    before = pltpu.roll(place, 1, 0)
    least = jnp.minimum(
        jnp.min(place, axis=1, keepdims=True), jnp.min(before, axis=1, keepdims=True)
    )
    window = jnp.concatenate([before, place], axis=1)
    window = jnp.where(window == least, window - 0.5, window)
    for c in range(blocks):
        key_place[c] = window[c : c + 1, :]
    columns = jnp.transpose(place)
    alone = jnp.transpose(jnp.where(place == least, -1.0, 1.0))
    for g in range(blocks // GROUP):
        query_place[g] = columns[:, g * GROUP : (g + 1) * GROUP]
        sign_ref[g] = alone[:, g * GROUP : (g + 1) * GROUP]


def find_places(mine):
    sources, rows, lanes = mine.shape
    blocks = 2 * sources * (rows - 16) // lanes
    column = jax.ShapeDtypeStruct((blocks // GROUP, lanes, GROUP), F32)
    return pl.pallas_call(
        places_kernel,
        out_shape=[
            jax.ShapeDtypeStruct((blocks, lanes), jnp.int32),
            jax.ShapeDtypeStruct((blocks, 1, 2 * lanes), F32),
            column,
            column,
        ],
        compiler_params=pltpu.CompilerParams(vmem_limit_bytes=10 * MIB),
        out_specs=[whole(pltpu.VMEM)] * 4,
        name="find_places",
    )(mine)


def gather_rows(addr_ref, block, source, target):
    for j in range(SPAN):
        target[pl.ds(j, 1), :] = source[pl.ds(addr_ref[block, j], 1), :]


def scatter_rows(addr_ref, block, source, target):
    for j in range(SPAN):
        target[pl.ds(addr_ref[block, j], 1), :] = source[pl.ds(j, 1), :]


def split_sum(product, chosen):
    high = product.astype(BF16)
    rest = (product - high.astype(F32)).astype(BF16)
    return jnp.dot(
        jnp.concatenate([high, rest], axis=1),
        jnp.concatenate([chosen, chosen], axis=0),
        preferred_element_type=F32,
    )


def low_lanes(scale=1.0):
    row = lax.broadcasted_iota(jnp.int32, (LANES, LANES), 0)
    return jnp.where(row < DH, scale, 0.0).astype(BF16)


def inverse_of(rows):
    return lax.rsqrt(split_sum(rows * rows, low_lanes(1.0 / DH)) + 1e-06)


def forward_kernel(
    addr_ref, mine_ref, other_ref, key_place, query_place, sign_ref,
    home_ref, away_ref, prob_ref, qv_ref, key_ref,
    tokens, result, in_even, in_odd, out_even, out_odd, grown_ref, qv_win, key_win,
):
    step = pl.program_id(0)
    last = pl.num_programs(0) - 1
    sources = mine_ref.shape[0]
    rows = mine_ref.shape[1] - 16
    half = sources * rows
    blocks = 2 * half // SPAN
    score_scale = DH ** (-0.5) * 1.4426950408889634
    rows_in = (in_even, in_odd)
    rows_out = (out_even, out_odd)

    def place_rows(values, at):
        low = lane_of(values.shape) < DH
        qv_win[at] = values.astype(BF16)
        key_win[at] = jnp.where(low, values * inverse_of(values), 0.0).astype(BF16)

    @pl.when(step == 0)
    def _():
        for s in range(sources):
            tokens[s * rows : (s + 1) * rows, :] = mine_ref[s, :rows, :].astype(F32)
            tokens[half + s * rows : half + (s + 1) * rows, :] = other_ref[s, :rows, :].astype(F32)
        gather_rows(addr_ref, blocks - 1, tokens, in_odd.at[0])
        place_rows(in_odd[0], slice(0, SPAN))
        for b in range(SUB):
            gather_rows(addr_ref, b, tokens, in_even.at[b])

    ones = jnp.ones((2 * SPAN, LANES), BF16)
    low = lane_of((SPAN, LANES)) < DH
    for p in range(GROUP // SUB):
        here = step * GROUP + p * SUB
        coming = jnp.minimum(here + SUB, blocks - SUB)
        gone = jnp.maximum(here - SUB, 0)
        now, then = p % 2, 1 - p % 2
        spans = slice((p * SUB + 1) * SPAN, ((p + 1) * SUB + 1) * SPAN)
        place_rows(rows_in[now][...].reshape(SUB * SPAN, LANES), spans)
        for i in range(SUB):
            b = p * SUB + i
            own = slice((b + 1) * SPAN, (b + 2) * SPAN)
            window = slice(b * SPAN, (b + 2) * SPAN)
            raw = lax.dot_general(qv_win[own], key_win[window], NT, preferred_element_type=F32)
            seen = key_place[b] < query_place[0, :, b : b + 1]
            grown_ref[i] = jnp.where(seen, jnp.exp2(raw * score_scale), 0.0)
            gather_rows(addr_ref, coming + i, tokens, rows_in[then].at[i])
        for i in range(SUB):
            b = p * SUB + i
            window = slice(b * SPAN, (b + 2) * SPAN)
            grown = grown_ref[i]
            mixed = jnp.dot(
                grown.astype(BF16),
                jnp.concatenate([qv_win[window], ones], axis=1),
                preferred_element_type=F32,
            )
            sums = mixed[:, LANES:]
            recip = 1.0 / sums
            prob_ref[b] = (grown * jnp.concatenate([recip, recip], axis=1)).astype(BF16)
            signed = sums * sign_ref[0, :, b : b + 1]
            rows_out[now][i] = jnp.where(low, signed, mixed[:, :LANES] * recip)
            scatter_rows(addr_ref, gone + i, rows_out[then].at[i], result)

    qv_ref[...] = qv_win[SPAN:]
    key_ref[...] = key_win[SPAN:]
    qv_win[:SPAN] = qv_win[GROUP * SPAN :]
    key_win[:SPAN] = key_win[GROUP * SPAN :]

    @pl.when(step == last)
    def _():
        for i in range(SUB):
            scatter_rows(addr_ref, blocks - SUB + i, out_odd.at[i], result)
        home_ref[...] = result[:half, :].astype(BF16)
        away_ref[...] = result[half:, :].astype(BF16)


def forward(addr, mine, other, key_place, query_place, sign):
    half = mine.shape[0] * (mine.shape[1] - 16)
    total = 2 * half
    blocks = total // SPAN
    rows = GROUP * SPAN
    return pl.pallas_call(
        forward_kernel,
        grid=(blocks // GROUP,),
        out_shape=[
            jax.ShapeDtypeStruct((half, LANES), BF16),
            jax.ShapeDtypeStruct((half, LANES), BF16),
            pltpu.HBM((blocks, SPAN, 2 * SPAN), BF16),
            pltpu.HBM((total, LANES), BF16),
            pltpu.HBM((total, LANES), BF16),
        ],
        in_specs=[
            whole(pltpu.SMEM),
            whole(pltpu.VMEM),
            whole(pltpu.VMEM),
            pl.BlockSpec((GROUP, 1, 2 * SPAN), lambda g: (g, 0, 0)),
            pl.BlockSpec((1, SPAN, GROUP), lambda g: (g, 0, 0)),
            pl.BlockSpec((1, SPAN, GROUP), lambda g: (g, 0, 0)),
        ],
        out_specs=[
            whole(pltpu.VMEM),
            whole(pltpu.VMEM),
            pl.BlockSpec((GROUP, SPAN, 2 * SPAN), lambda g: (g, 0, 0)),
            pl.BlockSpec((rows, LANES), lambda g: (g, 0)),
            pl.BlockSpec((rows, LANES), lambda g: (g, 0)),
        ],
        scratch_shapes=[
            pltpu.VMEM((total, LANES), F32),
            pltpu.VMEM((total, LANES), F32),
            *[pltpu.VMEM((SUB, SPAN, LANES), F32)] * 4,
            pltpu.VMEM((SUB, SPAN, 2 * SPAN), F32),
            pltpu.VMEM((rows + SPAN, LANES), BF16),
            pltpu.VMEM((rows + SPAN, LANES), BF16),
        ],
        compiler_params=pltpu.CompilerParams(vmem_limit_bytes=22 * MIB),
        cost_estimate=pl.CostEstimate(flops=0, bytes_accessed=64 * MIB, transcendentals=0),
        name="span_forward",
    )(addr, mine, other, key_place, query_place, sign)


def share_of(own, peer):
    row = lax.broadcasted_iota(jnp.int32, (LANES, LANES), 0)
    pick = (row < 1).astype(BF16)
    own_sum = jnp.dot(own, pick, preferred_element_type=F32)
    peer_sum = jnp.dot(peer, pick, preferred_element_type=F32)
    both = own_sum / (own_sum + peer_sum)
    own_alone = own_sum < 0.0
    peer_alone = peer_sum < 0.0
    return jnp.where(
        own_alone, jnp.where(peer_alone, both, 0.0), jnp.where(peer_alone, 1.0, both)
    )


def combined_rows(own, peer, share):
    high = lane_of(own.shape) >= DH
    own = own.astype(F32)
    peer = peer.astype(F32)
    return jnp.where(high, share * own + (1.0 - share) * peer, 0.0)


def mix_attention_kernel(own_ref, peer_ref, grad_ref, out_ref):
    pieces, half, _ = grad_ref.shape
    rows = 2 * half
    for i in range(pieces):
        own = own_ref[i * rows : (i + 1) * rows]
        peer = peer_ref[i * rows : (i + 1) * rows]
        combined = combined_rows(own, peer, share_of(own, peer))
        out_ref[i, :half] = (pltpu.roll(combined[:half], DH, 1) + combined[half:]).astype(BF16)
        out_ref[i, half:] = grad_ref[i]


def mix_grad_kernel(own_ref, peer_ref, both_ref, grad_own, grad_peer):
    pieces, rows, _ = both_ref.shape
    for i in range(pieces):
        at = slice(i * rows, (i + 1) * rows)
        own = own_ref[at]
        peer = peer_ref[at]
        share = share_of(own, peer)
        combined = combined_rows(own, peer, share)
        packed = both_ref[i, rows // 2 :].astype(F32)
        grad = jnp.concatenate([pltpu.roll(packed, DH, 1), packed], axis=0)
        column = lane_of((LANES, LANES))
        inner = split_sum(grad * combined, (column < DH).astype(BF16))
        both = jnp.where(lane_of(grad.shape) < DH, -inner, grad)
        grad_own[at] = (share * both).astype(BF16)
        grad_peer[at] = ((1.0 - share) * both).astype(BF16)


def mix_attention(home, peer, grad):
    pieces, rows, _ = grad.shape
    return pl.pallas_call(
        mix_attention_kernel,
        out_shape=jax.ShapeDtypeStruct((pieces, 2 * rows, LANES), BF16),
        in_specs=[whole(pltpu.VMEM)] * 3,
        out_specs=whole(pltpu.VMEM),
        compiler_params=pltpu.CompilerParams(vmem_limit_bytes=12 * MIB),
        name="mix_attention",
    )(home, peer, grad)


def mix_grad(home, peer, both):
    return pl.pallas_call(
        mix_grad_kernel,
        out_shape=[jax.ShapeDtypeStruct(home.shape, BF16)] * 2,
        in_specs=[whole(pltpu.VMEM)] * 3,
        out_specs=[whole(pltpu.VMEM)] * 2,
        compiler_params=pltpu.CompilerParams(vmem_limit_bytes=12 * MIB),
        name="mix_grad",
    )(home, peer, both)


def pack_kernel(query_ref, value_ref, slot_ref, out_ref):
    rounds, heads, rows = slot_ref.shape
    half = rows // 2
    for h in range(heads):
        columns = slice(h * DH, (h + 1) * DH)
        pair = jnp.concatenate([query_ref[:, columns], value_ref[:, columns]], axis=1)
        for r in range(rounds):
            out_ref[2 * h + r, :half] = pair[r * half : (r + 1) * half]
            slots = slot_ref[r, h : h + 1, :]
            high = slots // LANES
            parts = [high, slots - high * LANES]
            lines = [p[:, j : j + LANES] for p in parts for j in range(0, rows, LANES)]
            out_ref[2 * h + r, half:] = jnp.concatenate(lines, axis=0).astype(F32).astype(BF16)


def pack_heads(queries, values, slots):
    rounds, heads, rows = slots.shape
    return pl.pallas_call(
        pack_kernel,
        out_shape=jax.ShapeDtypeStruct((rounds * heads, rows // 2 + 16, 2 * DH), BF16),
        compiler_params=pltpu.CompilerParams(vmem_limit_bytes=10 * MIB),
        out_specs=whole(pltpu.VMEM),
        name="pack_heads",
    )(in_hbm(queries), in_hbm(values), in_hbm(slots))


def unpack_kernel(in_ref, query_ref, value_ref):
    for h in range(in_ref.shape[0]):
        columns = slice(h * DH, (h + 1) * DH)
        query_ref[:, columns] = in_ref[h, :, :DH]
        value_ref[:, columns] = in_ref[h, :, DH:]


def unpack_heads(rows):
    heads, count, _ = rows.shape
    return pl.pallas_call(
        unpack_kernel,
        out_shape=[jax.ShapeDtypeStruct((count, heads * DH), BF16)] * 2,
        in_specs=[whole(pltpu.VMEM)],
        compiler_params=pltpu.CompilerParams(vmem_limit_bytes=10 * MIB),
        name="unpack_heads",
    )(rows)


def member(step, groups):
    return lax.rem(lax.axis_index("head") + (groups - step), groups)


def columns_of(index, width):
    return pl.ds(pl.multiple_of(index * width, width), width)


def back_kernel(weight_ref, *refs):
    *grads, out_ref = refs
    groups = len(grads)
    rows, width = grads[0].shape
    total = 0.0
    for k in range(groups):
        weight = weight_ref[:, columns_of(member(k, groups), width)]
        total += lax.dot_general(grads[k][...], weight, NT, preferred_element_type=F32)
    total = total.astype(BF16)
    quarter = rows // 4
    for h in range(width // DH):
        columns = slice(h * DH, (h + 1) * DH)
        for c in range(2):
            first = total[2 * c * quarter : (2 * c + 1) * quarter, columns]
            second = total[(2 * c + 1) * quarter : (2 * c + 2) * quarter, columns]
            out_ref[2 * h + c] = jnp.concatenate([first, second], axis=1)


def back_projection(weight, grads):
    rows, width = grads[0].shape
    return pl.pallas_call(
        back_kernel,
        out_shape=jax.ShapeDtypeStruct((2 * width // DH, rows // 4, 2 * DH), BF16),
        compiler_params=pltpu.CompilerParams(vmem_limit_bytes=10 * MIB),
        out_specs=whole(pltpu.VMEM),
        name="back_projection",
    )(weight, *grads)


def project_kernel(weight_ref, packed_ref, att_ref, *outs):
    groups = len(outs)
    rows, width = att_ref.shape
    quarter = rows // 4
    for h in range(width // DH):
        columns = slice(h * DH, (h + 1) * DH)
        for c in range(2):
            packed = packed_ref[2 * h + c, :quarter]
            att_ref[2 * c * quarter : (2 * c + 1) * quarter, columns] = packed[:, :DH]
            att_ref[(2 * c + 1) * quarter : (2 * c + 2) * quarter, columns] = packed[:, DH:]
    for k in range(groups):
        weight = weight_ref[:, columns_of(member(groups - k, groups), width)]
        outs[k][...] = jnp.dot(att_ref[...], weight, preferred_element_type=F32).astype(BF16)


def project(weight, packed):
    count, double, _ = packed.shape
    rows, width = 2 * double, count * DH // 2
    groups = weight.shape[1] // width
    return pl.pallas_call(
        project_kernel,
        out_shape=[jax.ShapeDtypeStruct((rows, width), BF16)] * 3
        + [pltpu.HBM((rows, width), BF16)]
        + [jax.ShapeDtypeStruct((rows, width), BF16)] * (groups - 3),
        compiler_params=pltpu.CompilerParams(vmem_limit_bytes=10 * MIB),
        in_specs=[whole(pltpu.VMEM)] * 2,
        out_specs=[whole(pltpu.VMEM)] * 3 + [pl.BlockSpec()] + [whole(pltpu.VMEM)] * (groups - 3),
        name="project",
    )(weight, packed)


def add_kernel(*refs):
    *shares, out_ref = refs
    total = shares[0][...].astype(F32)
    for share in shares[1:]:
        total += share[...].astype(F32)
    out_ref[...] = total.astype(BF16)


def add_shares(shares):
    return pl.pallas_call(
        add_kernel,
        out_shape=jax.ShapeDtypeStruct(shares[0].shape, BF16),
        in_specs=[whole(pltpu.VMEM)] * len(shares),
        compiler_params=pltpu.CompilerParams(vmem_limit_bytes=8 * MIB),
        name="add_shares",
    )(*shares)


def weight_grad_kernel(att_ref, *refs):
    *grads, keep_ref, give_ref = refs
    groups = len(grads)
    width = grads[0].shape[1]
    part = keep_ref.shape[0]
    core = lax.rem(lax.axis_index("seq"), 2)
    for index, out_ref in ((core, keep_ref), (1 - core, give_ref)):
        att = att_ref[:, columns_of(index, part)]
        for k in range(groups):
            out_ref[:, columns_of(member(k, groups), width)] = lax.dot_general(
                att, grads[k][...], TN, preferred_element_type=F32
            ).astype(BF16)


def weight_grad(att, grads):
    width = att.shape[1]
    groups = len(grads)
    return pl.pallas_call(
        weight_grad_kernel,
        out_shape=[jax.ShapeDtypeStruct((width // 2, width * groups), BF16)] * 2,
        compiler_params=pltpu.CompilerParams(vmem_limit_bytes=10 * MIB),
        out_specs=[whole(pltpu.VMEM)] * 2,
        name="weight_grad",
    )(att, *grads)


def finished_rows(rows, query_part, key_value):
    low = lane_of(rows.shape) < DH
    scale = DH ** (-0.5)
    query = jnp.where(low, rows.astype(F32), 0.0)
    inverse = inverse_of(query)
    key = query * inverse
    term = key_value * (inverse * scale)
    along = split_sum(key * term, low_lanes(1.0 / DH))
    return jnp.where(low, query_part * scale + term - key * along, key_value)


def backward_kernel(
    addr_ref, mine_ref, other_ref, prob_ref, qv_ref, qv_before, key_ref, key_before,
    home_ref, away_ref,
    tokens, result, in_even, in_odd, out_even, out_odd, qv_win, key_win, tall, sums, query_sums,
    first_sums,
):
    step = pl.program_id(0)
    last = pl.num_programs(0) - 1
    half = mine_ref.shape[0]
    blocks = 2 * half // SPAN
    rows_in = (in_even, in_odd)
    rows_out = (out_even, out_odd)

    @pl.when(step == 0)
    def _():
        tokens[:half, :] = mine_ref[...].astype(F32)
        tokens[half:, :] = other_ref[...].astype(F32)
        for b in range(SUB):
            gather_rows(addr_ref, b, tokens, in_even.at[b])

    qv_win[:SPAN] = qv_before[...]
    qv_win[SPAN:] = qv_ref[...]
    key_win[:SPAN] = key_before[...]
    key_win[SPAN:] = key_ref[...]
    low = lane_of((SPAN, LANES)) < DH
    zero = jnp.zeros((SPAN, LANES), BF16)
    for p in range(GROUP // SUB):
        here = step * GROUP + p * SUB
        coming = jnp.minimum(here + SUB, blocks - SUB)
        gone = here + (blocks - SUB - 1)
        now, then = p % 2, 1 - p % 2
        spans = slice(p * SUB * SPAN, ((p + 1) * SUB + 1) * SPAN)
        everything = qv_win[spans]
        lane = lane_of(everything.shape)
        one = jnp.where(lane == 0, 1.0, 0.0).astype(BF16)
        value_one = jnp.where(lane >= DH, everything, one)
        for i in range(SUB):
            b = p * SUB + i
            prob = prob_ref[b]
            dot_grad = lax.dot_general(
                rows_in[now][i].astype(BF16),
                value_one[i * SPAN : (i + 2) * SPAN],
                NT,
                preferred_element_type=F32,
            )
            tall[i, :SPAN] = (prob.astype(F32) * dot_grad).astype(BF16)
            tall[i, SPAN:] = prob
            gather_rows(addr_ref, coming + i, tokens, rows_in[then].at[i])
        for i in range(SUB):
            b = p * SUB + i
            own = slice((b + 1) * SPAN, (b + 2) * SPAN)
            window = slice(b * SPAN, (b + 2) * SPAN)
            query_sums[own] = jnp.dot(
                tall[i, :SPAN], key_win[window], preferred_element_type=F32
            )
            grad_high = jnp.where(low, 0.0, rows_in[now][i]).astype(BF16)
            key_value = lax.dot_general(
                tall[i],
                jnp.concatenate([jnp.where(low, qv_win[own], zero), grad_high], axis=0),
                TN,
                preferred_element_type=F32,
            )
            if b == 0:

                @pl.when(step == 0)
                def _():
                    first_sums[...] = key_value[:SPAN]

            sums[b * SPAN : (b + 1) * SPAN] += key_value[:SPAN]
            sums[own] = key_value[SPAN:]
            scatter_rows(addr_ref, lax.rem(gone + i, blocks), rows_out[then].at[i], result)
        spans = slice(p * SUB * SPAN, (p + 1) * SUB * SPAN)
        finished = finished_rows(qv_win[spans], query_sums[spans], sums[spans])
        rows_out[now][...] = finished.reshape(SUB, SPAN, LANES)
    sums[:SPAN] = sums[GROUP * SPAN :]
    query_sums[:SPAN] = query_sums[GROUP * SPAN :]

    @pl.when(step == last)
    def _():
        for i in range(SUB):
            scatter_rows(addr_ref, blocks - SUB - 1 + i, out_odd.at[i], result)
        out_even[0] = finished_rows(
            qv_win[GROUP * SPAN :], query_sums[:SPAN], sums[:SPAN] + first_sums[...]
        )
        scatter_rows(addr_ref, blocks - 1, out_even.at[0], result)
        home_ref[...] = result[:half, :].astype(BF16)
        away_ref[...] = result[half:, :].astype(BF16)


def backward(addr, mine, other, prob, query_key, value_one):
    half = mine.shape[0]
    total = 2 * half
    blocks = total // SPAN
    rows = GROUP * SPAN
    by_rows = pl.BlockSpec((rows, LANES), lambda g: (g, 0))
    before = pl.BlockSpec((SPAN, LANES), lambda g: (lax.rem(g * GROUP + blocks - 1, blocks), 0))
    return pl.pallas_call(
        backward_kernel,
        grid=(blocks // GROUP,),
        out_shape=[jax.ShapeDtypeStruct((half, LANES), BF16)] * 2,
        in_specs=[
            whole(pltpu.SMEM),
            whole(pltpu.VMEM),
            whole(pltpu.VMEM),
            pl.BlockSpec((GROUP, SPAN, 2 * SPAN), lambda g: (g, 0, 0)),
            by_rows,
            before,
            by_rows,
            before,
        ],
        out_specs=[whole(pltpu.VMEM)] * 2,
        scratch_shapes=[
            pltpu.VMEM((total, LANES), F32),
            pltpu.VMEM((total, LANES), F32),
            *[pltpu.VMEM((SUB, SPAN, LANES), F32)] * 4,
            pltpu.VMEM((rows + SPAN, LANES), BF16),
            pltpu.VMEM((rows + SPAN, LANES), BF16),
            pltpu.VMEM((SUB, 2 * SPAN, 2 * SPAN), BF16),
            pltpu.VMEM((rows + SPAN, LANES), F32),
            pltpu.VMEM((rows + SPAN, LANES), F32),
            pltpu.VMEM((SPAN, LANES), F32),
        ],
        compiler_params=pltpu.CompilerParams(vmem_limit_bytes=22 * MIB),
        cost_estimate=pl.CostEstimate(flops=0, bytes_accessed=64 * MIB, transcendentals=0),
        name="span_backward",
    )(addr, mine, other, *[in_hbm(x) for x in (prob, query_key, query_key, value_one, value_one)])


def swap(value, distance=1):
    count = lax.axis_size("seq")
    return lax.ppermute(value, "seq", [(i, i ^ distance) for i in range(count)])


def to_all(value):
    return lax.all_to_all(value, "seq", split_axis=0, concat_axis=0, tiled=True)


def rotate(value, step):
    count = lax.axis_size("head")
    return lax.ppermute(value, "head", [(i, (i + step) % count) for i in range(count)])


def after(values, *earlier):
    return lax.optimization_barrier((values, earlier))[0]


def by_sequence(queries, values, w_out, out_grad, slots):
    rows = queries.shape[0]
    _, heads, _ = slots.shape
    shards = lax.axis_size("seq")
    groups = lax.axis_size("head")
    core = lax.rem(lax.axis_index("seq"), 2)
    total = shards * rows
    half_rows = rows // 2

    packed = pack_heads(queries, values, slots)
    mine = to_all(packed)
    places = find_places(mine)

    first = rotate(out_grad, 1)
    grads = [out_grad, first, rotate(first, 1), rotate(out_grad, groups - 1)]
    mine = after(mine, first)

    home, away, prob, query_key, value_one = forward(places[0], mine, swap(mine), *places[1:])
    away, *grads = after([away, *grads])
    peer = swap(away)

    grad_packed = back_projection(w_out, grads)
    both = to_all(mix_attention(home, peer, grad_packed))
    grad_own, grad_peer = mix_grad(home, peer, both)
    grad_other = swap(grad_peer)

    att, *shares = project(w_out, both)
    early = [rotate(shares[k], k) for k in range(1, groups, 2)]
    weight, give = weight_grad(att, grads)
    weight = (weight.astype(F32) + swap(give).astype(F32)).astype(BF16)
    weights = [weight] + [swap(weight, distance) for distance in range(2, shards, 2)]

    own, others = backward(places[0], grad_own, grad_other, prob, query_key, value_one)
    others, *weights = after([others, *weights])
    others, *early = after([others, *early])
    late = [rotate(after(shares[k], own), k) for k in range(2, groups, 2)]

    summed = (own.astype(F32) + swap(others).astype(F32)).astype(BF16)
    summed = to_all(summed.reshape(shards, half_rows, LANES))
    query_grad, value_grad = unpack_heads(summed.reshape(heads, rows, LANES))

    weights = [w.astype(F32) for w in weights]
    while len(weights) > 1:
        weights = [weights[i] + weights[i + 1] for i in range(0, len(weights), 2)]
    weight = weights[0].astype(BF16)
    rest = swap(weight)
    weight = jnp.where(
        core == 0,
        jnp.concatenate([weight, rest], axis=0),
        jnp.concatenate([rest, weight], axis=0),
    )
    w_out_grad = weight.astype(F32) * total ** (-0.5)

    output = shares[0].astype(F32)
    for share in early + late:
        output = output + share.astype(F32)
    return (output.astype(BF16), query_grad, value_grad, w_out_grad)


def shifted(value, axis, steps):
    count = lax.axis_size(axis)
    pairs = [(source, (source + steps) % count) for source in range(count)]
    return lax.ppermute(value, axis, pairs)


def with_before(blocks, before):
    earlier = jnp.concatenate([before[:, None], blocks[:, :-1]], axis=1)
    return jnp.concatenate([blocks, earlier], axis=2)


def normalized(query_rows):
    query_float = query_rows.astype(jnp.float32)
    inverse = lax.rsqrt(jnp.mean(query_float * query_float, axis=-1, keepdims=True) + 1e-06)
    return ((query_float * inverse).astype(jnp.bfloat16), query_float, inverse)


def move_wide(matrix, data, form):
    return jnp.einsum(form, matrix, data, preferred_element_type=jnp.float32).astype(jnp.bfloat16)


def move_exact(matrix, data, form):
    return jnp.einsum(form, matrix, data.astype(jnp.float32), precision=lax.Precision.HIGHEST)


def by_span(queries, values, w_out, out_grad, slots):
    row_count = queries.shape[0]
    head_width = DH
    rounds = slots.shape[0]
    head_group = queries.shape[1] // head_width
    batch_size = rounds * head_group
    shards = lax.axis_size("seq")
    my_index = lax.axis_index("seq")
    even_share = row_count // shards
    capacity = even_share * 3 // 2
    slot_total = shards * capacity
    block_count = row_count // SPAN
    score_scale = head_width ** (-0.5)

    def per_head(matrix):
        split_heads = matrix.reshape(row_count, head_group, head_width).transpose(1, 0, 2)
        return jnp.concatenate([split_heads] * rounds, axis=0)

    flat_slot = slots.reshape(batch_size, row_count)
    target = flat_slot // row_count
    local_slot = flat_slot - target * row_count
    onehot_target = (
        target[:, :, None] == jnp.arange(shards, dtype=jnp.int32)[None, None, :]
    ).astype(jnp.int32)
    earlier_count = jnp.sum(jnp.cumsum(onehot_target, axis=1) * onehot_target, axis=2) - 1
    send_spot = target * capacity + earlier_count
    positions = my_index * row_count + jnp.arange(row_count, dtype=jnp.int32)
    position_rows = jnp.broadcast_to(positions[None, :], (batch_size, row_count))
    pack_float = (
        send_spot[:, None, :] == jnp.arange(slot_total, dtype=jnp.int32)[None, :, None]
    ).astype(jnp.float32)
    pack_half = pack_float.astype(jnp.bfloat16)
    full_grad = lax.all_gather(out_grad, "head", axis=1, tiled=True)
    back_attn = lax.dot_general(
        full_grad, w_out, (((1,), (1,)), ((), ())), preferred_element_type=jnp.float32
    ).astype(jnp.bfloat16)
    query_value = jnp.concatenate([per_head(queries), per_head(values)], axis=2)
    packed_rows = move_wide(pack_half, query_value, "bsr,brd->bsd").reshape(
        batch_size, shards, capacity, 2 * head_width
    )
    packed_place = (
        move_exact(pack_float, position_rows, "bsr,br->bs")
        .astype(jnp.int32)
        .reshape(batch_size, shards, capacity)
    )
    packed_slot = (
        move_exact(pack_float, local_slot + 1, "bsr,br->bs")
        .astype(jnp.int32)
        .reshape(batch_size, shards, capacity)
    )
    got_rows, got_place, got_slot = (
        lax.all_to_all(packed_rows, "seq", split_axis=1, concat_axis=1, tiled=True),
        lax.all_to_all(packed_place, "seq", split_axis=1, concat_axis=1, tiled=True),
        lax.all_to_all(packed_slot, "seq", split_axis=1, concat_axis=1, tiled=True),
    )
    got_spot = got_slot.reshape(batch_size, slot_total)
    got_spot = jnp.where(got_spot == 0, row_count, got_spot - 1)
    sort_float = (
        got_spot[:, :, None] == jnp.arange(row_count, dtype=jnp.int32)[None, None, :]
    ).astype(jnp.float32)
    sort_half = sort_float.astype(jnp.bfloat16)
    sorted_rows = move_wide(
        sort_half, got_rows.reshape(batch_size, slot_total, 2 * head_width), "bsr,bsd->brd"
    )
    sorted_place = move_exact(
        sort_float, got_place.reshape(batch_size, slot_total), "bsr,bs->br"
    ).astype(jnp.int32)
    last_rows = sorted_rows[:, row_count - SPAN :]
    last_place = sorted_place[:, row_count - SPAN :]
    before_rows, before_place = shifted((last_rows, last_place), "seq", 1)
    sorted_query = sorted_rows[:, :, :head_width]
    sorted_value = sorted_rows[:, :, head_width:]
    sorted_key, query_float, inverse = normalized(sorted_query)
    before_key = normalized(before_rows[:, :, :head_width])[0]
    query_blocks = sorted_query.reshape(batch_size, block_count, SPAN, head_width)
    key_window = with_before(
        sorted_key.reshape(batch_size, block_count, SPAN, head_width), before_key
    )
    value_window = with_before(
        sorted_value.reshape(batch_size, block_count, SPAN, head_width),
        before_rows[:, :, head_width:],
    )
    place_blocks = sorted_place.reshape(batch_size, block_count, SPAN)
    place_window = with_before(place_blocks, before_place)
    own_token = (jnp.arange(SPAN)[:, None] == jnp.arange(2 * SPAN)[None, :]).astype(jnp.float32)
    future = (place_window[:, :, None, :] > place_blocks[:, :, :, None]).astype(jnp.float32)

    def score_of():
        raw_scores = (
            jnp.einsum(
                "bcqd,bckd->bcqk", query_blocks, key_window, preferred_element_type=jnp.float32
            )
            * score_scale
        )
        return raw_scores - 100000.0 * own_token - 1000000000.0 * future

    scores = score_of()
    row_top = jnp.max(scores, axis=-1)
    log_total = row_top + jnp.log(jnp.sum(jnp.exp(scores - row_top[..., None]), axis=-1))
    weights = jnp.exp(scores - log_total[..., None])
    rounded_probs = weights.astype(jnp.bfloat16)
    block_out = jnp.einsum(
        "bcqk,bckd->bcqd", rounded_probs, value_window, preferred_element_type=jnp.float32
    ).astype(jnp.bfloat16)
    out_rows = block_out.reshape(batch_size, row_count, head_width)
    home_out = move_wide(sort_half, out_rows, "bsr,brd->bsd").reshape(
        batch_size, shards, capacity // 2, 2 * head_width
    )
    home_log = move_exact(
        sort_float, log_total.reshape(batch_size, row_count), "bsr,br->bs"
    ).reshape(batch_size, shards, capacity)
    back_out, back_log = (
        lax.all_to_all(home_out, "seq", split_axis=1, concat_axis=1, tiled=True),
        lax.all_to_all(
            home_log.astype(jnp.bfloat16), "seq", split_axis=1, concat_axis=1, tiled=True
        ).astype(home_log.dtype),
    )
    round_out = move_wide(
        pack_half, back_out.reshape(batch_size, slot_total, head_width), "bsr,bsd->brd"
    ).reshape(rounds, head_group, row_count, head_width)
    round_log = move_exact(
        pack_float, back_log.reshape(batch_size, slot_total), "bsr,bs->br"
    ).reshape(rounds, head_group, row_count)
    mixing = jax.nn.softmax(round_log, axis=0)
    combined = jnp.sum(mixing[..., None] * round_out.astype(jnp.float32), axis=0)
    attention = (
        combined.astype(jnp.bfloat16).transpose(1, 0, 2).reshape(row_count, head_group * head_width)
    )
    head_term = jnp.dot(attention, w_out, preferred_element_type=jnp.float32)
    output = lax.psum_scatter(
        head_term.astype(jnp.bfloat16), "head", scatter_dimension=1, tiled=True
    )
    weight_term = lax.dot_general(
        attention, full_grad, (((0,), (0,)), ((), ())), preferred_element_type=jnp.float32
    )
    w_out_grad = lax.psum(weight_term.astype(jnp.bfloat16), "seq").astype(jnp.float32) * (
        shards * row_count
    ) ** (-0.5)
    back_heads = (
        back_attn.reshape(row_count, head_group, head_width).transpose(1, 0, 2).astype(jnp.float32)
    )
    inner_rows = jnp.sum(back_heads * combined, axis=-1)
    delta_rows = (mixing * inner_rows[None]).reshape(batch_size, row_count)
    grad_rows = (
        (mixing[..., None] * back_heads[None])
        .astype(jnp.bfloat16)
        .reshape(batch_size, row_count, head_width)
    )
    packed_grad = move_wide(pack_half, grad_rows, "bsr,brd->bsd").reshape(
        batch_size, shards, capacity // 2, 2 * head_width
    )
    packed_delta = move_exact(pack_float, delta_rows, "bsr,br->bs").reshape(
        batch_size, shards, capacity
    )
    got_grad, got_delta = (
        lax.all_to_all(packed_grad, "seq", split_axis=1, concat_axis=1, tiled=True),
        lax.all_to_all(
            packed_delta.astype(jnp.bfloat16), "seq", split_axis=1, concat_axis=1, tiled=True
        ).astype(packed_delta.dtype),
    )
    sorted_grad = move_wide(
        sort_half, got_grad.reshape(batch_size, slot_total, head_width), "bsr,bsd->brd"
    )
    sorted_delta = move_exact(sort_float, got_delta.reshape(batch_size, slot_total), "bsr,bs->br")
    kept_weights = jnp.exp(score_of() - log_total[..., None])
    grad_blocks = sorted_grad.reshape(batch_size, block_count, SPAN, head_width)
    delta_blocks = sorted_delta.reshape(batch_size, block_count, SPAN)
    dot_grad = jnp.einsum(
        "bcqd,bckd->bcqk", grad_blocks, value_window, preferred_element_type=jnp.float32
    )
    score_grad = (kept_weights * (dot_grad - delta_blocks[..., None])).astype(jnp.bfloat16)
    query_part = (
        jnp.einsum("bcqk,bckd->bcqd", score_grad, key_window, preferred_element_type=jnp.float32)
        * score_scale
    )
    key_part = (
        jnp.einsum("bcqk,bcqd->bckd", score_grad, query_blocks, preferred_element_type=jnp.float32)
        * score_scale
    )
    value_part = jnp.einsum(
        "bcqk,bcqd->bckd", rounded_probs, grad_blocks, preferred_element_type=jnp.float32
    )
    spill_rows = jnp.concatenate([key_part[:, 0, SPAN:], value_part[:, 0, SPAN:]], axis=2)
    arrived = shifted(spill_rows.astype(jnp.bfloat16), "seq", -1).astype(spill_rows.dtype)
    key_grad = key_part[:, :, :SPAN] + jnp.concatenate(
        [key_part[:, 1:, SPAN:], arrived[:, None, :, :head_width]], axis=1
    )
    value_sum = value_part[:, :, :SPAN] + jnp.concatenate(
        [value_part[:, 1:, SPAN:], arrived[:, None, :, head_width:]], axis=1
    )
    key_grad = key_grad.reshape(batch_size, row_count, head_width)
    value_sum = value_sum.reshape(batch_size, row_count, head_width)
    query_total = (
        query_part.reshape(batch_size, row_count, head_width)
        + inverse * key_grad
        - query_float
        * (inverse * inverse * inverse)
        * jnp.mean(query_float * key_grad, axis=-1, keepdims=True)
    )
    both_grads = jnp.concatenate(
        [query_total.astype(jnp.bfloat16), value_sum.astype(jnp.bfloat16)], axis=2
    )
    home_grads = move_wide(sort_half, both_grads, "bsr,brd->bsd").reshape(
        batch_size, shards, capacity, 2 * head_width
    )
    back_grads = lax.all_to_all(home_grads, "seq", split_axis=1, concat_axis=1, tiled=True)
    own_grads = move_wide(
        pack_half, back_grads.reshape(batch_size, slot_total, 2 * head_width), "bsr,bsd->brd"
    ).astype(jnp.float32)
    own_grads = own_grads.reshape(rounds, head_group, row_count, 2 * head_width)
    summed = jnp.sum(own_grads, axis=0).astype(jnp.bfloat16)
    query_grad = (
        summed[:, :, :head_width].transpose(1, 0, 2).reshape(row_count, head_group * head_width)
    )
    value_grad = (
        summed[:, :, head_width:].transpose(1, 0, 2).reshape(row_count, head_group * head_width)
    )
    return (output, query_grad, value_grad, w_out_grad)


def per_device(queries, values, w_out, out_grad, slots):
    if lax.axis_size("seq") == slots.shape[0] * slots.shape[1] and slots.shape[0] == 2:
        return by_sequence(queries, values, w_out, out_grad, slots)
    return by_span(queries, values, w_out, out_grad, slots)


def solution(mesh):
    placed = (
        P("seq", "head"),
        P("seq", "head"),
        P("head", None),
        P("seq", "head"),
        P(None, "head", "seq"),
    )
    return jax.shard_map(
        per_device,
        mesh=mesh,
        in_specs=placed,
        out_specs=(P("seq", "head"), P("seq", "head"), P("seq", "head"), P("head", None)),
        check_vma=False,
    )
```
